128 devices in a mesh: dp: 64 (over x, z_hi, y, core), tensor: 2 (over z_lo).
Axes of the slice: x: 4, y: 4, z: 4 (z_hi: 2, z_lo: 2; z = z_hi * 2 + z_lo), core: 2. Of those that a mesh axis runs over, the one named last changes fastest.
Arguments:
- hidden: bfloat16 [32768, 1536], P(('dp', 'tensor')), may hold values from -24 to 24
- segments: int32 [64, 512], P('dp'), may hold values from 0 to 3, never falling along the last dimension, each value on 1 to 384 neighbouring positions
- norm_gain: float32 [1536], replicated, may hold values from 0.5 to 1.5
- in_weight: bfloat16 [2, 1536, 3072], P(None, 'dp', 'tensor'), may hold values from -0.15625 to 0.15625
- bc_weight: bfloat16 [1536, 256], P('dp'), may hold values from -0.15625 to 0.15625
- step_weight: bfloat16 [1536, 48], P('dp', 'tensor'), may hold values from -0.15625 to 0.15625
- conv_weight: float32 [4, 3328], replicated, may hold values from -3 to 3
- conv_bias: float32 [3328], replicated, may hold values from -1.2 to 1.2
- step_bias: float32 [48], replicated, may hold values from -6 to -2
- decay_log: float32 [48], replicated, may hold values from 0 to 2.77
- skip_gain: float32 [48], replicated, may hold values from 0.1 to 1.9
- gate_gain: float32 [3072], replicated, may hold values from 0.5 to 1.5
- out_weight: bfloat16 [3072, 1536], P('tensor', 'dp'), may hold values from -0.109375 to 0.109375
- cotangent: bfloat16 [32768, 1536], P(('dp', 'tensor')), may hold values from -24 to 24
Outputs:
- mixed: bfloat16 [32768, 1536], P(('dp', 'tensor'))
- grad_hidden: float32 [32768, 1536], P(('dp', 'tensor'))
- grad_norm_gain: float32 [1536], replicated
- grad_in_weight: float32 [2, 1536, 3072], P(None, 'dp', 'tensor')
- grad_bc_weight: float32 [1536, 256], P('dp')
- grad_step_weight: float32 [1536, 48], P('dp', 'tensor')
- grad_conv_weight: float32 [4, 3328], replicated
- grad_conv_bias: float32 [3328], replicated
- grad_step_bias: float32 [48], replicated
- grad_decay_log: float32 [48], replicated
- grad_skip_gain: float32 [48], replicated
- grad_gate_gain: float32 [3072], replicated
- grad_out_weight: float32 [3072, 1536], P('tensor', 'dp')
The draws below stay inside these ranges and needn't reach their ends.
Inputs may be any that keep to these rules, and one draw needn't show every extreme that they name: `segments`: in each row, the 512 tokens of one pack, segment numbers never fall; 4 documents of 1 to 384 tokens each, one of exactly 384.
All inputs are finite; a program needn't handle non-finite values.
Results may differ from the reference program's by a relative error of at most 0.011.
Values may be sent and summed in bfloat16 or wider, within the bound.
No kernel may reach another device: no remote copies, remote signals or barrier semaphores. Data moves between devices by JAX's collectives and lax.ppermute only.
A program may use at most 128 MiB of HBM per device.

```python
import math
import jax
import jax.numpy as jnp
import numpy as np
from jax import lax

D = 1536
HEADS = 48
STATE = 128
CONV = 4
SEGS = 4
INNER = 3072
GROUP_TOK = 512
SEG_MOST = 384
GROUPS = 64
TOKENS = 32768


def strengthened(values, rng, source, target, parts, factor):
    owner, partner = [(jnp.arange(values.shape[axis_at]) // (values.shape[axis_at] // parts)).reshape([-1 if axis == axis_at else 1 for axis in range(values.ndim)]) for axis_at in (source, target)]
    chosen = jax.random.permutation(rng, parts)[partner]
    strong = (owner == chosen) | (owner == (partner + parts // 2) % parts)
    return jnp.where(strong, factor * values, values)


def level_of(key, shape, shards, smallest, top_value):
    factor_of = 1.0
    for axis_at, parts in shards:
        steps = jax.random.uniform(jax.random.fold_in(jax.random.fold_in(key, 6), axis_at), (parts,), jnp.float32, smallest / len(shards), top_value / len(shards))
        factor_of = factor_of * jnp.repeat(jnp.exp(steps), shape[axis_at] // parts).reshape((-1,) + (1,) * (len(shape) - 1 - axis_at))
    return factor_of


def split_up(number_of, total, bound, lean):
    weights = [(1 << 20) // math.isqrt(standing ** lean) + 1 for standing in range(2, number_of + 1)]
    spare, counts = total - bound - (number_of - 1), [1] * (number_of - 1)
    while spare > 0:
        free = [i for i in range(number_of - 1) if counts[i] < bound]
        mass, left = sum([weights[i] for i in free]), spare
        for i in free:
            extra = min(bound - counts[i], max(1, left * weights[i] // mass), spare)
            counts[i] = counts[i] + extra
            spare = spare - extra
    return np.array([bound] + counts)


def uneven_parts(key, count, total, most, skew):
    if count == 2:
        one = jax.random.randint(key, (), max(1, total - most), min(most, total - 1) + 1)
        return jnp.stack([one, total - one])
    sizes = jnp.asarray(split_up(count, total, most, skew), jnp.int32)
    pairs = (count - 1) // 2
    giver, receiver = sizes[1:1 + 2 * pairs:2], sizes[2:2 + 2 * pairs:2]
    room = jnp.minimum(giver - 1, most - receiver)
    moved = jax.random.randint(jax.random.fold_in(key, 1), (pairs,), 0, 1 << 20) % (room + 1)
    sizes = sizes.at[1:1 + 2 * pairs:2].set(giver - moved).at[2:2 + 2 * pairs:2].set(receiver + moved)
    return sizes[jax.random.permutation(jax.random.fold_in(key, 2), count)]


def gaussian(stream_key, dims, width, bound, cuts=(), held_as=jnp.bfloat16):
    drawn = width * jax.random.normal(stream_key, dims, jnp.float32)
    if cuts:
        drawn = drawn * level_of(stream_key, dims, cuts, -0.22, 0.18)
    return jnp.clip(drawn, -bound, bound).astype(held_as)


def heavy_noise(stream_key, dims, scale, most, split, heavy, dtype=jnp.bfloat16):
    array = scale * jax.random.normal(stream_key, dims, jnp.float32)
    if split:
        array = array * level_of(stream_key, dims, split, -0.22, 0.18)
    return jnp.clip(strengthened(array, jax.random.fold_in(stream_key, 3), *heavy), -most, most).astype(dtype)


def setup_inputs(seed: int = 0) -> dict:
    arg_keys = jax.random.split(jax.random.key(seed), 15)
    return {
        "hidden": heavy_noise(arg_keys[0], (TOKENS, D), 1.0, 24.0, ((0, 128),), (0, 1, 128, 5.5)),
        "segments": jax.vmap(lambda own: jnp.searchsorted(jnp.cumsum(uneven_parts(own, SEGS, GROUP_TOK, SEG_MOST, 1)), jnp.arange(GROUP_TOK), side="right"))(jax.random.split(arg_keys[1], GROUPS)).reshape((GROUPS, GROUP_TOK)).astype(jnp.int32),
        "norm_gain": jnp.clip(1.0 + 0.1 * jax.random.normal(arg_keys[2], (D,), jnp.float32), 0.5, 1.5),
        "in_weight": gaussian(arg_keys[3], (2, D, INNER), D ** -0.5, 0.15625, ((1, 64), (2, 2))),
        "bc_weight": gaussian(arg_keys[4], (D, 2 * STATE), D ** -0.5, 0.15625, ((0, 64),)),
        "step_weight": gaussian(arg_keys[5], (D, HEADS), D ** -0.5, 0.15625, ((0, 64), (1, 2))),
        "conv_weight": gaussian(arg_keys[6], (CONV, INNER + 2 * STATE), CONV ** -0.5, 3.0, (), jnp.float32),
        "conv_bias": gaussian(arg_keys[7], (INNER + 2 * STATE,), 0.3, 1.2, (), jnp.float32),
        "step_bias": jnp.clip(jax.random.uniform(arg_keys[8], (HEADS,), jnp.float32, -6.0, -2.0), -6.0, -2.0),
        "decay_log": jnp.clip(jax.random.uniform(arg_keys[9], (HEADS,), jnp.float32, 0.0, 2.77), 0.0, 2.77),
        "skip_gain": jnp.clip(1.0 + 0.18 * jax.random.normal(arg_keys[10], (HEADS,), jnp.float32), 0.1, 1.9),
        "gate_gain": jnp.clip(1.0 + 0.1 * jax.random.normal(arg_keys[11], (INNER,), jnp.float32), 0.5, 1.5),
        "out_weight": gaussian(arg_keys[12], (INNER, D), INNER ** -0.5, 0.109375, ((0, 2), (1, 64))),
        "cotangent": heavy_noise(arg_keys[13], (TOKENS, D), 1.0, 24.0, ((0, 128),), (0, 1, 128, 5.5)),
    }


@jax.custom_vjp
def low(v):
    return lax.optimization_barrier(v.astype(jnp.bfloat16)).astype(jnp.float32)

@jax.custom_vjp
def low_back(v):
    return v

def low_keep(v):
    return (low(v), None)

def low_pass(kept, grad):
    return (grad,)

def back_keep(v):
    return (v, None)

def back_low(kept, grad):
    return (low(grad),)
low.defvjp(low_keep, low_pass)
low_back.defvjp(back_keep, back_low)
EPS = 1e-05
PRECISE = lax.Precision.HIGHEST

def shift_down(values, offset):
    if offset == 0:
        return values
    return jnp.pad(values, ((0, 0), (offset, 0), (0, 0)))[:, :values.shape[1]]

def seg_masks(segments, kernel):
    masks_out = []
    for tap_index in range(kernel):
        offset = kernel - 1 - tap_index
        earlier = jnp.pad(segments, ((0, 0), (offset, 0)), constant_values=-1)[:, :segments.shape[1]]
        masks_out.append((earlier == segments).astype(jnp.float32))
    return masks_out

def mix_group(c_proj, b_proj, act_heads, step_size, decay_sum, seg_row):
    length = seg_row.shape[0]
    positions = jnp.arange(length)
    visible = (positions[:, None] >= positions[None, :]) & (seg_row[:, None] == seg_row[None, :])
    visible_f = visible.astype(jnp.float32)
    scores = low_back(jnp.dot(c_proj, b_proj.T, precision=PRECISE))
    log_decay = decay_sum[:, None, :] - decay_sum[None, :, :]
    decay_dt = jnp.exp(jnp.where(visible[:, :, None], log_decay, 0.0)) * visible_f[:, :, None] * step_size[None, :, :]
    weights = low(scores[:, :, None] * decay_dt)
    return low_back(jnp.einsum('ijh,jhp->ihp', weights, act_heads, precision=PRECISE))

def forward(hidden, norm_gain, in_weight, bc_weight, step_weight, conv_weight, conv_bias, step_bias, decay_log, skip_gain, gate_gain, out_weight, segments):
    groups, length = segments.shape
    inner_total = out_weight.shape[0]
    state_size = bc_weight.shape[1] // 2
    head_count = step_weight.shape[1]
    head_size = inner_total // head_count
    kernel = conv_weight.shape[0]
    norm_scale = lax.rsqrt(lax.optimization_barrier(jnp.mean(hidden * hidden, axis=-1, keepdims=True)) + EPS)
    normed = low(hidden * norm_scale * norm_gain)
    gate_pre = low_back(jnp.dot(normed, in_weight[0], precision=PRECISE))
    inner_pre = low_back(jnp.dot(normed, in_weight[1], precision=PRECISE))
    bc_pre = low_back(jnp.dot(normed, bc_weight, precision=PRECISE))
    step_pre = low_back(jnp.dot(normed, step_weight, precision=PRECISE)) + step_bias
    channels = jnp.concatenate([inner_pre, bc_pre], axis=1).reshape(groups, length, -1)
    conv_masks = seg_masks(segments, kernel)
    conv_out = conv_bias
    for tap_index in range(kernel):
        offset = kernel - 1 - tap_index
        conv_out = conv_out + conv_weight[tap_index] * shift_down(channels, offset) * conv_masks[tap_index][:, :, None]
    activated = jax.nn.silu(conv_out)
    inner_act = low(activated[:, :, :inner_total])
    b_proj = low(activated[:, :, inner_total:inner_total + state_size])
    c_proj = low(activated[:, :, inner_total + state_size:])
    step_size = jax.nn.softplus(step_pre).reshape(groups, length, head_count)
    decay_rate = -jnp.exp(decay_log)
    decay_sum = jnp.cumsum(step_size * decay_rate, axis=1)
    act_heads = inner_act.reshape(groups, length, head_count, head_size)
    mixer_out = lax.map(lambda pieces: jax.checkpoint(mix_group)(*pieces), (c_proj, b_proj, act_heads, step_size, decay_sum, segments))
    mixer_y = (mixer_out + skip_gain[:, None] * act_heads).reshape(groups * length, inner_total)
    gated = mixer_y * jax.nn.silu(gate_pre)
    gate_scale = lax.rsqrt(lax.optimization_barrier(jnp.mean(gated * gated, axis=-1, keepdims=True)) + EPS)
    gnormed = low(gated * gate_scale * gate_gain)
    return hidden + jnp.dot(gnormed, out_weight, precision=PRECISE)

def reference(hidden, segments, norm_gain, in_weight, bc_weight, step_weight, conv_weight, conv_bias, step_bias, decay_log, skip_gain, gate_gain, out_weight, cotangent):
    floats = tuple((array_in.astype(jnp.float32) for array_in in (hidden, norm_gain, in_weight, bc_weight, step_weight, conv_weight, conv_bias, step_bias, decay_log, skip_gain, gate_gain, out_weight)))

    def apply_block(*arrays):
        return forward(*arrays, segments)
    output, pullback = jax.vjp(apply_block, *floats)
    gradients = pullback(cotangent.astype(jnp.float32))
    return (output.astype(jnp.bfloat16), gradients[0], gradients[1], gradients[2], gradients[3], gradients[4], gradients[5], gradients[6], gradients[7], gradients[8], gradients[9], gradients[10], gradients[11])
```

```python
import jax
import jax.numpy as jnp
from jax import lax
from jax.experimental import pallas as pl
from jax.experimental.pallas import tpu as pltpu
from jax.sharding import PartitionSpec as P

EPS = 1e-05
LOG2E = 1.4426950408889634
BF = jnp.bfloat16
F32 = jnp.float32
LEN = 512
TILE = 128
BLOCK = 256
VMEM_BYTES = 50 * 1024 * 1024

SWAP = [(0, 1), (1, 0)]


def dp_index(x, z, y, c):
    return ((x * 2 + z) * 4 + y) * 2 + c


def dp_pairs(move):
    return [
        (dp_index(x, z, y, c), dp_index(*move(x, z, y, c)))
        for x in range(4)
        for z in range(2)
        for y in range(4)
        for c in range(2)
    ]


CORE = dp_pairs(lambda x, z, y, c: (x, z, y, 1 - c))
ZHI = dp_pairs(lambda x, z, y, c: (x, 1 - z, y, c))
XS = {k: dp_pairs(lambda x, z, y, c, k=k: ((x + k) % 4, z, y, c)) for k in (1, 2, 3)}
YS = {k: dp_pairs(lambda x, z, y, c, k=k: (x, z, (y + k) % 4, c)) for k in (1, 2, 3)}
PLANES = [[2 * i + c for i in range(32)] for c in range(2)]


def send(values, pairs):
    return lax.ppermute(values, "dp", pairs)


def swap_tensor(values):
    return lax.ppermute(values, "tensor", SWAP)


def place(pieces, spots, axis, count):
    shape = list(pieces[0].shape)
    shape.insert(axis, count)
    whole = jnp.zeros(tuple(shape), pieces[0].dtype)
    for piece, spot in zip(pieces, spots):
        start = [0] * len(shape)
        start[axis] = spot
        whole = lax.dynamic_update_slice(whole, jnp.expand_dims(piece, axis), tuple(start))
    return whole


def ring_gather(values, perms, here, axis):
    pieces = [values] + [send(values, perms[k]) for k in (1, 3, 2)]
    return place(pieces, [here, (here + 3) % 4, (here + 1) % 4, (here + 2) % 4], axis, 4)


def gather_rows(own, spot):
    x, z, y, c = spot
    half = own.shape[1] // 2
    mine = lax.dynamic_slice_in_dim(own, c * half, half, 1)
    got = send(lax.dynamic_slice_in_dim(own, (1 - c) * half, half, 1), CORE)
    rows = jnp.concatenate([jnp.where(c == 0, mine, got), jnp.where(c == 0, got, mine)], 0)
    other = send(rows, ZHI)
    both = jnp.stack([jnp.where(z == 0, rows, other), jnp.where(z == 0, other, rows)], 0)
    part_a = ring_gather(both[..., : half // 2], YS, y, 1)
    part_b = ring_gather(both[..., half // 2 :], XS, x, 0)
    part_a = ring_gather(part_a, XS, x, 0)
    part_b = ring_gather(part_b, YS, y, 2)
    peer_a, peer_b = send(part_a, CORE), send(part_b, CORE)
    return tuple(v.reshape(1536, half // 2) for v in (part_a, part_b, peer_a, peer_b))


def reduce_rows(own, peer, c):
    got = send(peer.astype(BF), CORE)
    pair = (own + got.astype(F32)).astype(BF).reshape(32, 48, own.shape[1])
    spread = lax.all_to_all(pair, "dp", 0, 0, tiled=True, axis_index_groups=PLANES)
    total = jnp.sum(spread.astype(F32), axis=0)
    mine = lax.dynamic_slice_in_dim(total, c * 24, 24, 0)
    other = send(lax.dynamic_slice_in_dim(total, (1 - c) * 24, 24, 0), CORE)
    return mine, other


def reduce_small(values):
    values = values + send(values, CORE)
    values = values + send(values, ZHI)
    for perms in (YS, XS):
        got = [send(values, perms[k]) for k in (1, 2, 3)]
        values = (values + got[1]) + (got[0] + got[2])
    return values


def dot(left, right):
    return jnp.dot(left, right, preferred_element_type=F32)


def dot_rows(left, right):
    return lax.dot_general(left, right, (((0,), (0,)), ((), ())), preferred_element_type=F32)


def dot_cols(left, right):
    return lax.dot_general(left, right, (((1,), (1,)), ((), ())), preferred_element_type=F32)


def silu_slope(values):
    sig = jax.nn.sigmoid(values)
    return sig * (1.0 + values * (1.0 - sig))


def down(values, offset):
    return values if offset == 0 else pltpu.roll(values, offset, 0)


def up(values, offset):
    return values if offset == 0 else pltpu.roll(values, values.shape[0] - offset, 0)


def conv_of(pre, taps, bias, masks):
    out = bias + taps[3:4] * pre
    for offset in (1, 2, 3):
        out = out + taps[3 - offset : 4 - offset] * (down(pre, offset) * masks[:, offset : offset + 1])
    return out


def lane_halves(values):
    low = lax.broadcasted_iota(jnp.int32, (1, TILE), 1) < 64
    zero = jnp.zeros_like(values)
    return jnp.where(low, values, zero), jnp.where(low, zero, values)


def params(semantics="arbitrary"):
    return pltpu.CompilerParams(dimension_semantics=(semantics,), vmem_limit_bytes=VMEM_BYTES)


def mix_kernel(normed, own_a, own_b, peer_a, peer_b, taps, bias, masks, scores, cols, rows, pre, act, mixed):
    step = pl.program_id(0)
    for test, weight in (
        (step < 2, own_a),
        (step == 2, own_b),
        ((step == 3) | (step == 4), peer_a),
        (step == 5, peer_b),
    ):

        @pl.when(test)
        def _(weight=weight):
            pre[...] = dot(normed[...], weight[...])

    conv_out = conv_of(pre[...], taps[...], bias[...], masks[...])
    act[...] = (conv_out * jax.nn.sigmoid(conv_out)).astype(BF)
    for pair in range(2):
        lanes = slice(pair * TILE, (pair + 1) * TILE)
        halves = lane_halves(act[:, lanes])
        for tile in range(4):
            here = slice(tile * TILE, (tile + 1) * TILE)
            weights, values = [], []
            for side in range(2):
                head = 2 * pair + side
                sums = cols[0, here, head : head + 1]
                if tile:
                    decay = jnp.exp2(sums - rows[0, 4 + head : 5 + head, : tile * TILE])
                    weights.append((scores[here, : tile * TILE] * decay).astype(BF))
                    values.append(halves[side][: tile * TILE])
                decay = jnp.exp2(
                    jnp.minimum(sums - rows[0, 4 + head : 5 + head, here], rows[0, 8 + head : 9 + head, here])
                )
                weights.append((scores[here, here] * decay).astype(BF))
                values.append(halves[side][here])
            mixed[here, lanes] = dot(jnp.concatenate(weights, 1), jnp.concatenate(values, 0))


def mix_forward(normed, weights, taps, bias, masks, scores, cols, rows):
    full = lambda *shape: pl.BlockSpec(shape, lambda i: (0,) * len(shape))
    block = lambda count: pl.BlockSpec((count, BLOCK), lambda i: (0, i))
    return pl.pallas_call(
        mix_kernel,
        grid=(6,),
        in_specs=[
            full(LEN, 1536),
            pl.BlockSpec((1536, BLOCK), lambda i: (0, jnp.minimum(i, 1))),
            pl.BlockSpec((1536, BLOCK), lambda i: (0, 0)),
            pl.BlockSpec((1536, BLOCK), lambda i: (0, jnp.clip(i - 3, 0, 1))),
            pl.BlockSpec((1536, BLOCK), lambda i: (0, 0)),
            block(4),
            block(1),
            full(LEN, 4),
            full(LEN, LEN),
            pl.BlockSpec((1, LEN, 16), lambda i: (i, 0, 0)),
            pl.BlockSpec((1, 16, LEN), lambda i: (i, 0, 0)),
        ],
        out_specs=[block(LEN)] * 3,
        out_shape=[
            jax.ShapeDtypeStruct((LEN, 1536), F32),
            jax.ShapeDtypeStruct((LEN, 1536), BF),
            jax.ShapeDtypeStruct((LEN, 1536), F32),
        ],
        compiler_params=params(),
        cost_estimate=pl.CostEstimate(flops=4_000_000_000, bytes_accessed=16_000_000, transcendentals=5_000_000),
        name="mix_forward",
    )(normed, *weights, taps, bias, masks, scores, cols, rows)


def gate_kernel(normed, cot, gate_own, gate_peer, out_own, out_peer, act, mixed, skip, gain, gate_pre, grad_gn, stats, squares, dots):
    step = pl.program_id(0)
    for test, gate_w, out_w in ((step < 3, gate_own, out_own), (step >= 3, gate_peer, out_peer)):

        @pl.when(test)
        def _(gate_w=gate_w, out_w=out_w):
            gate_pre[...] = dot(normed[...], gate_w[...])
            grad_gn[...] = dot(cot[...], out_w[...])

    @pl.when(step == 0)
    def _():
        squares[...] = jnp.zeros_like(squares)
        dots[...] = jnp.zeros_like(dots)

    pre = gate_pre[...]
    mixer_y = mixed[...] + skip[...] * act[...].astype(F32)
    gated = mixer_y * (pre * jax.nn.sigmoid(pre))
    square = gated * gated
    product = grad_gn[...] * gain[...] * gated
    squares[...] += square[:, :TILE] + square[:, TILE:]
    dots[...] += product[:, :TILE] + product[:, TILE:]

    @pl.when(step == 5)
    def _():
        stats[0:1, :] = jnp.sum(squares[...].T, axis=0, keepdims=True)
        stats[1:2, :] = jnp.sum(dots[...].T, axis=0, keepdims=True)
        stats[2:8, :] = jnp.zeros((6, LEN), F32)


def gate_forward(normed, cot, gate_w, out_w, act, mixed, skip, gain):
    full = lambda *shape: pl.BlockSpec(shape, lambda i: (0,) * len(shape))
    block = lambda count: pl.BlockSpec((count, BLOCK), lambda i: (0, i))
    early = pl.BlockSpec((1536, BLOCK), lambda i: (0, jnp.minimum(i, 2)))
    late = pl.BlockSpec((1536, BLOCK), lambda i: (0, jnp.maximum(i - 3, 0)))
    return pl.pallas_call(
        gate_kernel,
        grid=(6,),
        in_specs=[full(LEN, 1536), full(LEN, 1536), early, late, early, late, block(LEN), block(LEN), block(1), block(1)],
        out_specs=[block(LEN), block(LEN), full(8, LEN)],
        out_shape=[
            jax.ShapeDtypeStruct((LEN, 1536), F32),
            jax.ShapeDtypeStruct((LEN, 1536), F32),
            jax.ShapeDtypeStruct((8, LEN), F32),
        ],
        scratch_shapes=[pltpu.VMEM((LEN, TILE), F32)] * 2,
        compiler_params=params(),
        cost_estimate=pl.CostEstimate(flops=4_900_000_000, bytes_accessed=24_000_000, transcendentals=800_000),
        name="gate_forward",
    )(normed, cot, *gate_w, *out_w, act, mixed, skip, gain)


def slope_kernel(stats, gate_pre, grad_gn, act, mixed, skip, gain, gate_low, gnormed, grad_y, gain_grad, scale, dots):
    @pl.when(pl.program_id(0) == 0)
    def _():
        inv = lax.rsqrt(stats[0:1, :] * (1.0 / 3072.0) + EPS)
        scale[...] = jnp.broadcast_to(inv, (TILE, LEN)).T
        dots[...] = jnp.broadcast_to(inv * inv * inv * stats[1:2, :] * (1.0 / 3072.0), (TILE, LEN)).T

    for part in range(2):
        lanes = slice(part * TILE, (part + 1) * TILE)
        q = scale[...]
        pre = gate_pre[:, lanes]
        sig = jax.nn.sigmoid(pre)
        gate_act = pre * sig
        mixer_y = mixed[:, lanes] + skip[:, lanes] * act[:, lanes].astype(F32)
        gated = mixer_y * gate_act
        scaled = gated * q
        gnormed[:, lanes] = (scaled * gain[:, lanes]).astype(BF)
        upper = grad_gn[:, lanes]
        gain_grad[:, lanes] = jnp.sum(upper * scaled, axis=0, keepdims=True)
        grad_gated = q * gain[:, lanes] * upper - gated * dots[...]
        grad_y[:, lanes] = grad_gated * gate_act
        gate_low[:, lanes] = (grad_gated * mixer_y * (sig * (1.0 + pre * (1.0 - sig)))).astype(BF)


def gate_backward(stats, gate_pre, grad_gn, act, mixed, skip, gain):
    full = lambda *shape: pl.BlockSpec(shape, lambda i: (0,) * len(shape))
    block = lambda count: pl.BlockSpec((count, BLOCK), lambda i: (0, i))
    return pl.pallas_call(
        slope_kernel,
        grid=(6,),
        in_specs=[full(8, LEN), block(LEN), block(LEN), block(LEN), block(LEN), block(1), block(1)],
        out_specs=[block(LEN), block(LEN), block(LEN), block(1)],
        out_shape=[
            jax.ShapeDtypeStruct((LEN, 1536), BF),
            jax.ShapeDtypeStruct((LEN, 1536), BF),
            jax.ShapeDtypeStruct((LEN, 1536), F32),
            jax.ShapeDtypeStruct((1, 1536), F32),
        ],
        scratch_shapes=[pltpu.VMEM((LEN, TILE), F32)] * 2,
        compiler_params=params(),
        cost_estimate=pl.CostEstimate(flops=20_000_000, bytes_accessed=18_000_000, transcendentals=800_000),
        name="gate_backward",
    )(stats, gate_pre, grad_gn, act, mixed, skip, gain)


def back_kernel(grad_y, act, mixed, pre, scores, taps, bias, masks, cols, rows, skip, inner_low, sums, flows, grad_scores, grad_act):
    step = pl.program_id(0)

    @pl.when(step == 0)
    def _():
        grad_scores[...] = jnp.zeros_like(grad_scores)

    pairs = []
    for pair in range(2):
        lanes = slice(pair * TILE, (pair + 1) * TILE)
        low = grad_y[:, lanes].astype(BF)
        pairs.append((lane_halves(act[:, lanes]), low, lane_halves(low)))
    for tile in range(4):
        here = slice(tile * TILE, (tile + 1) * TILE)
        after = slice((tile + 1) * TILE, LEN)
        add_diag, add_rest = 0.0, 0.0
        for pair in range(2):
            act_halves, low, low_halves = pairs[pair]
            weights, values = [], []
            for side in range(2):
                head = 2 * pair + side
                back = cols[0, here, 4 + head : 5 + head]
                most = cols[0, here, 8 + head : 9 + head]
                mine = act_halves[side][here]
                decay = jnp.exp2(jnp.minimum(rows[0, head : head + 1, here] - back, most))
                grad_w = dot_cols(mine, low[here])
                add_diag = add_diag + grad_w * decay
                weights.append((scores[here, here] * decay).astype(BF))
                values.append(low_halves[side][here])
                if tile < 3:
                    decay = jnp.exp2(rows[0, head : head + 1, after] - back)
                    grad_w = dot_cols(mine, low[after])
                    add_rest = add_rest + grad_w * decay
                    weights.append((scores[here, after] * decay).astype(BF))
                    values.append(low_halves[side][after])
            lanes = slice(pair * TILE, (pair + 1) * TILE)
            grad_act[here, lanes] = dot(jnp.concatenate(weights, 1), jnp.concatenate(values, 0))
        grad_scores[here, here] += add_diag
        if tile < 3:
            grad_scores[here, after] += add_rest

    low_lane = lax.broadcasted_iota(jnp.int32, (1, TILE), 1) < 64
    for pair in range(2):
        lanes = slice(pair * TILE, (pair + 1) * TILE)
        values = act[:, lanes].astype(F32)
        grad = grad_y[:, lanes]
        row_flow = grad.astype(BF).astype(F32) * mixed[:, lanes]
        col_flow = values * grad_act[:, lanes]
        for side, mask in ((0, low_lane), (1, ~low_lane)):
            head = 2 * pair + side
            flows[0, :, head : head + 1] = jnp.sum(jnp.where(mask, row_flow, 0.0), axis=1, keepdims=True)
            flows[0, :, 4 + head : 5 + head] = jnp.sum(jnp.where(mask, col_flow, 0.0), axis=1, keepdims=True)
        taps_l, masks_v = taps[:, lanes], masks[...]
        pre_l = pre[:, lanes]
        conv_out = conv_of(pre_l, taps_l, bias[:, lanes], masks_v)
        grad_conv = (grad_act[:, lanes] + skip[:, lanes] * grad) * silu_slope(conv_out)
        grad_pre = taps_l[3:4] * grad_conv
        sums[3:4, lanes] = jnp.sum(grad_conv * pre_l, axis=0, keepdims=True)
        for offset in (1, 2, 3):
            masked = grad_conv * masks_v[:, offset : offset + 1]
            tap = 3 - offset
            sums[tap : tap + 1, lanes] = jnp.sum(masked * down(pre_l, offset), axis=0, keepdims=True)
            grad_pre = grad_pre + taps_l[tap : tap + 1] * up(masked, offset)
        sums[4:5, lanes] = jnp.sum(grad_conv, axis=0, keepdims=True)
        sums[5:6, lanes] = jnp.sum(grad * values, axis=0, keepdims=True)
        sums[6:8, lanes] = jnp.zeros((2, TILE), F32)
        inner_low[:, lanes] = grad_pre.astype(BF)


def mix_backward(grad_y, act, mixed, pre, scores_t, taps, bias, masks, cols, rows, skip):
    full = lambda *shape: pl.BlockSpec(shape, lambda i: (0,) * len(shape))
    block = lambda count: pl.BlockSpec((count, BLOCK), lambda i: (0, i))
    return pl.pallas_call(
        back_kernel,
        grid=(6,),
        in_specs=[
            block(LEN),
            block(LEN),
            block(LEN),
            block(LEN),
            full(LEN, LEN),
            block(4),
            block(1),
            full(LEN, 4),
            pl.BlockSpec((1, LEN, 16), lambda i: (i, 0, 0)),
            pl.BlockSpec((1, 16, LEN), lambda i: (i, 0, 0)),
            block(1),
        ],
        out_specs=[
            block(LEN),
            block(8),
            pl.BlockSpec((1, LEN, 8), lambda i: (i, 0, 0)),
            full(LEN, LEN),
        ],
        out_shape=[
            jax.ShapeDtypeStruct((LEN, 1536), BF),
            jax.ShapeDtypeStruct((8, 1536), F32),
            jax.ShapeDtypeStruct((6, LEN, 8), F32),
            jax.ShapeDtypeStruct((LEN, LEN), F32),
        ],
        scratch_shapes=[pltpu.VMEM((LEN, BLOCK), F32)],
        compiler_params=params(),
        cost_estimate=pl.CostEstimate(flops=4_000_000_000, bytes_accessed=14_000_000, transcendentals=5_000_000),
        name="mix_backward",
    )(grad_y, act, mixed, pre, scores_t, taps, bias, masks, cols, rows, skip)


def on_device(
    hidden,
    segments,
    norm_gain,
    in_weight,
    bc_weight,
    step_weight,
    conv_weight,
    conv_bias,
    step_bias,
    decay_log,
    skip_gain,
    gate_gain,
    out_weight,
    cotangent,
):
    t = lax.axis_index("tensor")
    d = lax.axis_index("dp")
    spot = (d // 16, (d // 8) % 2, (d // 2) % 4, d % 2)
    c = spot[3]

    def tokens(mine):
        other = swap_tensor(mine)
        return jnp.concatenate([jnp.where(t == 0, mine, other), jnp.where(t == 0, other, mine)], 0)

    def own_first(values, size):
        base = 2 * t * size
        return jnp.concatenate(
            [
                lax.dynamic_slice_in_dim(values, base + c * size, size, values.ndim - 1),
                lax.dynamic_slice_in_dim(values, base + (1 - c) * size, size, values.ndim - 1),
            ],
            values.ndim - 1,
        )

    def natural(values, size):
        return jnp.where(c == 0, values, jnp.concatenate([values[..., size:], values[..., :size]], -1))

    hidden_all = tokens(hidden)
    step_pad = jnp.zeros((24, 116), BF)
    first = jnp.concatenate(
        [
            piece
            for j in range(2)
            for piece in (
                in_weight[1][:, j * 768 : (j + 1) * 768],
                bc_weight[:, j * 128 : (j + 1) * 128],
                step_weight[:, j * 12 : (j + 1) * 12],
                step_pad,
            )
        ],
        1,
    )
    out_rows = out_weight.T
    second = jnp.concatenate(
        [
            piece
            for j in range(2)
            for piece in (in_weight[0][:, j * 768 : (j + 1) * 768], out_rows[:, j * 768 : (j + 1) * 768])
        ],
        1,
    )
    inner_w = gather_rows(first, spot)
    own_a, own_b, peer_a, peer_b = inner_w
    gate_own, out_own, gate_peer, out_peer = gather_rows(second, spot)
    cot_all = tokens(cotangent)

    resid = hidden_all.astype(F32)
    norm_scale = lax.rsqrt(jnp.mean(resid * resid, axis=-1, keepdims=True) + EPS)
    normed = (resid * norm_scale * norm_gain).astype(BF)

    taps = own_first(conv_weight[:, :3072], 768)
    bias = own_first(conv_bias[None, :3072], 768)
    gain = own_first(gate_gain[None, :], 768)
    skip = jnp.repeat(own_first(skip_gain, 12), 64)[None, :]
    rate = -jnp.exp(own_first(decay_log, 12))
    step_off = own_first(step_bias, 12)

    seg = segments[0]
    masks = jnp.stack(
        [(jnp.pad(seg, (o, 0), constant_values=-1)[:LEN] == seg).astype(F32) for o in range(4)], 1
    )
    where_at = jnp.arange(LEN)
    visible = ((where_at[:, None] >= where_at[None, :]) & (seg[:, None] == seg[None, :])).astype(F32)

    tail_own = dot(normed, own_b[:, 256:])
    tail_peer = dot(normed, peer_b[:, 256:])
    bc_pre = jnp.concatenate(
        [
            jnp.where(c == 0, tail_own, tail_peer)[:, :128],
            jnp.where(c == 0, tail_peer, tail_own)[:, :128],
        ],
        1,
    )
    bc_taps, bc_bias = conv_weight[:, 3072:], conv_bias[3072:]

    def shifted(values, offset):
        return values if offset == 0 else jnp.pad(values, ((offset, 0), (0, 0)))[:LEN]

    bc_conv = bc_bias
    for o in range(4):
        bc_conv = bc_conv + bc_taps[3 - o] * shifted(bc_pre, o) * masks[:, o : o + 1]
    bc_act = jax.nn.silu(bc_conv).astype(BF)
    b_proj, c_proj = bc_act[:, :128], bc_act[:, 128:]
    scores = dot_cols(c_proj, b_proj) * visible
    scores_t = dot_cols(b_proj, c_proj) * visible.T

    step_pre = jnp.concatenate([tail_own[:, 128:140], tail_peer[:, 128:140]], 1) + step_off
    step_size = jax.nn.softplus(step_pre)
    decay_sum = jnp.cumsum(step_size * rate, axis=0)
    sums2 = decay_sum * LOG2E
    log_step = jnp.log2(step_size)
    back2 = sums2 - log_step
    cols = jnp.concatenate(
        [v.reshape(LEN, 6, 4) for v in (sums2, back2, log_step, jnp.zeros_like(sums2))], 2
    ).transpose(1, 0, 2)
    rows = cols.transpose(0, 2, 1)

    pre, act, mixed_y = mix_forward(normed, inner_w, taps, bias, masks, scores, cols, rows)
    gate_pre, grad_gn, stats = gate_forward(
        normed, cot_all, (gate_own, gate_peer), (out_own, out_peer), act, mixed_y, skip, gain
    )
    stats = stats + swap_tensor(stats)
    gate_low, gnormed, grad_y, gain_grad = gate_backward(stats, gate_pre, grad_gn, act, mixed_y, skip, gain)

    def own_tokens(values):
        values = values.astype(BF)
        got = swap_tensor(lax.dynamic_slice_in_dim(values, (1 - t) * 256, 256, 0))
        return lax.dynamic_slice_in_dim(values, t * 256, 256, 0).astype(F32) + got.astype(F32)

    branch = own_tokens(dot_cols(gnormed[:, :768], out_own) + dot_cols(gnormed[:, 768:], out_peer))
    mixed = (hidden.astype(F32) + branch).astype(BF)

    inner_low, sums, flows, grad_scores = mix_backward(
        grad_y, act, mixed_y, pre, scores_t, taps, bias, masks, cols, rows, skip
    )

    grad_scores = grad_scores * visible.T
    grad_scores = (grad_scores + swap_tensor(grad_scores.astype(BF)).astype(F32)).astype(BF)
    grad_c = dot_rows(grad_scores, b_proj)
    grad_b = dot(grad_scores, c_proj)
    bc_grad = jnp.concatenate([grad_b, grad_c], 1) * silu_slope(bc_conv)
    bc_grad_pre = 0.0
    bc_tap_grads = []
    for tap in range(4):
        o = 3 - tap
        part = bc_grad * masks[:, o : o + 1]
        moved = part if o == 0 else jnp.pad(part, ((0, o), (0, 0)))[o:]
        bc_grad_pre = bc_grad_pre + bc_taps[tap] * moved
        bc_tap_grads.append(jnp.sum(part * shifted(bc_pre, o), axis=0))
    bc_tap_grads.append(jnp.sum(bc_grad, axis=0))
    bc_low = bc_grad_pre.astype(BF)

    flows = flows.transpose(1, 0, 2)
    row_flow, col_flow = flows[:, :, :4].reshape(LEN, 24), flows[:, :, 4:].reshape(LEN, 24)
    grad_rate = jnp.cumsum((row_flow - col_flow)[::-1], axis=0)[::-1]
    step_sig = jax.nn.sigmoid(step_pre)
    tiny = step_size < 1e-30
    ratio = jnp.where(tiny, 1.0, step_sig / jnp.where(tiny, 1.0, step_size))
    grad_step_pre = col_flow * ratio + grad_rate * rate * step_sig
    decay_grad = jnp.sum(grad_rate * step_size, axis=0) * rate
    step_bias_grad = jnp.sum(grad_step_pre, axis=0)
    skip_grad = jnp.sum(sums[5].reshape(24, 64), axis=1)
    step_low = grad_step_pre.astype(BF)

    pad_cols = lambda v: jnp.pad(v, ((0, 0), (0, 116)))
    own_tail = jnp.concatenate(
        [jnp.where(c == 0, bc_low[:, :128], bc_low[:, 128:]), pad_cols(step_low[:, :12])], 1
    )
    peer_tail = jnp.concatenate(
        [jnp.where(c == 0, bc_low[:, 128:], bc_low[:, :128]), pad_cols(step_low[:, 12:])], 1
    )
    only_first = jnp.concatenate(
        [jnp.broadcast_to((t == 0).astype(BF), (128,)), jnp.ones((128,), BF)]
    )
    grad_normed = (
        dot_cols(gate_low[:, :768], gate_own)
        + dot_cols(gate_low[:, 768:], gate_peer)
        + dot_cols(inner_low[:, :512], own_a)
        + dot_cols(inner_low[:, 768:1280], peer_a)
        + dot_cols(jnp.concatenate([inner_low[:, 512:768], own_tail * only_first], 1), own_b)
        + dot_cols(jnp.concatenate([inner_low[:, 1280:], peer_tail * only_first], 1), peer_b)
    )
    norm_gain_grad = jnp.sum(grad_normed * resid * norm_scale, axis=0)
    grad_mine = own_tokens(grad_normed)
    mine = hidden.astype(F32)
    scale_mine = lax.dynamic_slice_in_dim(norm_scale, t * 256, 256, 0)
    pre_stat = jnp.sum(grad_mine * norm_gain * mine, axis=-1, keepdims=True)
    grad_hidden = (
        cotangent.astype(F32)
        + scale_mine * norm_gain * grad_mine
        - mine * scale_mine**3 * pre_stat / 1536
    )

    low_own = jnp.concatenate([inner_low[:, :768], own_tail, gate_low[:, :768]], 1)
    low_peer = jnp.concatenate([inner_low[:, 768:], peer_tail, gate_low[:, 768:]], 1)
    part_own = jnp.concatenate([dot_rows(normed, low_own), dot_rows(cot_all, gnormed[:, :768])], 1)
    part_peer = jnp.concatenate([dot_rows(normed, low_peer), dot_rows(cot_all, gnormed[:, 768:])], 1)
    rows_own, rows_peer = reduce_rows(part_own, part_peer, c)

    def halves(start, size):
        mine_cols = rows_own[:, start : start + size]
        other_cols = rows_peer[:, start : start + size]
        return jnp.concatenate(
            [jnp.where(c == 0, mine_cols, other_cols), jnp.where(c == 0, other_cols, mine_cols)], 1
        )

    grad_in = jnp.stack([halves(1024, 768), halves(0, 768)])
    grad_bc = halves(768, 128)
    grad_step = halves(896, 12)
    grad_out = halves(1792, 768).T

    misc = jnp.concatenate(
        [
            jnp.stack(bc_tap_grads).reshape(-1),
            natural(step_bias_grad, 12),
            natural(decay_grad, 12),
            natural(skip_grad, 12),
            jnp.zeros((184,), F32),
        ]
    )
    small = jnp.concatenate(
        [natural(jnp.concatenate([sums[:5], gain_grad], 0), 768), norm_gain_grad[None], misc[None]], 0
    )
    small = reduce_small(small)
    small_other = swap_tensor(small)
    both = jnp.concatenate(
        [jnp.where(t == 0, small, small_other), jnp.where(t == 0, small_other, small)], 1
    )
    bc_sums = small[7, :1280].reshape(5, 256)
    heads = jnp.concatenate([both[7, 1280:1352].reshape(3, 24), both[7, 2816:2888].reshape(3, 24)], 1)
    return (
        mixed,
        grad_hidden,
        small[6] + small_other[6],
        grad_in,
        grad_bc,
        grad_step,
        jnp.concatenate([both[:4], bc_sums[:4]], 1),
        jnp.concatenate([both[4], bc_sums[4]]),
        heads[0],
        heads[1],
        heads[2],
        both[5],
        grad_out,
    )


def solution(mesh):
    return jax.shard_map(
        on_device,
        mesh=mesh,
        in_specs=(
            P(("dp", "tensor"), None),
            P("dp", None),
            P(),
            P(None, "dp", "tensor"),
            P("dp", None),
            P("dp", "tensor"),
            P(),
            P(),
            P(),
            P(),
            P(),
            P(),
            P("tensor", "dp"),
            P(("dp", "tensor"), None),
        ),
        out_specs=(
            P(("dp", "tensor"), None),
            P(("dp", "tensor"), None),
            P(),
            P(None, "dp", "tensor"),
            P("dp", None),
            P("dp", "tensor"),
            P(),
            P(),
            P(),
            P(),
            P(),
            P(),
            P("tensor", "dp"),
        ),
        check_vma=False,
    )
```

```python
import jax
import jax.numpy as jnp
from jax import lax
from jax.experimental import pallas as pl
from jax.experimental.pallas import tpu as pltpu
from jax.sharding import PartitionSpec as P

EPS = 1e-05
LOG2E = 1.4426950408889634
BF = jnp.bfloat16
F32 = jnp.float32
LEN = 512
TILE = 128
BLOCK = 256
QUICK = pl.CostEstimate(flops=1000, bytes_accessed=1000, transcendentals=0)

SWAP = [(0, 1), (1, 0)]


def dp_index(x, z, y, c):
    return ((x * 2 + z) * 4 + y) * 2 + c


def dp_pairs(move):
    return [
        (dp_index(x, z, y, c), dp_index(*move(x, z, y, c)))
        for x in range(4)
        for z in range(2)
        for y in range(4)
        for c in range(2)
    ]


CORE = dp_pairs(lambda x, z, y, c: (x, z, y, 1 - c))
ZHI = dp_pairs(lambda x, z, y, c: (x, 1 - z, y, c))
XS = {k: dp_pairs(lambda x, z, y, c, k=k: ((x + k) % 4, z, y, c)) for k in (1, 2, 3)}
YS = {k: dp_pairs(lambda x, z, y, c, k=k: (x, z, (y + k) % 4, c)) for k in (1, 2, 3)}


def send(values, pairs):
    return lax.ppermute(values, "dp", pairs)


def swap_tensor(values):
    return lax.ppermute(values, "tensor", SWAP)


def near_core(shape, kind):
    return pltpu.VMEM(shape, kind)


def anywhere(count):
    return [pl.BlockSpec(memory_space=pl.ANY)] * count


def in_vmem(count):
    return [pl.BlockSpec(memory_space=pltpu.VMEM)] * count


def after(values, *first):
    return pl.pallas_call(
        lambda *refs: None,
        in_specs=anywhere(1 + len(first)),
        out_specs=pl.BlockSpec(memory_space=pl.ANY),
        out_shape=jax.ShapeDtypeStruct(values.shape, values.dtype),
        input_output_aliases={0: 0},
        cost_estimate=QUICK,
        name="after",
    )(values, *first)


def sides(values, perms):
    return [values, send(values, perms[1]), send(values, perms[3])]


def opposite(pieces, perms, axis, *first):
    half = pieces[0].shape[axis] // 2
    front = lax.slice_in_dim(pieces[1], 0, half, axis=axis)
    back = lax.slice_in_dim(pieces[2], half, 2 * half, axis=axis)
    if first:
        front, back = after(front, *first), after(back, *first)
    return [send(front, perms[1]), send(back, perms[3])]


def ring(values, perms):
    return [values] + [send(values, perms[k]) for k in (1, 3, 2)]


BACK = (0, 1, 3, 2)


def copy_all(copies, sems):
    started = [pltpu.make_async_copy(source, target, sems.at[i]) for i, (source, target) in enumerate(copies)]
    for copy in started:
        copy.start()
    for copy in started:
        copy.wait()


def place_near(a_pieces, b_pieces, start, width, first=()):
    def kernel(*refs):
        d = lax.axis_index("dp")
        x, y = d // 16, (d // 2) % 4
        a_whole, b_whole, sems = refs[8 + len(first) :]
        copies = []
        for i, back in enumerate(BACK):
            at_y, at_x = lax.rem(y + 4 - back, 4), lax.rem(x + 4 - back, 4)
            copies.append((refs[i].at[:, :, pl.ds(start, width)], a_whole.at[:, at_y]))
            copies.append((refs[4 + i].at[:, :, pl.ds(start, width)], b_whole.at[at_x]))
        copy_all(copies, sems)

    return pl.pallas_call(
        kernel,
        in_specs=in_vmem(8) + anywhere(len(first)),
        out_specs=in_vmem(2),
        out_shape=[jax.ShapeDtypeStruct(shape, BF) for shape in ((2, 4, 48, width), (4, 2, 48, width))],
        scratch_shapes=[pltpu.SemaphoreType.DMA((8,))],
        compiler_params=pltpu.CompilerParams(vmem_limit_bytes=16 * 1024 * 1024),
        cost_estimate=QUICK,
        name="place_near",
    )(*a_pieces, *b_pieces, *first)


def place_far(a_pieces, b_pieces, columns, first=()):
    count = a_pieces[0].shape[-1] // columns

    def kernel(*refs):
        d = lax.axis_index("dp")
        x, y = d // 16, (d // 2) % 4
        whole, sems = refs[10 + len(first) :]
        copies = []
        for i, back in enumerate((0, 1, 3, 2, 2)):
            at_y, at_x = lax.rem(y + 4 - back, 4), lax.rem(x + 4 - back, 4)
            for j in range(count):
                lanes = pl.ds(j * columns, columns)
                z = pl.ds(i - 3, 1) if i > 2 else pl.ds(0, 2)
                xs = pl.ds(2 * (i - 3), 2) if i > 2 else pl.ds(0, 4)
                copies.append((refs[i].at[:, :, :, lanes], whole.at[j, at_x, z]))
                copies.append((refs[5 + i].at[:, :, :, lanes], whole.at[count + j, xs, :, at_y]))
        copy_all(copies, sems)

    return pl.pallas_call(
        kernel,
        in_specs=in_vmem(10) + anywhere(len(first)),
        out_specs=pl.BlockSpec(memory_space=pltpu.VMEM),
        out_shape=jax.ShapeDtypeStruct((2 * count, 4, 2, 4, 48, columns), BF),
        scratch_shapes=[pltpu.SemaphoreType.DMA((10 * count,))],
        compiler_params=pltpu.CompilerParams(vmem_limit_bytes=24 * 1024 * 1024),
        cost_estimate=QUICK,
        name="place_far",
    )(*a_pieces, *b_pieces, *first).reshape(2 * count, 1536, columns)


def pack_kernel(in_weight, bc_weight, step_weight, out_weight, mine, other):
    c = lax.rem(lax.axis_index("dp"), 2)
    out_rows = out_weight[...].T
    steps = step_weight[...]
    for target, half in ((mine, c), (other, 1 - c)):
        at = pl.multiple_of(half * 768, 128)
        target[:, 0:512] = in_weight[1, :, pl.ds(at, 512)]
        target[:, 512:1280] = in_weight[0, :, pl.ds(at, 768)]
        target[:, 1280:1536] = in_weight[1, :, pl.ds(pl.multiple_of(at + 512, 128), 256)]
        target[:, 1536:1664] = bc_weight[:, pl.ds(pl.multiple_of(half * 128, 128), 128)]
        second = jnp.full((24, 12), half) == 1
        own = jnp.where(second, steps[:, 12:].astype(F32), steps[:, :12].astype(F32))
        gap = jnp.zeros((24, 4), F32)
        parts = [own[:, 0:4], gap, own[:, 4:8], gap, own[:, 8:12], jnp.zeros((24, 108), F32)]
        target[:, 1664:1792] = jnp.concatenate(parts, 1).astype(BF)
        wanted = jnp.full((24, 768), half) == 1
        pieces = (out_rows[:, 768:].astype(F32), out_rows[:, :768].astype(F32))
        target[:, 1792:2560] = jnp.where(wanted, *pieces).astype(BF)


def pack(in_weight, bc_weight, step_weight, out_weight):
    return pl.pallas_call(
        pack_kernel,
        in_specs=in_vmem(4),
        out_specs=in_vmem(2),
        out_shape=[jax.ShapeDtypeStruct((24, 2560), BF)] * 2,
        compiler_params=pltpu.CompilerParams(vmem_limit_bytes=16 * 1024 * 1024),
        cost_estimate=QUICK,
        name="pack",
    )(in_weight, bc_weight, step_weight, out_weight)


def pair_rows(mine, other, c):
    got = send(other, CORE)
    return jnp.concatenate([jnp.where(c == 0, mine, got), jnp.where(c == 0, got, mine)], 0)


def pair_planes(rows, z):
    other = send(rows, ZHI)
    return jnp.stack([jnp.where(z == 0, rows, other), jnp.where(z == 0, other, rows)], 0)


def here():
    d = lax.axis_index("dp")
    return d // 16, (d // 2) % 4


def ahead(at, k):
    return lax.rem(at + k, 4)


def pieces_kernel(by_x, own, widths, left, *refs):
    rights, refs = refs[: len(widths)], refs[len(widths) :]
    got = refs[0] if own else None
    outs = refs[1:6] if own else refs[:1]
    x, y = here()
    right = jnp.concatenate([r[:, a:b] if len(r.shape) == 2 else r[a] for r, (a, b) in zip(rights, widths)], 1)

    def write(k, part, values):
        if not own:
            outs[0][(k, *part)] = values.astype(BF)
            return
        values = values + got[(k, *part)].astype(F32)
        if k == 2 and by_x:
            outs[3][...] = values[:192].astype(BF)
            outs[4][...] = values[192:].astype(BF)
        elif k == 2:
            outs[3 + part[0] // 2][part[0] % 2, part[1]] = values.astype(BF)
        else:
            outs[(0, 1, None, 2)[k]][part or Ellipsis] = values

    if by_x:
        for k in range(4):
            rows = pl.ds(pl.multiple_of(ahead(x, k) * 384, 128), 384)
            write(k, (), dot_rows(left[:, rows], right))
    else:
        whole = refs[-1]
        for i in range(4):
            whole[i] = dot_rows(left[:, i * 384 : (i + 1) * 384], right)
        for k in range(4):
            for i in range(4):
                for z in range(2):
                    rows = pl.ds(pl.multiple_of((z * 4 + ahead(y, k)) * 48, 16), 48)
                    write(k, (i, z), whole[i, rows, :])


def weight_pieces(by_x, left, rights, widths, got=(), first=()):
    width = sum(b - a if r.ndim == 2 else b for r, (a, b) in zip(rights, widths))
    shape = (384, width) if by_x else (4, 2, 48, width)
    if got:
        near, far = jax.ShapeDtypeStruct(shape, F32), jax.ShapeDtypeStruct((shape[0] // 2, *shape[1:]), BF)
        outs = [near] * 3 + [far] * 2
    else:
        outs = jax.ShapeDtypeStruct((4, *shape), BF)
    count = 1 + len(rights) + len(got)

    def kernel(*refs):
        pieces_kernel(by_x, bool(got), widths, *refs[:count], *refs[count + len(first) :])

    return pl.pallas_call(
        kernel,
        in_specs=in_vmem(count) + anywhere(len(first)),
        out_specs=in_vmem(5) if got else in_vmem(1)[0],
        out_shape=outs,
        scratch_shapes=[] if by_x else [pltpu.VMEM((4, 384, width), F32)],
        compiler_params=pltpu.CompilerParams(vmem_limit_bytes=24 * 1024 * 1024),
        cost_estimate=QUICK,
        name="weight_pieces",
    )(left, *rights, *got, *first)


def pass_kernel(plus, minus, left, right, *refs):
    on, back = refs[-2:]
    half = left.shape[0]
    on[:half] = (plus[:half] + left[...].astype(F32)).astype(BF)
    on[half:] = plus[half:].astype(BF)
    back[:half] = minus[:half].astype(BF)
    back[half:] = (minus[half:] + right[...].astype(F32)).astype(BF)


def pass_on(by_x, pieces, *first):
    perms = XS if by_x else YS
    left, right = send(pieces[3], perms[1]), send(pieces[4], perms[3])
    shape = jax.ShapeDtypeStruct(pieces[1].shape, BF)
    return pl.pallas_call(
        pass_kernel,
        in_specs=in_vmem(4) + anywhere(len(first)),
        out_specs=in_vmem(2),
        out_shape=[shape, shape],
        compiler_params=pltpu.CompilerParams(vmem_limit_bytes=16 * 1024 * 1024),
        cost_estimate=QUICK,
        name="pass_on",
    )(pieces[1], pieces[2], left, right, *first)


def near_sum_kernel(by_x, own, one, two, *outs):
    outs = outs[-5:]
    x, y = here()
    total = own[...] + one[...].astype(F32) + two[...].astype(F32)
    whole = outs[4]
    whole[...] = total.reshape(whole.shape)
    for k in range(4):
        if by_x:
            for z in range(2):
                outs[k][z] = whole[z, ahead(y, k)].astype(outs[k].dtype)
        else:
            outs[k][...] = whole[ahead(x, k)].astype(outs[k].dtype)


def near_sum(by_x, own, got, first):
    width = own.shape[-1]
    shape = (2, 48, width)
    return pl.pallas_call(
        lambda *refs: near_sum_kernel(by_x, *refs),
        in_specs=in_vmem(3) + anywhere(len(first)),
        out_specs=in_vmem(4),
        out_shape=[jax.ShapeDtypeStruct(shape, F32)] + [jax.ShapeDtypeStruct(shape, BF)] * 3,
        scratch_shapes=[pltpu.VMEM((2, 4, 48, width) if by_x else (4, 2, 48, width), F32)],
        compiler_params=pltpu.CompilerParams(vmem_limit_bytes=16 * 1024 * 1024),
        cost_estimate=QUICK,
        name="near_sum",
    )(own, *got, *first)


def scatter_near(by_x, pieces, passed, *first):
    near = XS if by_x else YS
    return near_sum(by_x, pieces[0], [send(passed[0], near[1]), send(passed[1], near[3])], first)


def scatter_far(by_x, pieces):
    far = YS if by_x else XS
    got = [send(pieces[k], far[k]).astype(F32) for k in (1, 2, 3)]
    return pieces[0] + got[1] + (got[0] + got[2])


def plane_sum(values, z):
    other = lax.dynamic_index_in_dim(values, 1 - z, 0, keepdims=False).astype(BF)
    return lax.dynamic_index_in_dim(values, z, 0, keepdims=False) + send(other, ZHI).astype(F32)


def own_rows(total, c):
    mine = lax.dynamic_slice_in_dim(total, c * 24, 24, 0)
    other = send(lax.dynamic_slice_in_dim(total, (1 - c) * 24, 24, 0), CORE)
    return jnp.where(c == 0, mine, other), jnp.where(c == 0, other, mine)


def reduce_small(values):
    values = values + send(values, CORE)
    early = values = values + send(values, ZHI)
    for perms in (YS, XS):
        got = [send(values, perms[k]) for k in (1, 2, 3)]
        values = (values + got[1]) + (got[0] + got[2])
    return values, early


def dot(left, right):
    return jnp.dot(left, right, preferred_element_type=F32)


def dot_rows(left, right):
    return lax.dot_general(left, right, (((0,), (0,)), ((), ())), preferred_element_type=F32)


def dot_cols(left, right):
    return lax.dot_general(left, right, (((1,), (1,)), ((), ())), preferred_element_type=F32)


def silu_slope(values):
    sig = jax.nn.sigmoid(values)
    return sig * (1.0 + values * (1.0 - sig))


def down(values, offset):
    return values if offset == 0 else pltpu.roll(values, offset, 0)


def up(values, offset):
    return values if offset == 0 else pltpu.roll(values, values.shape[0] - offset, 0)


def conv_of(pre, taps, bias, masks):
    out = bias + taps[3:4] * pre
    for offset in (1, 2, 3):
        out = out + taps[3 - offset : 4 - offset] * (down(pre, offset) * masks[:, offset : offset + 1])
    return out


def lane_halves(values):
    low = lax.broadcasted_iota(jnp.int32, (1, TILE), 1) < 64
    zero = jnp.zeros_like(values)
    return jnp.where(low, values, zero), jnp.where(low, zero, values)


def params(mebibytes):
    return pltpu.CompilerParams(dimension_semantics=("arbitrary",), vmem_limit_bytes=mebibytes * 1024 * 1024)


def full(*shape):
    return pl.BlockSpec(shape, lambda i: (0,) * len(shape), pipeline_mode=pl.Buffered(1))


def out_full(*shape):
    return pl.BlockSpec(shape, lambda i: (0,) * len(shape))


def block(count):
    return pl.BlockSpec((count, BLOCK), lambda i: (0, i))


WIDE = 384


def wide(count):
    return pl.BlockSpec((count, WIDE), lambda i: (0, i))


def running(values):
    row = lax.broadcasted_iota(jnp.int32, values.shape, 0)
    offset = 1
    while offset < values.shape[0]:
        values = values + jnp.where(row >= offset, pltpu.roll(values, offset, 0), 0.0)
        offset *= 2
    return values


def visible_of(seg_col, seg_row, later_rows):
    row = lax.broadcasted_iota(jnp.int32, (LEN, LEN), 0)
    col = lax.broadcasted_iota(jnp.int32, (LEN, LEN), 1)
    ordered = (row <= col) if later_rows else (row >= col)
    return ordered & (seg_col[...] == seg_row[...])


def prep_kernel(normed, tail_own, tail_peer, seg_col, seg_row, masks, taps, bias, heads, scores, scores_t, act, pre, cols, rows, steps):
    own = dot(normed[...], tail_own[0])
    peer = dot(normed[...], tail_peer[0])
    core0 = jnp.full((LEN, TILE), lax.rem(lax.axis_index("dp"), 2)) == 0
    pre[:, :TILE] = jnp.where(core0, own[:, :TILE], peer[:, :TILE])
    pre[:, TILE:] = jnp.where(core0, peer[:, :TILE], own[:, :TILE])
    conv_out = conv_of(pre[...], taps[...], bias[...], masks[...])
    act[...] = (conv_out * jax.nn.sigmoid(conv_out)).astype(BF)
    b_proj, c_proj = act[:, :TILE], act[:, TILE:]
    scores[...] = jnp.where(visible_of(seg_col, seg_row, False), dot_cols(c_proj, b_proj), 0.0)
    scores_t[...] = jnp.where(visible_of(seg_col, seg_row, True), dot_cols(b_proj, c_proj), 0.0)
    step_pre = own[:, TILE:] + pltpu.roll(peer[:, TILE:], 24, 1) + heads[0:1, :]
    step_size = jnp.maximum(step_pre, 0.0) + jnp.log1p(jnp.exp(-jnp.abs(step_pre)))
    sums = running(step_size * heads[1:2, :]) * LOG2E
    logs = jnp.log(step_size) * LOG2E
    steps[0] = step_pre
    steps[1] = step_size
    for i, values in enumerate((sums, sums - logs, logs)):
        cols[i] = values
        rows[i] = values.T


def prepare(normed, inner_own, inner_peer, seg_col, seg_row, masks, taps, bias, heads):
    tail = pl.BlockSpec((1, 1536, 256), lambda i: (3, 0, 0), pipeline_mode=pl.Buffered(1))
    shapes = [
        ((LEN, LEN), F32),
        ((LEN, LEN), F32),
        ((LEN, 256), BF),
        ((LEN, 256), F32),
        ((3, LEN, TILE), F32),
        ((3, TILE, LEN), F32),
        ((2, LEN, TILE), F32),
    ]
    return pl.pallas_call(
        prep_kernel,
        grid=(1,),
        in_specs=[in_vmem(1)[0], tail, tail, full(LEN, 1), full(1, LEN), full(LEN, 4), full(4, 256), full(1, 256), full(8, TILE)],
        out_specs=in_vmem(len(shapes)),
        out_shape=[near_core(shape, kind) for shape, kind in shapes],
        compiler_params=params(24),
        cost_estimate=QUICK,
        name="prepare",
    )(normed, inner_own, inner_peer, seg_col, seg_row, masks, taps, bias, heads)


def norm_kernel(hidden, cotangent, other, gain, whole, normed, scale, cot):
    first = jnp.full((256, 1536), lax.axis_index("tensor")) == 0
    mine, theirs = hidden[...].astype(F32), other[0:256].astype(F32)
    for part, values in enumerate((jnp.where(first, mine, theirs), jnp.where(first, theirs, mine))):
        rows = slice(part * 256, (part + 1) * 256)
        whole[rows, :] = values.astype(BF)
        inv = lax.rsqrt(jnp.sum(values * values, axis=1, keepdims=True) * (1.0 / 1536.0) + EPS)
        scale[rows, :] = jnp.broadcast_to(inv, (256, TILE))
        normed[rows, :] = (values * inv * gain[...]).astype(BF)
    mine, theirs = cotangent[...].astype(F32), other[256:512].astype(F32)
    cot[0:256, :] = jnp.where(first, mine, theirs).astype(BF)
    cot[256:512, :] = jnp.where(first, theirs, mine).astype(BF)


def norm_of(hidden, cotangent, other, gain):
    whole = near_core((LEN, 1536), BF)
    return pl.pallas_call(
        norm_kernel,
        in_specs=in_vmem(4),
        out_specs=in_vmem(4),
        out_shape=[whole, whole, jax.ShapeDtypeStruct((LEN, TILE), F32), whole],
        compiler_params=pltpu.CompilerParams(vmem_limit_bytes=24 * 1024 * 1024),
        cost_estimate=QUICK,
        name="input_norm",
    )(hidden, cotangent, other, gain)


def mix_kernel(half, normed, weight, taps, bias, masks, scores, cols, rows, pre, act, mixed):
    pre[...] = dot(normed[...], weight[0])
    conv_out = conv_of(pre[...], taps[...], bias[...], masks[...])
    act[...] = (conv_out * jax.nn.sigmoid(conv_out)).astype(BF)
    sums_all = pltpu.roll(cols[0], lax.rem(TILE - 24 * half - 8 * pl.program_id(0), TILE), 1)
    for pair in range(2):
        lanes = slice(pair * TILE, (pair + 1) * TILE)
        halves = lane_halves(act[:, lanes])
        for tile in range(4):
            here = slice(tile * TILE, (tile + 1) * TILE)
            weights, values = [], []
            for side in range(2):
                head = 2 * pair + side
                sums = sums_all[here, head : head + 1]
                if tile:
                    decay = jnp.exp2(sums - rows[1, head : head + 1, : tile * TILE])
                    weights.append((scores[here, : tile * TILE] * decay).astype(BF))
                    values.append(halves[side][: tile * TILE])
                decay = jnp.exp2(jnp.minimum(sums - rows[1, head : head + 1, here], rows[2, head : head + 1, here]))
                weights.append((scores[here, here] * decay).astype(BF))
                values.append(halves[side][here])
            mixed[here, lanes] = dot(jnp.concatenate(weights, 1), jnp.concatenate(values, 0))


def third_of(count, half):
    return pl.BlockSpec((count, BLOCK), lambda i: (0, 3 * half + i))


def rows_of(half):
    return pl.BlockSpec((3, 8, LEN), lambda i: (0, 3 * half + i, 0))


def mix_forward(half, normed, weight, taps, bias, masks, scores, cols, rows):
    return pl.pallas_call(
        lambda *refs: mix_kernel(half, *refs),
        grid=(3,),
        in_specs=[
            in_vmem(1)[0],
            pl.BlockSpec((1, 1536, BLOCK), lambda i: (i, 0, 0)),
            third_of(4, half),
            third_of(1, half),
            full(LEN, 4),
            in_vmem(1)[0],
            in_vmem(1)[0],
            rows_of(half),
        ],
        out_specs=[block(LEN)] * 3,
        out_shape=[
            jax.ShapeDtypeStruct((LEN, 768), F32),
            near_core((LEN, 768), BF),
            near_core((LEN, 768), F32),
        ],
        compiler_params=params(20),
        cost_estimate=QUICK,
        name="mix_forward",
    )(normed, weight, taps, bias, masks, scores, cols, rows)


def gate_kernel(last, normed, cot, gate_w, out_w, act, mixed, skip, gain, *refs):
    step = pl.program_id(0)
    before = refs[0] if last else None
    gate_pre, grad_gn, stats, squares, dots = refs[last:]

    @pl.when(step == 0)
    def _():
        squares[...] = before[0] if last else jnp.zeros_like(squares)
        dots[...] = before[1] if last else jnp.zeros_like(dots)

    pre = dot(normed[...], gate_w[0])
    upper = dot(cot[...], out_w[0])
    gate_pre[...] = pre
    grad_gn[...] = upper
    mixer_y = mixed[...] + skip[...] * act[...].astype(F32)
    gated = mixer_y * (pre * jax.nn.sigmoid(pre))
    square = gated * gated
    product = upper * gain[...] * gated
    squares[...] += square[:, :TILE] + square[:, TILE : 2 * TILE] + square[:, 2 * TILE :]
    dots[...] += product[:, :TILE] + product[:, TILE : 2 * TILE] + product[:, 2 * TILE :]

    @pl.when(step == 1)
    def _():
        if last:
            stats[0:1, :] = jnp.sum(squares[...].T, axis=0, keepdims=True)
            stats[1:2, :] = jnp.sum(dots[...].T, axis=0, keepdims=True)
            stats[2:8, :] = jnp.zeros((6, LEN), F32)
        else:
            stats[0] = squares[...]
            stats[1] = dots[...]


def half_of(count, half):
    return pl.BlockSpec((count, WIDE), lambda i: (0, 2 * half + i))


def gate_forward(half, normed, cot, rest, act, mixed, skip, gain, before=()):
    weight = lambda part: pl.BlockSpec((1, 1536, WIDE), lambda i: (2 * part + i, 0, 0))
    stats = (8, LEN) if half else (2, LEN, TILE)
    return pl.pallas_call(
        lambda *refs: gate_kernel(half, *refs),
        grid=(2,),
        in_specs=[
            *in_vmem(2),
            weight(0),
            weight(1),
            wide(LEN),
            wide(LEN),
            half_of(1, half),
            half_of(1, half),
        ]
        + [full(2, LEN, TILE)] * half,
        out_specs=[wide(LEN), wide(LEN), out_full(*stats)],
        out_shape=[
            near_core((LEN, 768), F32),
            near_core((LEN, 768), F32),
            jax.ShapeDtypeStruct(stats, F32),
        ],
        scratch_shapes=[pltpu.VMEM((LEN, TILE), F32)] * 2,
        compiler_params=params(24),
        cost_estimate=QUICK,
        name="gate_forward",
    )(normed, cot, rest, rest, act, mixed, skip, gain, *before)


def slope_kernel(last, stats, others, gate_pre, grad_gn, act, mixed, skip, gain, normed, cot, gate_w, out_w, *refs):
    step = pl.program_id(0)
    if last:
        branch_0, gate_0, grad_y, gain_grad, branch, gate_sum, gate_low, gnormed, scale, dots, branch_sum = refs
    else:
        grad_y, gain_grad, branch, gate_sum, peer_gate, peer_out, scale, dots, gate_low, gnormed, whole = refs

    @pl.when(step == 0)
    def _():
        inv = lax.rsqrt((stats[0:1, :] + others[0:1, :]) * (1.0 / 3072.0) + EPS)
        both = (stats[1:2, :] + others[1:2, :]) * (1.0 / 3072.0)
        scale[...] = jnp.broadcast_to(inv, (TILE, LEN)).T
        dots[...] = jnp.broadcast_to(inv * inv * inv * both, (TILE, LEN)).T

    for part in range(3):
        lanes = slice(part * TILE, (part + 1) * TILE)
        q = scale[...]
        pre = gate_pre[:, lanes]
        sig = jax.nn.sigmoid(pre)
        gate_act = pre * sig
        mixer_y = mixed[:, lanes] + skip[:, lanes] * act[:, lanes].astype(F32)
        gated = mixer_y * gate_act
        scaled = gated * q
        gnormed[:, lanes] = (scaled * gain[:, lanes]).astype(BF)
        upper = grad_gn[:, lanes]
        gain_grad[:, lanes] = jnp.sum(upper * scaled, axis=0, keepdims=True)
        grad_gated = q * gain[:, lanes] * upper - gated * dots[...]
        grad_y[:, lanes] = grad_gated * gate_act
        gate_low[:, lanes] = (grad_gated * mixer_y * (sig * (1.0 + pre * (1.0 - sig)))).astype(BF)

    for left, weight, before, total in (
        (gnormed, out_w, branch_0 if last else None, branch_sum if last else branch),
        (gate_low, gate_w, gate_0 if last else None, gate_sum),
    ):
        part = dot_cols(left[...], weight[0])

        @pl.when(step == 0)
        def _(part=part, before=before, total=total):
            total[...] = part if before is None else before[...] + part

        @pl.when(step == 1)
        def _(part=part, total=total):
            total[...] += part

    if last:

        @pl.when(step == 1)
        def _():
            branch[...] = branch_sum[...].astype(BF)

    else:
        x, y = here()
        for k in range(4):
            rows = pl.ds(pl.multiple_of(ahead(x, k) * 384, 128), 384)
            peer_gate[k] = dot_rows(normed[:, rows], gate_low[...]).astype(BF)
        for i in range(4):
            whole[...] = dot_rows(cot[:, i * 384 : (i + 1) * 384], gnormed[...])
            for k in range(4):
                for z in range(2):
                    rows = pl.ds(pl.multiple_of((z * 4 + ahead(y, k)) * 48, 16), 48)
                    peer_out[k, i, z] = whole[rows, :].astype(BF)


def gate_backward(half, stats, others, gate_pre, grad_gn, act, mixed, skip, gain, normed, cot, rest, before=()):
    weight = lambda part: pl.BlockSpec((1, 1536, WIDE), lambda i: (2 * part + i, 0, 0))
    last = not half
    wide_sum = near_core((LEN, 1536), F32)
    outs = [near_core((LEN, 768), F32), jax.ShapeDtypeStruct((1, 768), F32)]
    low = near_core((LEN, 768), BF)
    if last:
        outs += [jax.ShapeDtypeStruct((LEN, 1536), BF), wide_sum, low, low]
        out_specs = [wide(LEN), wide(1), *in_vmem(2), wide(LEN), wide(LEN)]
        scratch = [pltpu.VMEM((LEN, 1536), F32)]
    else:
        outs += [wide_sum, wide_sum, jax.ShapeDtypeStruct((4, 384, 768), BF), jax.ShapeDtypeStruct((4, 4, 2, 48, 768), BF)]
        out_specs = [wide(LEN), wide(1), *in_vmem(2)]
        out_specs += [
            pl.BlockSpec((4, 384, WIDE), lambda i: (0, 0, i)),
            pl.BlockSpec((4, 4, 2, 48, WIDE), lambda i: (0, 0, 0, 0, i)),
        ]
        scratch = [pltpu.VMEM((LEN, WIDE), BF)] * 2 + [pltpu.VMEM((384, WIDE), F32)]
    return pl.pallas_call(
        lambda *refs: slope_kernel(last, *refs),
        grid=(2,),
        in_specs=[
            full(8, LEN),
            full(8, LEN),
            wide(LEN),
            wide(LEN),
            wide(LEN),
            wide(LEN),
            half_of(1, half),
            half_of(1, half),
            *in_vmem(2),
            weight(0),
            weight(1),
            *in_vmem(len(before)),
        ],
        out_specs=out_specs,
        out_shape=outs,
        scratch_shapes=[pltpu.VMEM((LEN, TILE), F32)] * 2 + scratch,
        compiler_params=params(30),
        cost_estimate=QUICK,
        name="gate_backward",
    )(stats, others, gate_pre, grad_gn, act, mixed, skip, gain, normed, cot, rest, rest, *before)


def back_kernel(half, grad_y, act, mixed, pre, scores, taps, bias, masks, cols, rows, skip, *refs):
    step = pl.program_id(0)
    if half:
        inner_low, sums, flows, grad_scores, grad_act = refs[-5:]
    else:
        flows_0, scores_0 = refs[:2]
        inner_low, sums, flows, grad_scores, scores_low, grad_act = refs[-6:]

    @pl.when(step == 0)
    def _():
        grad_scores[...] = jnp.zeros_like(grad_scores) if half else scores_0[...]
        flows[...] = jnp.zeros_like(flows) if half else flows_0[...]

    turn = lax.rem(TILE - 24 * half - 8 * step, TILE)
    back_all, most_all = pltpu.roll(cols[1], turn, 1), pltpu.roll(cols[2], turn, 1)

    pairs = []
    for pair in range(2):
        lanes = slice(pair * TILE, (pair + 1) * TILE)
        low = grad_y[:, lanes].astype(BF)
        pairs.append((lane_halves(act[:, lanes]), low, lane_halves(low)))
    for tile in range(4):
        here = slice(tile * TILE, (tile + 1) * TILE)
        after = slice((tile + 1) * TILE, LEN)
        add_diag, add_rest = 0.0, 0.0
        for pair in range(2):
            act_halves, low, low_halves = pairs[pair]
            weights, values = [], []
            stacked = jnp.concatenate([act_halves[0][here], act_halves[1][here]], 0)
            grad_w = dot_cols(stacked, low[tile * TILE :])
            for side in range(2):
                head = 2 * pair + side
                back = back_all[here, head : head + 1]
                most = most_all[here, head : head + 1]
                own = slice(side * TILE, (side + 1) * TILE)
                decay = jnp.exp2(jnp.minimum(rows[0, head : head + 1, here] - back, most))
                add_diag = add_diag + grad_w[own, :TILE] * decay
                weights.append((scores[here, here] * decay).astype(BF))
                values.append(low_halves[side][here])
                if tile < 3:
                    decay = jnp.exp2(rows[0, head : head + 1, after] - back)
                    add_rest = add_rest + grad_w[own, TILE:] * decay
                    weights.append((scores[here, after] * decay).astype(BF))
                    values.append(low_halves[side][after])
            lanes = slice(pair * TILE, (pair + 1) * TILE)
            grad_act[here, lanes] = dot(jnp.concatenate(weights, 1), jnp.concatenate(values, 0))
        grad_scores[here, here] += add_diag
        if tile < 3:
            grad_scores[here, after] += add_rest

    if not half:

        @pl.when(step == 2)
        def _():
            scores_low[...] = grad_scores[...].astype(BF)

    lane = lax.broadcasted_iota(jnp.int32, (1, TILE), 1)
    row_flows, col_flows = 0.0, 0.0

    low_lane = lax.broadcasted_iota(jnp.int32, (1, TILE), 1) < 64
    for pair in range(2):
        lanes = slice(pair * TILE, (pair + 1) * TILE)
        values = act[:, lanes].astype(F32)
        grad = grad_y[:, lanes]
        row_flow = grad.astype(BF).astype(F32) * mixed[:, lanes]
        col_flow = values * grad_act[:, lanes]
        for side, mask in ((0, low_lane), (1, ~low_lane)):
            head = 2 * pair + side
            here = lane == 24 * half + 8 * step + head
            row_flows += jnp.where(here, jnp.sum(jnp.where(mask, row_flow, 0.0), axis=1, keepdims=True), 0.0)
            col_flows += jnp.where(here, jnp.sum(jnp.where(mask, col_flow, 0.0), axis=1, keepdims=True), 0.0)
        taps_l, masks_v = taps[:, lanes], masks[...]
        pre_l = pre[:, lanes]
        conv_out = conv_of(pre_l, taps_l, bias[:, lanes], masks_v)
        grad_conv = (grad_act[:, lanes] + skip[:, lanes] * grad) * silu_slope(conv_out)
        grad_pre = taps_l[3:4] * grad_conv
        sums[3:4, lanes] = jnp.sum(grad_conv * pre_l, axis=0, keepdims=True)
        for offset in (1, 2, 3):
            masked = grad_conv * masks_v[:, offset : offset + 1]
            tap = 3 - offset
            sums[tap : tap + 1, lanes] = jnp.sum(masked * down(pre_l, offset), axis=0, keepdims=True)
            grad_pre = grad_pre + taps_l[tap : tap + 1] * up(masked, offset)
        sums[4:5, lanes] = jnp.sum(grad_conv, axis=0, keepdims=True)
        sums[5:6, lanes] = jnp.sum(grad * values, axis=0, keepdims=True)
        sums[6:8, lanes] = jnp.zeros((2, TILE), F32)
        inner_low[:, lanes] = grad_pre.astype(BF)
    flows[0] += row_flows
    flows[1] += col_flows


def mix_backward(half, grad_y, act, mixed, pre, scores_t, taps, bias, masks, cols, rows, skip, before=(), first=()):
    low = [] if half else [jax.ShapeDtypeStruct((LEN, LEN), BF)]
    return pl.pallas_call(
        lambda *refs: back_kernel(half, *refs),
        grid=(3,),
        in_specs=[
            block(LEN),
            block(LEN),
            block(LEN),
            block(LEN),
            in_vmem(1)[0],
            third_of(4, half),
            third_of(1, half),
            full(LEN, 4),
            in_vmem(1)[0],
            rows_of(half),
            third_of(1, half),
            *in_vmem(len(before)),
            *anywhere(len(first)),
        ],
        out_specs=[block(LEN), block(8), *in_vmem(2 + len(low))],
        out_shape=[
            near_core((LEN, 768), BF),
            jax.ShapeDtypeStruct((8, 768), F32),
            near_core((2, LEN, TILE), F32),
            near_core((LEN, LEN), F32),
        ]
        + low,
        scratch_shapes=[pltpu.VMEM((LEN, BLOCK), F32)],
        compiler_params=params(24),
        cost_estimate=QUICK,
        name="mix_backward",
    )(grad_y, act, mixed, pre, scores_t, taps, bias, masks, cols, rows, skip, *before, *first)


def tail_kernel(mine, other, act, pre, seg_col, seg_row, masks, taps, bias, heads, steps, flows, *refs):
    tails, shares, bc_sums, head_sums = refs[-4:]
    seen = visible_of(seg_col, seg_row, True)
    low = jnp.where(seen, mine[...] + other[...].astype(F32), 0.0).astype(BF)
    b_proj, c_proj = act[:, :TILE], act[:, TILE:]
    core0 = jnp.full((LEN, TILE), lax.rem(lax.axis_index("dp"), 2)) == 0
    first = jnp.full((LEN, TILE), lax.axis_index("tensor")) == 0
    bc_low = []
    for part, grad in ((0, dot(low, c_proj)), (1, dot_rows(low, b_proj))):
        lanes = slice(part * TILE, (part + 1) * TILE)
        taps_l, pre_l, masks_v = taps[:, lanes], pre[:, lanes], masks[...]
        grad_conv = grad * silu_slope(conv_of(pre_l, taps_l, bias[:, lanes], masks_v))
        grad_pre = taps_l[3:4] * grad_conv
        bc_sums[3:4, lanes] = jnp.sum(grad_conv * pre_l, axis=0, keepdims=True)
        for offset in (1, 2, 3):
            masked = grad_conv * masks_v[:, offset : offset + 1]
            tap = 3 - offset
            bc_sums[tap : tap + 1, lanes] = jnp.sum(masked * down(pre_l, offset), axis=0, keepdims=True)
            grad_pre = grad_pre + taps_l[tap : tap + 1] * up(masked, offset)
        bc_sums[4:5, lanes] = jnp.sum(grad_conv, axis=0, keepdims=True)
        bc_sums[5:8, lanes] = jnp.zeros((3, TILE), F32)
        bc_low.append(grad_pre)
    step_pre, step_size, rate = steps[0], steps[1], heads[1:2, :]
    change = flows[0] - flows[1]
    before = running(change)
    grad_rate = before[LEN - 1 : LEN, :] - before + change
    sig = jax.nn.sigmoid(step_pre)
    tiny = step_size < 1e-30
    ratio = jnp.where(tiny, 1.0, sig / jnp.where(tiny, 1.0, step_size))
    grad_pre = flows[1] * ratio + grad_rate * rate * sig
    head_sums[0:1, :] = jnp.sum(grad_pre, axis=0, keepdims=True)
    head_sums[1:2, :] = jnp.sum(grad_rate * step_size, axis=0, keepdims=True) * rate
    head_sums[2:8, :] = jnp.zeros((6, TILE), F32)
    own_lane = lax.broadcasted_iota(jnp.int32, (LEN, TILE), 1) < 24
    for part, bc, grad in (
        (0, jnp.where(core0, bc_low[0], bc_low[1]), grad_pre),
        (1, jnp.where(core0, bc_low[1], bc_low[0]), pltpu.roll(grad_pre, TILE - 24, 1)),
    ):
        step_low = jnp.where(own_lane, grad, 0.0).astype(BF)
        tails[part, :, :TILE] = bc.astype(BF)
        tails[part, :, TILE:] = step_low
        shares[part, :, :TILE] = jnp.where(first, bc, 0.0).astype(BF)
        shares[part, :, TILE:] = step_low


def tail_backward(mine, other, act, pre, seg_col, seg_row, masks, taps, bias, heads, steps, flows, *first):
    shapes = [((2, LEN, 256), BF), ((2, LEN, 256), BF), ((8, 256), F32), ((8, TILE), F32)]
    return pl.pallas_call(
        tail_kernel,
        in_specs=in_vmem(12) + anywhere(len(first)),
        out_specs=in_vmem(len(shapes)),
        out_shape=[jax.ShapeDtypeStruct(shape, kind) for shape, kind in shapes],
        compiler_params=pltpu.CompilerParams(vmem_limit_bytes=20 * 1024 * 1024),
        cost_estimate=QUICK,
        name="tail_backward",
    )(mine, other, act, pre, seg_col, seg_row, masks, taps, bias, heads, steps, flows, *first)


def normed_kernel(before, low_own, low_peer, shares, inner_own, inner_peer, resid, scale, *refs):
    low, gain, total = refs[-3:]
    step = pl.program_id(0)

    @pl.when(step == 0)
    def _():
        total[...] = before[...]

    for test, left, weight in (
        (step < 3, low_peer, inner_peer),
        ((step >= 3) & (step < 6), low_own, inner_own),
        (step == 6, shares, inner_own),
        (step == 7, shares, inner_peer),
    ):

        @pl.when(test)
        def _(left=left, weight=weight):
            values = left[0] if left is shares else left[...]
            total[...] += dot_cols(values, weight[0])

    @pl.when(step == 7)
    def _():
        for i in range(3):
            lanes = slice(i * LEN, (i + 1) * LEN)
            values = total[:, lanes]
            low[:, lanes] = values.astype(BF)
            gain[:, lanes] = jnp.sum(values * resid[:, lanes].astype(F32) * scale[:, :1], axis=0, keepdims=True)


def normed_backward(before, low_own, low_peer, shares, inner_own, inner_peer, resid, scale, *first):
    return pl.pallas_call(
        normed_kernel,
        grid=(8,),
        in_specs=[
            in_vmem(1)[0],
            pl.BlockSpec((LEN, BLOCK), lambda i: (0, jnp.clip(i - 3, 0, 2))),
            pl.BlockSpec((LEN, BLOCK), lambda i: (0, jnp.minimum(i, 2))),
            pl.BlockSpec((1, LEN, BLOCK), lambda i: (jnp.clip(i - 6, 0, 1), 0, 0)),
            pl.BlockSpec((1, 1536, BLOCK), lambda i: (jnp.clip(i - 3, 0, 3), 0, 0)),
            pl.BlockSpec((1, 1536, BLOCK), lambda i: (jnp.where(i < 3, i, 3), 0, 0)),
            in_vmem(1)[0],
            full(LEN, TILE),
        ]
        + anywhere(len(first)),
        out_specs=in_vmem(2),
        out_shape=[jax.ShapeDtypeStruct((LEN, 1536), BF), jax.ShapeDtypeStruct((1, 1536), F32)],
        scratch_shapes=[pltpu.VMEM((LEN, 1536), F32)],
        compiler_params=params(24),
        cost_estimate=QUICK,
        name="normed_backward",
    )(before, low_own, low_peer, shares, inner_own, inner_peer, resid, scale, *first)


def small_kernel(sums_own, sums_peer, gain_own, gain_peer, norm_grad, bc_sums, head_sums, whole):
    core = lax.rem(lax.axis_index("dp"), 2)
    whole[...] = jnp.zeros_like(whole)
    for row, own, peer in (
        (0, sums_own[0:5], sums_peer[0:5]),
        (5, gain_own[...], gain_peer[...]),
        (7, sums_own[5:6], sums_peer[5:6]),
    ):
        flag = jnp.full(own.shape, core) == 0
        whole[row : row + own.shape[0], :768] = jnp.where(flag, own, peer)
        whole[row : row + own.shape[0], 768:] = jnp.where(flag, peer, own)
    whole[6:7, :] = norm_grad[...]
    heads = head_sums[...]
    lane = lax.broadcasted_iota(jnp.int32, heads.shape, 1)
    turned = jnp.where(lane < 24, pltpu.roll(heads, TILE - 24, 1), pltpu.roll(heads, 24, 1))
    whole[8:10, :TILE] = jnp.where(jnp.full(heads.shape, core) == 0, heads, turned)[0:2]
    whole[10:15, :256] = bc_sums[0:5, :]


def small_of(*parts):
    return pl.pallas_call(
        small_kernel,
        in_specs=in_vmem(7),
        out_specs=in_vmem(1)[0],
        out_shape=jax.ShapeDtypeStruct((16, 1536), F32),
        compiler_params=pltpu.CompilerParams(vmem_limit_bytes=16 * 1024 * 1024),
        cost_estimate=QUICK,
        name="small_pack",
    )(*parts)


def precise(left, right):
    return jnp.dot(left, right, preferred_element_type=F32, precision=lax.Precision.HIGHEST)


def outputs_kernel(mine, other, conv_grad, bias_grad, gain_grad, norm_grad, heads):
    def halves(rows, width):
        flag = jnp.full(mine[rows, :width].shape, lax.axis_index("tensor")) == 0
        a, b = mine[rows, :width], other[rows, :width]
        return jnp.where(flag, a, b), jnp.where(flag, b, a)

    for rows, target in ((slice(0, 4), conv_grad), (slice(4, 5), bias_grad), (slice(5, 6), gain_grad)):
        low, high = halves(rows, 1536)
        target[:, :1536] = low
        target[:, 1536:3072] = high
    conv_grad[:, 3072:] = mine[10:14, :256]
    bias_grad[:, 3072:] = mine[14:15, :256]
    norm_grad[...] = mine[6:7, :] + other[6:7, :]
    lane = lax.broadcasted_iota(jnp.int32, (TILE, 24), 0)
    head = lax.broadcasted_iota(jnp.int32, (TILE, 24), 1)
    pick = (lane == (head // 4) * 8 + head % 4).astype(F32)
    unit = lax.broadcasted_iota(jnp.int32, (1536, 24), 0)
    fold = (unit // 64 == lax.broadcasted_iota(jnp.int32, (1536, 24), 1)).astype(F32)
    for part, values in enumerate(halves(slice(8, 16), TILE)):
        heads[0:8, part * 24 : part * 24 + 24] = precise(values, pick)
    for part, values in enumerate(halves(slice(0, 8), 1536)):
        heads[8:16, part * 24 : part * 24 + 24] = precise(values, fold)


def outputs_of(mine, other):
    shapes = [(4, 3328), (1, 3328), (1, 3072), (1, 1536), (16, 48)]
    return pl.pallas_call(
        outputs_kernel,
        in_specs=in_vmem(2),
        out_specs=in_vmem(5),
        out_shape=[jax.ShapeDtypeStruct(shape, F32) for shape in shapes],
        compiler_params=pltpu.CompilerParams(vmem_limit_bytes=16 * 1024 * 1024),
        cost_estimate=QUICK,
        name="small_unpack",
    )(mine, other)


def on_device(
    hidden,
    segments,
    norm_gain,
    in_weight,
    bc_weight,
    step_weight,
    conv_weight,
    conv_bias,
    step_bias,
    decay_log,
    skip_gain,
    gate_gain,
    out_weight,
    cotangent,
):
    t = lax.axis_index("tensor")
    d = lax.axis_index("dp")
    spot = (d // 16, (d // 8) % 2, (d // 2) % 4, d % 2)
    c = spot[3]

    def own_first(values, size):
        base = 2 * t * size
        return jnp.concatenate(
            [
                lax.dynamic_slice_in_dim(values, base + c * size, size, values.ndim - 1),
                lax.dynamic_slice_in_dim(values, base + (1 - c) * size, size, values.ndim - 1),
            ],
            values.ndim - 1,
        )

    def in_lanes(values):
        return jnp.pad(jnp.pad(values.reshape(6, 4), ((0, 0), (0, 4))).reshape(48), (0, 80))

    planes = pair_planes(pair_rows(*pack(in_weight, bc_weight, step_weight, out_weight), c), spot[1])
    tokens_other = swap_tensor(after(jnp.concatenate([hidden, cotangent], 0), planes))

    taps = own_first(conv_weight[:, :3072], 768)
    bias = own_first(conv_bias[None, :3072], 768)
    gain = own_first(gate_gain[None, :], 768)
    skip = jnp.repeat(own_first(skip_gain, 12), 64)[None, :]
    heads = jnp.stack(
        [in_lanes(own_first(step_bias, 12)), in_lanes(-jnp.exp(own_first(decay_log, 12)))]
        + [jnp.zeros((TILE,), F32)] * 6
    )
    bc_taps, bc_bias = conv_weight[:, 3072:], conv_bias[None, 3072:]
    seg = segments[0]
    seg_col, seg_row = segments.T, segments
    masks = jnp.stack(
        [(jnp.pad(seg, (o, 0), constant_values=-1)[:LEN] == seg).astype(F32) for o in range(4)], 1
    )

    a_near, b_near = ring(planes[..., :1280], YS), ring(planes[..., 1280:], XS)
    settings = (taps, bias, gain, skip, heads, bc_taps, bc_bias, seg_col, masks)
    a_first, b_first = place_near(a_near, b_near, 0, 512, settings)
    hidden_all, normed, norm_scale, cot_all = norm_of(hidden, cotangent, tokens_other, norm_gain[None])
    a_far, b_far = sides(a_first, XS), sides(b_first, YS)
    a_far, b_far = a_far + opposite(a_far, XS, 0), b_far + opposite(b_far, YS, 0)
    inner_own = place_far(a_far, b_far, 256, (normed,))
    inner_peer = send(inner_own, CORE)
    a_rest, b_rest = place_near(a_near, b_near, 512, 768, (inner_own,))
    a_rest, b_rest = sides(a_rest, XS), sides(b_rest, YS)

    scores, scores_t, bc_act, bc_pre, cols, rows, steps = prepare(
        normed, inner_own, inner_peer, seg_col, seg_row, masks, bc_taps, bc_bias, heads
    )
    mixer = (taps, bias, masks, scores, cols, rows)
    pre_own, act_own, mixed_own = mix_forward(0, normed, inner_own, *mixer)
    a_rest, b_rest = a_rest + opposite(a_rest, XS, 0, act_own), b_rest + opposite(b_rest, YS, 0, act_own)
    pre_peer, act_peer, mixed_peer = mix_forward(1, normed, inner_peer, *mixer)
    rest_own = place_far(a_rest, b_rest, WIDE, (act_peer,))
    rest_peer = send(rest_own, CORE)
    gate_own, gn_own, sums_own = gate_forward(0, normed, cot_all, rest_own, act_own, mixed_own, skip, gain)
    gate_peer, gn_peer, stats = gate_forward(1, normed, cot_all, rest_peer, act_peer, mixed_peer, skip, gain, (sums_own,))
    others = swap_tensor(stats)

    def own_tokens(values):
        got = swap_tensor(lax.dynamic_slice_in_dim(values, (1 - t) * 256, 256, 0))
        return lax.dynamic_slice_in_dim(values, t * 256, 256, 0).astype(F32) + got.astype(F32)

    grad_y_peer, gain_peer, branch_half, gate_half, gate_got, out_got = gate_backward(
        1, stats, others, gate_peer, gn_peer, act_peer, mixed_peer, skip, gain, normed, cot_all, rest_peer
    )
    gate_got, out_got = send(gate_got, CORE), send(out_got, CORE)
    grad_y_own, gain_own, branch, gate_grads, gate_low, gnormed = gate_backward(
        0, stats, others, gate_own, gn_own, act_own, mixed_own, skip, gain, normed, cot_all, rest_own, (branch_half, gate_half)
    )
    mixed = (hidden.astype(F32) + own_tokens(branch)).astype(BF)
    gate_pieces = weight_pieces(True, normed, (gate_low,), ((0, 768),), (gate_got,))
    out_pieces = weight_pieces(False, cot_all, (gnormed,), ((0, 768),), (out_got,))

    inner_peer_low, sums_peer, flows, grad_scores = mix_backward(
        1,
        grad_y_peer,
        act_peer,
        mixed_peer,
        pre_peer,
        scores_t,
        taps,
        bias,
        masks,
        cols,
        rows,
        skip,
        (),
        (gate_pieces[3], out_pieces[3]),
    )
    a_part = weight_pieces(True, normed, (inner_peer_low,), ((0, 512),))
    a_got = send(a_part, CORE)
    gate_passed, out_passed = pass_on(True, gate_pieces, a_part), pass_on(False, out_pieces, a_part)
    inner_own_low, sums_own, flows, grad_scores, scores_low = mix_backward(
        0,
        grad_y_own,
        act_own,
        mixed_own,
        pre_own,
        scores_t,
        taps,
        bias,
        masks,
        cols,
        rows,
        skip,
        (flows, grad_scores),
        (gate_passed[0], out_passed[0]),
    )
    scores_other = swap_tensor(scores_low)
    a_pieces = weight_pieces(True, normed, (inner_own_low,), ((0, 512),), (a_got,))
    gate_near = scatter_near(True, gate_pieces, gate_passed, a_pieces[3])
    out_near = scatter_near(False, out_pieces, out_passed, a_pieces[3])
    tails, shares, bc_sums, head_sums = tail_backward(
        grad_scores,
        scores_other,
        bc_act,
        bc_pre,
        seg_col,
        seg_row,
        masks,
        bc_taps,
        bc_bias,
        heads,
        steps,
        flows,
        gate_near[1],
        out_near[1],
    )
    b_got = send(weight_pieces(False, normed, (inner_peer_low, tails), ((512, 768), (1, 256))), CORE)
    a_passed = pass_on(True, a_pieces)
    b_pieces = weight_pieces(False, normed, (inner_own_low, tails), ((512, 768), (0, 256)), (b_got, ), (a_passed[0],))
    grad_low, norm_grad = normed_backward(
        gate_grads, inner_own_low, inner_peer_low, shares, inner_own, inner_peer, hidden_all, norm_scale, b_pieces[3]
    )
    b_passed = pass_on(False, b_pieces, norm_grad)
    a_near_sum = scatter_near(True, a_pieces, a_passed, b_passed[0])
    small = small_of(sums_own, sums_peer, gain_own, gain_peer, norm_grad, bc_sums, head_sums)
    small, small_early = reduce_small(small)
    b_near_sum = scatter_near(False, b_pieces, b_passed, small_early)
    parts = [
        scatter_far(True, a_near_sum),
        scatter_far(False, b_near_sum),
        scatter_far(True, gate_near),
        scatter_far(False, out_near),
    ]
    grad_mine = own_tokens(grad_low)
    mine = hidden.astype(F32)
    scale_mine = lax.dynamic_slice_in_dim(norm_scale, t * 256, 256, 0)[:, :1]
    pre_stat = jnp.sum(grad_mine * norm_gain * mine, axis=-1, keepdims=True)
    grad_hidden = (
        cotangent.astype(F32)
        + scale_mine * norm_gain * grad_mine
        - mine * scale_mine**3 * pre_stat / 1536
    )
    both_rows = own_rows(plane_sum(jnp.concatenate(parts, 2), spot[1]), c)

    def columns(rows_of, start, size):
        return jnp.concatenate([part[:, start : start + size] for part in rows_of], 1)

    grad_in = jnp.stack([columns(both_rows, 1024, 768), columns(both_rows, 0, 768)])
    grad_bc = columns(both_rows, 768, 128)
    grad_step = jnp.concatenate(
        [part[:, 896:920].reshape(24, 3, 8)[:, :, :4].reshape(24, 12) for part in both_rows], 1
    )
    grad_out = columns(both_rows, 1792, 768).T

    conv_grad, bias_grad, gate_gain_grad, norm_gain_grad, head_grads = outputs_of(small, swap_tensor(small))
    return (
        mixed,
        grad_hidden,
        norm_gain_grad[0],
        grad_in,
        grad_bc,
        grad_step,
        conv_grad,
        bias_grad[0],
        head_grads[0],
        head_grads[1],
        head_grads[15],
        gate_gain_grad[0],
        grad_out,
    )


def solution(mesh):
    return jax.shard_map(
        on_device,
        mesh=mesh,
        in_specs=(
            P(("dp", "tensor"), None),
            P("dp", None),
            P(),
            P(None, "dp", "tensor"),
            P("dp", None),
            P("dp", "tensor"),
            P(),
            P(),
            P(),
            P(),
            P(),
            P(),
            P("tensor", "dp"),
            P(("dp", "tensor"), None),
        ),
        out_specs=(
            P(("dp", "tensor"), None),
            P(("dp", "tensor"), None),
            P(),
            P(None, "dp", "tensor"),
            P("dp", None),
            P("dp", "tensor"),
            P(),
            P(),
            P(),
            P(),
            P(),
            P(),
            P("tensor", "dp"),
        ),
        check_vma=False,
    )
```

```python
import jax
import jax.numpy as jnp
from jax import lax
from jax.experimental import pallas as pl
from jax.experimental.pallas import tpu as pltpu
from jax.sharding import PartitionSpec as P

EPS = 1e-05
LOG2E = 1.4426950408889634
BF = jnp.bfloat16
F32 = jnp.float32
LEN = 512
TILE = 128
BLOCK = 256


def cost(us):
    return pl.CostEstimate(flops=int(us * 1.0 * 1e9), bytes_accessed=int(us * 1.0 * 2.5e6), transcendentals=0)


SWAP = [(0, 1), (1, 0)]


def dp_index(x, z, y, c):
    return ((x * 2 + z) * 4 + y) * 2 + c


def dp_pairs(move):
    return [
        (dp_index(x, z, y, c), dp_index(*move(x, z, y, c)))
        for x in range(4)
        for z in range(2)
        for y in range(4)
        for c in range(2)
    ]


CORE = dp_pairs(lambda x, z, y, c: (x, z, y, 1 - c))
ZHI = dp_pairs(lambda x, z, y, c: (x, 1 - z, y, c))
XS = {k: dp_pairs(lambda x, z, y, c, k=k: ((x + k) % 4, z, y, c)) for k in (1, 2, 3)}
YS = {k: dp_pairs(lambda x, z, y, c, k=k: (x, z, (y + k) % 4, c)) for k in (1, 2, 3)}


def send(values, pairs):
    return lax.ppermute(values, "dp", pairs)


def swap_tensor(values):
    return lax.ppermute(values, "tensor", SWAP)


def near_core(shape, kind):
    return pltpu.VMEM(shape, kind)


def outside(shape, kind):
    return pltpu.HBM(shape, kind)


def far_off(values):
    return pltpu.with_memory_space_constraint(values, pltpu.HBM)


def anywhere(count):
    return [pl.BlockSpec(memory_space=pl.ANY)] * count


def in_vmem(count):
    return [pl.BlockSpec(memory_space=pltpu.VMEM)] * count


def after(values, *first):
    return pl.pallas_call(
        lambda *refs: None,
        in_specs=anywhere(1 + len(first)),
        out_specs=pl.BlockSpec(memory_space=pl.ANY),
        out_shape=jax.ShapeDtypeStruct(values.shape, values.dtype),
        input_output_aliases={0: 0},
        cost_estimate=cost(0.01),
        name="after",
    )(values, *first)


def sides(values, perms):
    return [values, send(values, perms[1]), send(values, perms[3])]


def opposite(pieces, perms, axis):
    half = pieces[0].shape[axis] // 2
    front = lax.slice_in_dim(pieces[1], 0, half, axis=axis)
    back = lax.slice_in_dim(pieces[2], half, 2 * half, axis=axis)
    return [send(front, perms[1]), send(back, perms[3])]


def halves_kernel(a_back, a_ahead, b_back, b_ahead, first, a_front, a_rear, b_front, b_rear, sems):
    a_half, b_half = a_front.shape[0], b_front.shape[0]
    copy_all(
        [
            (a_back.at[pl.ds(0, a_half)], a_front),
            (a_ahead.at[pl.ds(a_half, a_half)], a_rear),
            (b_back.at[pl.ds(0, b_half)], b_front),
            (b_ahead.at[pl.ds(b_half, b_half)], b_rear),
        ],
        sems,
    )


def opposites(a_pieces, b_pieces, first):
    shapes = [(v.shape[0] // 2, *v.shape[1:]) for v in (a_pieces[0], a_pieces[0], b_pieces[0], b_pieces[0])]
    parts = pl.pallas_call(
        halves_kernel,
        in_specs=in_vmem(4) + anywhere(1),
        out_specs=in_vmem(4),
        out_shape=[jax.ShapeDtypeStruct(shape, BF) for shape in shapes],
        scratch_shapes=[pltpu.SemaphoreType.DMA((4,))],
        compiler_params=pltpu.CompilerParams(vmem_limit_bytes=16 * 1024 * 1024),
        cost_estimate=cost(1),
        name="halves",
    )(*a_pieces[1:], *b_pieces[1:], first)
    return [send(parts[0], XS[1]), send(parts[1], XS[3])], [send(parts[2], YS[1]), send(parts[3], YS[3])]


def ring(values, perms):
    return [values] + [send(values, perms[k]) for k in (1, 3, 2)]


BACK = (0, 1, 3, 2)


def copy_all(copies, sems):
    started = [pltpu.make_async_copy(source, target, sems.at[i]) for i, (source, target) in enumerate(copies)]
    for copy in started:
        copy.start()
    for copy in started:
        copy.wait()


def place_near(a_pieces, b_pieces, start, width, first=()):
    def kernel(*refs):
        d = lax.axis_index("dp")
        x, y = d // 16, (d // 2) % 4
        a_whole, b_whole, sems = refs[8 + len(first) :]
        copies = []
        for i, back in enumerate(BACK):
            at_y, at_x = lax.rem(y + 4 - back, 4), lax.rem(x + 4 - back, 4)
            copies.append((refs[i].at[:, :, pl.ds(start, width)], a_whole.at[:, at_y]))
            copies.append((refs[4 + i].at[:, :, pl.ds(start, width)], b_whole.at[at_x]))
        copy_all(copies, sems)

    return pl.pallas_call(
        kernel,
        in_specs=in_vmem(8) + anywhere(len(first)),
        out_specs=in_vmem(2),
        out_shape=[jax.ShapeDtypeStruct(shape, BF) for shape in ((2, 4, 48, width), (4, 2, 48, width))],
        scratch_shapes=[pltpu.SemaphoreType.DMA((8,))],
        compiler_params=pltpu.CompilerParams(vmem_limit_bytes=16 * 1024 * 1024),
        cost_estimate=cost(1.5),
        name="place_near",
    )(*a_pieces, *b_pieces, *first)


def place_far(a_pieces, b_pieces, columns, first=()):
    count = a_pieces[0].shape[-1] // columns

    def kernel(*refs):
        d = lax.axis_index("dp")
        x, y = d // 16, (d // 2) % 4
        whole, sems = refs[10 + len(first) :]
        copies = []
        for i, back in enumerate((0, 1, 3, 2, 2)):
            at_y, at_x = lax.rem(y + 4 - back, 4), lax.rem(x + 4 - back, 4)
            for j in range(count):
                lanes = pl.ds(j * columns, columns)
                z = pl.ds(i - 3, 1) if i > 2 else pl.ds(0, 2)
                xs = pl.ds(2 * (i - 3), 2) if i > 2 else pl.ds(0, 4)
                copies.append((refs[i].at[:, :, :, lanes], whole.at[j, at_x, z]))
                copies.append((refs[5 + i].at[:, :, :, lanes], whole.at[count + j, xs, :, at_y]))
        copy_all(copies, sems)

    return pl.pallas_call(
        kernel,
        in_specs=in_vmem(10) + anywhere(len(first)),
        out_specs=pl.BlockSpec(memory_space=pltpu.VMEM),
        out_shape=jax.ShapeDtypeStruct((2 * count, 4, 2, 4, 48, columns), BF),
        scratch_shapes=[pltpu.SemaphoreType.DMA((10 * count,))],
        compiler_params=pltpu.CompilerParams(vmem_limit_bytes=24 * 1024 * 1024),
        cost_estimate=cost(2),
        name="place_far",
    )(*a_pieces, *b_pieces, *first).reshape(2 * count, 1536, columns)


def pack_kernel(in_weight, bc_weight, step_weight, out_weight, mine, other):
    c = lax.rem(lax.axis_index("dp"), 2)
    out_rows = out_weight[...].T
    steps = step_weight[...]
    for target, half in ((mine, c), (other, 1 - c)):
        at = pl.multiple_of(half * 768, 128)
        target[:, 0:512] = in_weight[1, :, pl.ds(at, 512)]
        target[:, 512:1280] = in_weight[0, :, pl.ds(at, 768)]
        target[:, 1280:1536] = in_weight[1, :, pl.ds(pl.multiple_of(at + 512, 128), 256)]
        target[:, 1536:1664] = bc_weight[:, pl.ds(pl.multiple_of(half * 128, 128), 128)]
        second = jnp.full((24, 12), half) == 1
        own = jnp.where(second, steps[:, 12:].astype(F32), steps[:, :12].astype(F32))
        gap = jnp.zeros((24, 4), F32)
        parts = [own[:, 0:4], gap, own[:, 4:8], gap, own[:, 8:12], jnp.zeros((24, 108), F32)]
        target[:, 1664:1792] = jnp.concatenate(parts, 1).astype(BF)
        wanted = jnp.full((24, 768), half) == 1
        pieces = (out_rows[:, 768:].astype(F32), out_rows[:, :768].astype(F32))
        target[:, 1792:2560] = jnp.where(wanted, *pieces).astype(BF)


def pack(in_weight, bc_weight, step_weight, out_weight):
    return pl.pallas_call(
        pack_kernel,
        in_specs=in_vmem(4),
        out_specs=in_vmem(2),
        out_shape=[jax.ShapeDtypeStruct((24, 2560), BF)] * 2,
        compiler_params=pltpu.CompilerParams(vmem_limit_bytes=16 * 1024 * 1024),
        cost_estimate=cost(1.5),
        name="pack",
    )(in_weight, bc_weight, step_weight, out_weight)


def pair_rows(mine, other, c):
    got = send(other, CORE)
    return jnp.concatenate([jnp.where(c == 0, mine, got), jnp.where(c == 0, got, mine)], 0)


def pair_planes(rows, z):
    other = send(rows, ZHI)
    return jnp.stack([jnp.where(z == 0, rows, other), jnp.where(z == 0, other, rows)], 0)


def here():
    d = lax.axis_index("dp")
    return d // 16, (d // 2) % 4


def ahead(at, k):
    return lax.rem(at + k, 4)


def pieces_kernel(by_x, own, widths, left, *refs):
    rights, refs = refs[: len(widths)], refs[len(widths) :]
    got = refs[0] if own else None
    outs = refs[1:6] if own else refs[:1]
    x, y = here()
    right = jnp.concatenate([r[:, a:b] if len(r.shape) == 2 else r[a] for r, (a, b) in zip(rights, widths)], 1)

    def write(k, part, values):
        if not own:
            outs[0][(k, *part)] = values.astype(BF)
            return
        values = values + got[(k, *part)].astype(F32)
        if k == 2 and by_x:
            outs[3][...] = values[:192].astype(BF)
            outs[4][...] = values[192:].astype(BF)
        elif k == 2:
            outs[3 + part[0] // 2][part[0] % 2, part[1]] = values.astype(BF)
        else:
            outs[(0, 1, None, 2)[k]][part or Ellipsis] = values

    if by_x:
        for k in range(4):
            rows = pl.ds(pl.multiple_of(ahead(x, k) * 384, 128), 384)
            write(k, (), dot_rows(left[:, rows], right))
    else:
        whole = refs[-1]
        for i in range(4):
            whole[i] = dot_rows(left[:, i * 384 : (i + 1) * 384], right)
        for k in range(4):
            for i in range(4):
                for z in range(2):
                    rows = pl.ds(pl.multiple_of((z * 4 + ahead(y, k)) * 48, 16), 48)
                    write(k, (i, z), whole[i, rows, :])


def weight_pieces(by_x, left, rights, widths, got=(), first=()):
    width = sum(b - a if r.ndim == 2 else b for r, (a, b) in zip(rights, widths))
    shape = (384, width) if by_x else (4, 2, 48, width)
    if got:
        near, far = near_core(shape, F32), near_core((shape[0] // 2, *shape[1:]), BF)
        outs = [near] * 3 + [far] * 2
    else:
        outs = jax.ShapeDtypeStruct((4, *shape), BF)
    count = 1 + len(rights) + len(got)

    def kernel(*refs):
        pieces_kernel(by_x, bool(got), widths, *refs[:count], *refs[count + len(first) :])

    return pl.pallas_call(
        kernel,
        in_specs=in_vmem(count) + anywhere(len(first)),
        out_specs=in_vmem(5) if got else in_vmem(1)[0],
        out_shape=outs,
        scratch_shapes=[] if by_x else [pltpu.VMEM((4, 384, width), F32)],
        compiler_params=pltpu.CompilerParams(vmem_limit_bytes=24 * 1024 * 1024),
        cost_estimate=cost(2),
        name="weight_pieces",
    )(left, *rights, *got, *first)


def pass_kernel(plus, minus, left, right, *refs):
    on, back = refs[-2:]
    half = left.shape[0]
    on[:half] = (plus[:half] + left[...].astype(F32)).astype(BF)
    on[half:] = plus[half:].astype(BF)
    back[:half] = minus[:half].astype(BF)
    back[half:] = (minus[half:] + right[...].astype(F32)).astype(BF)


def pass_on(by_x, pieces, *first):
    perms = XS if by_x else YS
    left, right = send(pieces[3], perms[1]), send(pieces[4], perms[3])
    shape = near_core(pieces[1].shape, BF)
    return pl.pallas_call(
        pass_kernel,
        in_specs=in_vmem(4) + anywhere(len(first)),
        out_specs=in_vmem(2),
        out_shape=[shape, shape],
        compiler_params=pltpu.CompilerParams(vmem_limit_bytes=16 * 1024 * 1024),
        cost_estimate=cost(1),
        name="pass_on",
    )(pieces[1], pieces[2], left, right, *first)


def near_sum_kernel(by_x, own, one, two, *outs):
    outs = outs[-5:]
    x, y = here()
    total = own[...] + one[...].astype(F32) + two[...].astype(F32)
    whole = outs[4]
    whole[...] = total.reshape(whole.shape)
    for k in range(4):
        if by_x:
            for z in range(2):
                outs[k][z] = whole[z, ahead(y, k)].astype(outs[k].dtype)
        else:
            outs[k][...] = whole[ahead(x, k)].astype(outs[k].dtype)


def near_sum(by_x, own, got, first):
    width = own.shape[-1]
    shape = (2, 48, width)
    return pl.pallas_call(
        lambda *refs: near_sum_kernel(by_x, *refs),
        in_specs=in_vmem(3) + anywhere(len(first)),
        out_specs=in_vmem(4),
        out_shape=[near_core(shape, F32)] + [near_core(shape, BF)] * 3,
        scratch_shapes=[pltpu.VMEM((2, 4, 48, width) if by_x else (4, 2, 48, width), F32)],
        compiler_params=pltpu.CompilerParams(vmem_limit_bytes=16 * 1024 * 1024),
        cost_estimate=cost(1),
        name="near_sum",
    )(own, *got, *first)


def scatter_near(by_x, pieces, passed, *first):
    near = XS if by_x else YS
    return near_sum(by_x, pieces[0], [send(passed[0], near[1]), send(passed[1], near[3])], first)


def send_far(by_x, pieces):
    far = YS if by_x else XS
    return [send(pieces[k], far[k]) for k in (1, 2, 3)]


def sum_far(pieces, got):
    got = [values.astype(F32) for values in got]
    return pieces[0] + got[1] + (got[0] + got[2])


def plane_other(values, z):
    return send(lax.dynamic_index_in_dim(values, 1 - z, 0, keepdims=False).astype(BF), ZHI)


def plane_sum(values, other, z):
    return lax.dynamic_index_in_dim(values, z, 0, keepdims=False) + other.astype(F32)


def own_rows(total, c):
    mine = lax.dynamic_slice_in_dim(total, c * 24, 24, 0)
    other = send(lax.dynamic_slice_in_dim(total, (1 - c) * 24, 24, 0), CORE)
    return jnp.where(c == 0, mine, other), jnp.where(c == 0, other, mine)


def around(values, perms):
    got = [send(values, perms[k]) for k in (1, 2, 3)]
    return (values + got[1]) + (got[0] + got[2])


def dot(left, right):
    return jnp.dot(left, right, preferred_element_type=F32)


def dot_rows(left, right):
    return lax.dot_general(left, right, (((0,), (0,)), ((), ())), preferred_element_type=F32)


def dot_cols(left, right):
    return lax.dot_general(left, right, (((1,), (1,)), ((), ())), preferred_element_type=F32)


def silu_slope(values):
    sig = jax.nn.sigmoid(values)
    return sig * (1.0 + values * (1.0 - sig))


def down(values, offset):
    return values if offset == 0 else pltpu.roll(values, offset, 0)


def up(values, offset):
    return values if offset == 0 else pltpu.roll(values, values.shape[0] - offset, 0)


def conv_of(pre, taps, bias, masks):
    out = bias + taps[3:4] * pre
    for offset in (1, 2, 3):
        out = out + taps[3 - offset : 4 - offset] * (down(pre, offset) * masks[:, offset : offset + 1])
    return out


def lane_halves(values):
    low = lax.broadcasted_iota(jnp.int32, (1, TILE), 1) < 64
    zero = jnp.zeros_like(values)
    return jnp.where(low, values, zero), jnp.where(low, zero, values)


def params(mebibytes):
    return pltpu.CompilerParams(dimension_semantics=("arbitrary",), vmem_limit_bytes=mebibytes * 1024 * 1024)


def full(*shape):
    return pl.BlockSpec(shape, lambda i: (0,) * len(shape), pipeline_mode=pl.Buffered(1))


def out_full(*shape):
    return pl.BlockSpec(shape, lambda i: (0,) * len(shape))


def block(count):
    return pl.BlockSpec((count, BLOCK), lambda i: (0, i))


WIDE = 384


def wide(count):
    return pl.BlockSpec((count, WIDE), lambda i: (0, i))


def running(values):
    row = lax.broadcasted_iota(jnp.int32, values.shape, 0)
    offset = 1
    while offset < values.shape[0]:
        values = values + jnp.where(row >= offset, pltpu.roll(values, offset, 0), 0.0)
        offset *= 2
    return values


def visible_of(seg_col, seg_row, later_rows):
    row = lax.broadcasted_iota(jnp.int32, (LEN, LEN), 0)
    col = lax.broadcasted_iota(jnp.int32, (LEN, LEN), 1)
    ordered = (row <= col) if later_rows else (row >= col)
    return ordered & (seg_col[...] == seg_row[...])


def prep_kernel(normed, tail_own, tail_peer, seg_col, seg_row, masks, taps, bias, heads, bc_w, scores, scores_t, act, pre, cols, rows, steps):
    bc_w[0] = tail_own[0, :, :TILE]
    bc_w[1] = tail_peer[0, :, :TILE]
    own = dot(normed[...], tail_own[0])
    peer = dot(normed[...], tail_peer[0])
    core0 = jnp.full((LEN, TILE), lax.rem(lax.axis_index("dp"), 2)) == 0
    pre[:, :TILE] = jnp.where(core0, own[:, :TILE], peer[:, :TILE])
    pre[:, TILE:] = jnp.where(core0, peer[:, :TILE], own[:, :TILE])
    conv_out = conv_of(pre[...], taps[...], bias[...], masks[...])
    act[...] = (conv_out * jax.nn.sigmoid(conv_out)).astype(BF)
    b_proj, c_proj = act[:, :TILE], act[:, TILE:]
    scores[...] = jnp.where(visible_of(seg_col, seg_row, False), dot_cols(c_proj, b_proj), 0.0)
    scores_t[...] = jnp.where(visible_of(seg_col, seg_row, True), dot_cols(b_proj, c_proj), 0.0)
    step_pre = own[:, TILE:] + pltpu.roll(peer[:, TILE:], 24, 1) + heads[0:1, :]
    step_size = jnp.maximum(step_pre, 0.0) + jnp.log1p(jnp.exp(-jnp.abs(step_pre)))
    sums = running(step_size * heads[1:2, :]) * LOG2E
    logs = jnp.log(step_size) * LOG2E
    steps[0] = step_pre
    steps[1] = step_size
    for i, values in enumerate((sums, sums - logs, logs)):
        cols[i] = values
        rows[i] = values.T


def prepare(normed, inner_own, inner_peer, seg_col, seg_row, masks, taps, bias, heads):
    tail = pl.BlockSpec((1, 1536, 256), lambda i: (3, 0, 0), pipeline_mode=pl.Buffered(1))
    shapes = [
        ((2, 1536, TILE), BF),
        ((LEN, LEN), F32),
        ((LEN, LEN), F32),
        ((LEN, 256), BF),
        ((LEN, 256), F32),
        ((3, LEN, TILE), F32),
        ((3, TILE, LEN), F32),
        ((2, LEN, TILE), F32),
    ]
    return pl.pallas_call(
        prep_kernel,
        grid=(1,),
        in_specs=[in_vmem(1)[0], tail, tail, full(LEN, 1), full(1, LEN), full(LEN, 4), full(4, 256), full(1, 256), full(8, TILE)],
        out_specs=in_vmem(len(shapes)),
        out_shape=[(near_core if i in (1, 5, 6) else outside)(shape, kind) for i, (shape, kind) in enumerate(shapes)],
        compiler_params=params(24),
        cost_estimate=cost(2),
        name="prepare",
    )(normed, inner_own, inner_peer, seg_col, seg_row, masks, taps, bias, heads)


def norm_kernel(hidden, cotangent, other, gain, whole, normed, scale, cot):
    first = jnp.full((256, 1536), lax.axis_index("tensor")) == 0
    mine, theirs = hidden[...].astype(F32), other[0:256].astype(F32)
    for part, values in enumerate((jnp.where(first, mine, theirs), jnp.where(first, theirs, mine))):
        rows = slice(part * 256, (part + 1) * 256)
        whole[rows, :] = values.astype(BF)
        inv = lax.rsqrt(jnp.sum(values * values, axis=1, keepdims=True) * (1.0 / 1536.0) + EPS)
        scale[rows, :] = jnp.broadcast_to(inv, (256, TILE))
        normed[rows, :] = (values * inv * gain[...]).astype(BF)
    mine, theirs = cotangent[...].astype(F32), other[256:512].astype(F32)
    cot[0:256, :] = jnp.where(first, mine, theirs).astype(BF)
    cot[256:512, :] = jnp.where(first, theirs, mine).astype(BF)


def norm_of(hidden, cotangent, other, gain):
    whole = near_core((LEN, 1536), BF)
    return pl.pallas_call(
        norm_kernel,
        in_specs=in_vmem(4),
        out_specs=in_vmem(4),
        out_shape=[outside((LEN, 1536), BF), whole, outside((LEN, TILE), F32), whole],
        compiler_params=pltpu.CompilerParams(vmem_limit_bytes=24 * 1024 * 1024),
        cost_estimate=cost(2),
        name="input_norm",
    )(hidden, cotangent, other, gain)


def mix_kernel(half, normed, weight, taps, bias, masks, scores, cols, rows, pre, act, mixed):
    pre[...] = dot(normed[...], weight[0])
    conv_out = conv_of(pre[...], taps[...], bias[...], masks[...])
    act[...] = (conv_out * jax.nn.sigmoid(conv_out)).astype(BF)
    sums_all = pltpu.roll(cols[0], lax.rem(TILE - 24 * half - 8 * pl.program_id(0), TILE), 1)
    for pair in range(2):
        lanes = slice(pair * TILE, (pair + 1) * TILE)
        halves = lane_halves(act[:, lanes])
        for tile in range(4):
            here = slice(tile * TILE, (tile + 1) * TILE)
            weights, values = [], []
            for side in range(2):
                head = 2 * pair + side
                sums = sums_all[here, head : head + 1]
                if tile:
                    decay = jnp.exp2(sums - rows[1, head : head + 1, : tile * TILE])
                    weights.append((scores[here, : tile * TILE] * decay).astype(BF))
                    values.append(halves[side][: tile * TILE])
                decay = jnp.exp2(jnp.minimum(sums - rows[1, head : head + 1, here], rows[2, head : head + 1, here]))
                weights.append((scores[here, here] * decay).astype(BF))
                values.append(halves[side][here])
            mixed[here, lanes] = dot(jnp.concatenate(weights, 1), jnp.concatenate(values, 0))


def third_of(count, half):
    return pl.BlockSpec((count, BLOCK), lambda i: (0, 3 * half + i))


def rows_of(half):
    return pl.BlockSpec((3, 8, LEN), lambda i: (0, 3 * half + i, 0))


def mix_forward(half, normed, weight, taps, bias, masks, scores, cols, rows):
    return pl.pallas_call(
        lambda *refs: mix_kernel(half, *refs),
        grid=(3,),
        in_specs=[
            in_vmem(1)[0],
            pl.BlockSpec((1, 1536, BLOCK), lambda i: (i, 0, 0)),
            third_of(4, half),
            third_of(1, half),
            full(LEN, 4),
            in_vmem(1)[0],
            in_vmem(1)[0],
            rows_of(half),
        ],
        out_specs=[block(LEN)] * 3,
        out_shape=[
            outside((LEN, 768), F32),
            near_core((LEN, 768), BF),
            near_core((LEN, 768), F32),
        ],
        compiler_params=params(24),
        cost_estimate=cost(6.2),
        name="mix_forward",
    )(normed, weight, taps, bias, masks, scores, cols, rows)


def gate_kernel(last, normed, cot, gate_w, out_w, act, mixed, skip, gain, *refs):
    step = pl.program_id(0)
    before = refs[0] if last else None
    gate_pre, grad_gn, stats, squares, dots = refs[last:]

    @pl.when(step == 0)
    def _():
        squares[...] = before[0] if last else jnp.zeros_like(squares)
        dots[...] = before[1] if last else jnp.zeros_like(dots)

    pre = dot(normed[...], gate_w[0])
    upper = dot(cot[...], out_w[0])
    gate_pre[...] = pre
    grad_gn[...] = upper
    mixer_y = mixed[...] + skip[...] * act[...].astype(F32)
    gated = mixer_y * (pre * jax.nn.sigmoid(pre))
    square = gated * gated
    product = upper * gain[...] * gated
    squares[...] += square[:, :TILE] + square[:, TILE : 2 * TILE] + square[:, 2 * TILE :]
    dots[...] += product[:, :TILE] + product[:, TILE : 2 * TILE] + product[:, 2 * TILE :]

    @pl.when(step == 1)
    def _():
        if last:
            stats[0:1, :] = jnp.sum(squares[...].T, axis=0, keepdims=True)
            stats[1:2, :] = jnp.sum(dots[...].T, axis=0, keepdims=True)
            stats[2:8, :] = jnp.zeros((6, LEN), F32)
        else:
            stats[0] = squares[...]
            stats[1] = dots[...]


def half_of(count, half):
    return pl.BlockSpec((count, WIDE), lambda i: (0, 2 * half + i))


def gate_forward(half, normed, cot, rest, act, mixed, skip, gain, before=()):
    weight = lambda part: pl.BlockSpec((1, 1536, WIDE), lambda i: (2 * part + i, 0, 0))
    stats = (8, LEN) if half else (2, LEN, TILE)
    kept = near_core
    return pl.pallas_call(
        lambda *refs: gate_kernel(half, *refs),
        grid=(2,),
        in_specs=[
            *in_vmem(2),
            weight(0),
            weight(1),
            wide(LEN),
            wide(LEN),
            half_of(1, half),
            half_of(1, half),
        ]
        + [full(2, LEN, TILE)] * half,
        out_specs=[wide(LEN), wide(LEN), out_full(*stats)],
        out_shape=[
            kept((LEN, 768), F32),
            kept((LEN, 768), F32),
            jax.ShapeDtypeStruct(stats, F32),
        ],
        scratch_shapes=[pltpu.VMEM((LEN, TILE), F32)] * 2,
        compiler_params=params(24),
        cost_estimate=cost(4.2),
        name="gate_forward",
    )(normed, cot, rest, rest, act, mixed, skip, gain, *before)


def slope_kernel(stats, others, *refs):
    peer_in, own_in, skip, gain, normed, cot = refs[0:4], refs[4:8], *refs[8:12]
    peer_out, own_out, gain_grad = refs[12:15], refs[15:18], refs[18]
    part_gate, part_out, scale, dots, whole = refs[19:]
    step = pl.program_id(0)

    @pl.when(step == 0)
    def _():
        inv = lax.rsqrt((stats[0:1, :] + others[0:1, :]) * (1.0 / 3072.0) + EPS)
        both = (stats[1:2, :] + others[1:2, :]) * (1.0 / 3072.0)
        scale[...] = jnp.broadcast_to(inv, (TILE, LEN)).T
        dots[...] = jnp.broadcast_to(inv * inv * inv * both, (TILE, LEN)).T

    def slopes(gate_pre, grad_gn, act, mixed, grad_y, gate_low, gnormed):
        for part in range(3):
            lanes = slice(part * TILE, (part + 1) * TILE)
            q = scale[...]
            pre = gate_pre[:, lanes]
            sig = jax.nn.sigmoid(pre)
            gate_act = pre * sig
            mixer_y = mixed[:, lanes] + skip[:, lanes] * act[:, lanes].astype(F32)
            gated = mixer_y * gate_act
            scaled = gated * q
            gnormed[:, lanes] = (scaled * gain[:, lanes]).astype(BF)
            upper = grad_gn[:, lanes]
            gain_grad[:, lanes] = jnp.sum(upper * scaled, axis=0, keepdims=True)
            grad_gated = q * gain[:, lanes] * upper - gated * dots[...]
            grad_y[:, lanes] = grad_gated * gate_act
            gate_low[:, lanes] = (grad_gated * mixer_y * (sig * (1.0 + pre * (1.0 - sig)))).astype(BF)

    @pl.when(step >= 2)
    def _():
        slopes(*own_in, *own_out)

    @pl.when(step < 2)
    def _():
        slopes(*peer_in, *peer_out)
        x, y = here()
        for k in range(4):
            rows = pl.ds(pl.multiple_of(ahead(x, k) * 384, 128), 384)
            part_gate[k] = dot_rows(normed[:, rows], peer_out[1][...]).astype(BF)
        for i in range(4):
            whole[...] = dot_rows(cot[:, i * 384 : (i + 1) * 384], peer_out[2][...])
            for k in range(4):
                for z in range(2):
                    rows = pl.ds(pl.multiple_of((z * 4 + ahead(y, k)) * 48, 16), 48)
                    part_out[k, i, z] = whole[rows, :].astype(BF)


def gate_backward(stats, others, peer, own, skip, gain, normed, cot):
    early, late = lambda i: jnp.minimum(i, 1), lambda i: jnp.maximum(i - 2, 0)
    early_block, late_block = [pl.BlockSpec((LEN, WIDE), lambda i, at=at: (0, at(i))) for at in (early, late)]
    turned = pl.BlockSpec((1, WIDE), lambda i: (0, (i + 2) % 4))
    low, full_y = outside((LEN, 768), BF), outside((LEN, 768), F32)
    return pl.pallas_call(
        slope_kernel,
        grid=(4,),
        in_specs=[full(8, LEN), full(8, LEN)] + [early_block] * 4 + [late_block] * 4 + [turned] * 2 + in_vmem(2),
        out_specs=[early_block] * 3
        + [late_block] * 3
        + [
            turned,
            pl.BlockSpec((4, 384, WIDE), lambda i: (0, 0, early(i))),
            pl.BlockSpec((4, 4, 2, 48, WIDE), lambda i: (0, 0, 0, 0, early(i))),
        ],
        out_shape=[full_y, low, low] * 2
        + [
            jax.ShapeDtypeStruct((1, 1536), F32),
            jax.ShapeDtypeStruct((4, 384, 768), BF),
            jax.ShapeDtypeStruct((4, 4, 2, 48, 768), BF),
        ],
        scratch_shapes=[pltpu.VMEM((LEN, TILE), F32)] * 2 + [pltpu.VMEM((384, WIDE), F32)],
        compiler_params=params(28),
        cost_estimate=cost(10),
        name="gate_backward",
    )(stats, others, *peer, *own, skip, gain, normed, cot)


def product_kernel(own, peer, weight_own, weight_peer, *refs):
    target, total = refs[-2:]
    step = pl.program_id(0)
    for test, left, weight in ((step < 2, own, weight_own), (step >= 2, peer, weight_peer)):

        @pl.when(test)
        def _(left=left, weight=weight):
            part = dot_cols(left[...], weight[0])

            @pl.when(step == 0)
            def _():
                total[...] = part

            @pl.when(step > 0)
            def _():
                total[...] += part

    @pl.when(step == 3)
    def _():
        target[...] = total[...].astype(target.dtype)


def product(own, peer, rest_own, rest_peer, kind, target, *first):
    early = lambda i: jnp.minimum(i, 1)
    late = lambda i: jnp.maximum(i - 2, 0)
    return pl.pallas_call(
        product_kernel,
        grid=(4,),
        in_specs=[
            pl.BlockSpec((LEN, WIDE), lambda i: (0, early(i))),
            pl.BlockSpec((LEN, WIDE), lambda i: (0, late(i))),
            pl.BlockSpec((1, 1536, WIDE), lambda i: (2 * kind + early(i), 0, 0)),
            pl.BlockSpec((1, 1536, WIDE), lambda i: (2 * kind + late(i), 0, 0)),
        ]
        + anywhere(len(first)),
        out_specs=in_vmem(1)[0],
        out_shape=jax.ShapeDtypeStruct((LEN, 1536), target),
        scratch_shapes=[pltpu.VMEM((LEN, 1536), F32)],
        compiler_params=params(24),
        cost_estimate=cost(4),
        name="product",
    )(far_off(own), far_off(peer), far_off(rest_own), far_off(rest_peer), *first)


SEEN = [(j, i) for j in range(4) for i in range(j, 4)]


def back_kernel(half, grad_y, act, mixed, pre, scores, taps, bias, masks, cols, rows, skip, *refs):
    step = pl.program_id(0)
    if half:
        inner_low, sums, flows, grad_scores, grad_act = refs[-5:]
    else:
        flows_0, scores_0 = refs[:2]
        inner_low, sums, flows, grad_scores, scores_low, grad_act = refs[-6:]

    @pl.when(step == 0)
    def _():
        grad_scores[...] = jnp.zeros_like(grad_scores) if half else scores_0[...]
        flows[...] = jnp.zeros_like(flows) if half else flows_0[...]

    turn = lax.rem(TILE - 24 * half - 8 * step, TILE)
    back_all, most_all = pltpu.roll(cols[1], turn, 1), pltpu.roll(cols[2], turn, 1)

    pairs = []
    for pair in range(2):
        lanes = slice(pair * TILE, (pair + 1) * TILE)
        low = grad_y[:, lanes].astype(BF)
        pairs.append((lane_halves(act[:, lanes]), low, lane_halves(low)))
    for tile in range(4):
        here = slice(tile * TILE, (tile + 1) * TILE)
        after = slice((tile + 1) * TILE, LEN)
        add_diag, add_rest = 0.0, 0.0
        for pair in range(2):
            act_halves, low, low_halves = pairs[pair]
            weights, values = [], []
            stacked = jnp.concatenate([act_halves[0][here], act_halves[1][here]], 0)
            grad_w = dot_cols(stacked, low[tile * TILE :])
            for side in range(2):
                head = 2 * pair + side
                back = back_all[here, head : head + 1]
                most = most_all[here, head : head + 1]
                own = slice(side * TILE, (side + 1) * TILE)
                decay = jnp.exp2(jnp.minimum(rows[0, head : head + 1, here] - back, most))
                add_diag = add_diag + grad_w[own, :TILE] * decay
                weights.append((scores[here, here] * decay).astype(BF))
                values.append(low_halves[side][here])
                if tile < 3:
                    decay = jnp.exp2(rows[0, head : head + 1, after] - back)
                    add_rest = add_rest + grad_w[own, TILE:] * decay
                    weights.append((scores[here, after] * decay).astype(BF))
                    values.append(low_halves[side][after])
            lanes = slice(pair * TILE, (pair + 1) * TILE)
            grad_act[here, lanes] = dot(jnp.concatenate(weights, 1), jnp.concatenate(values, 0))
        grad_scores[here, here] += add_diag
        if tile < 3:
            grad_scores[here, after] += add_rest

    if not half:

        @pl.when(step == 2)
        def _():
            for at, (j, i) in enumerate(SEEN):
                rows_j, cols_i = slice(j * TILE, (j + 1) * TILE), slice(i * TILE, (i + 1) * TILE)
                scores_low[at] = grad_scores[rows_j, cols_i].astype(BF)

    lane = lax.broadcasted_iota(jnp.int32, (1, TILE), 1)
    row_flows, col_flows = 0.0, 0.0

    low_lane = lax.broadcasted_iota(jnp.int32, (1, TILE), 1) < 64
    for pair in range(2):
        lanes = slice(pair * TILE, (pair + 1) * TILE)
        values = act[:, lanes].astype(F32)
        grad = grad_y[:, lanes]
        row_flow = grad.astype(BF).astype(F32) * mixed[:, lanes]
        col_flow = values * grad_act[:, lanes]
        for side, mask in ((0, low_lane), (1, ~low_lane)):
            head = 2 * pair + side
            here = lane == 24 * half + 8 * step + head
            row_flows += jnp.where(here, jnp.sum(jnp.where(mask, row_flow, 0.0), axis=1, keepdims=True), 0.0)
            col_flows += jnp.where(here, jnp.sum(jnp.where(mask, col_flow, 0.0), axis=1, keepdims=True), 0.0)
        taps_l, masks_v = taps[:, lanes], masks[...]
        pre_l = pre[:, lanes]
        conv_out = conv_of(pre_l, taps_l, bias[:, lanes], masks_v)
        grad_conv = (grad_act[:, lanes] + skip[:, lanes] * grad) * silu_slope(conv_out)
        grad_pre = taps_l[3:4] * grad_conv
        sums[3:4, lanes] = jnp.sum(grad_conv * pre_l, axis=0, keepdims=True)
        for offset in (1, 2, 3):
            masked = grad_conv * masks_v[:, offset : offset + 1]
            tap = 3 - offset
            sums[tap : tap + 1, lanes] = jnp.sum(masked * down(pre_l, offset), axis=0, keepdims=True)
            grad_pre = grad_pre + taps_l[tap : tap + 1] * up(masked, offset)
        sums[4:5, lanes] = jnp.sum(grad_conv, axis=0, keepdims=True)
        sums[5:6, lanes] = jnp.sum(grad * values, axis=0, keepdims=True)
        sums[6:8, lanes] = jnp.zeros((2, TILE), F32)
        inner_low[:, lanes] = grad_pre.astype(BF)
    flows[0] += row_flows
    flows[1] += col_flows


def mix_backward(half, grad_y, act, mixed, pre, scores_t, taps, bias, masks, cols, rows, skip, before=(), first=()):
    low = [] if half else [jax.ShapeDtypeStruct((10, TILE, TILE), BF)]
    return pl.pallas_call(
        lambda *refs: back_kernel(half, *refs),
        grid=(3,),
        in_specs=[
            block(LEN),
            block(LEN),
            block(LEN),
            block(LEN),
            in_vmem(1)[0],
            third_of(4, half),
            third_of(1, half),
            full(LEN, 4),
            in_vmem(1)[0],
            rows_of(half),
            third_of(1, half),
            *in_vmem(len(before)),
            *anywhere(len(first)),
        ],
        out_specs=[block(LEN), block(8), *in_vmem(2 + len(low))],
        out_shape=[
            near_core((LEN, 768), BF),
            jax.ShapeDtypeStruct((8, 768), F32),
            near_core((2, LEN, TILE), F32),
            near_core((LEN, LEN), F32),
        ]
        + low,
        scratch_shapes=[pltpu.VMEM((LEN, BLOCK), F32)],
        compiler_params=params(24),
        cost_estimate=cost(9.8),
        name="mix_backward",
    )(grad_y, act, mixed, pre, scores_t, taps, bias, masks, cols, rows, skip, *before, *first)


def tail_kernel(mine, other, act, pre, seg_col, seg_row, masks, taps, bias, shares, *refs):
    tails, bc_sums, both = refs[-3:]
    seen = visible_of(seg_col, seg_row, True)
    for at, (j, i) in enumerate(SEEN):
        tile = (slice(j * TILE, (j + 1) * TILE), slice(i * TILE, (i + 1) * TILE))
        both[tile] = mine[tile] + other[at].astype(F32)
        if i > j:
            both[tile[1], tile[0]] = jnp.zeros((TILE, TILE), F32)
    low = jnp.where(seen, both[...], 0.0).astype(BF)
    b_proj, c_proj = act[:, :TILE], act[:, TILE:]
    core0 = jnp.full((LEN, TILE), lax.rem(lax.axis_index("dp"), 2)) == 0
    bc_low = []
    for part, grad in ((0, dot(low, c_proj)), (1, dot_rows(low, b_proj))):
        lanes = slice(part * TILE, (part + 1) * TILE)
        taps_l, pre_l, masks_v = taps[:, lanes], pre[:, lanes], masks[...]
        grad_conv = grad * silu_slope(conv_of(pre_l, taps_l, bias[:, lanes], masks_v))
        grad_pre = taps_l[3:4] * grad_conv
        bc_sums[3:4, lanes] = jnp.sum(grad_conv * pre_l, axis=0, keepdims=True)
        for offset in (1, 2, 3):
            masked = grad_conv * masks_v[:, offset : offset + 1]
            tap = 3 - offset
            bc_sums[tap : tap + 1, lanes] = jnp.sum(masked * down(pre_l, offset), axis=0, keepdims=True)
            grad_pre = grad_pre + taps_l[tap : tap + 1] * up(masked, offset)
        bc_sums[4:5, lanes] = jnp.sum(grad_conv, axis=0, keepdims=True)
        bc_sums[5:8, lanes] = jnp.zeros((3, TILE), F32)
        bc_low.append(grad_pre)
    for part, bc in ((0, jnp.where(core0, bc_low[0], bc_low[1])), (1, jnp.where(core0, bc_low[1], bc_low[0]))):
        tails[part, :, :TILE] = bc.astype(BF)
        tails[part, :, TILE:] = shares[part, :, TILE:]


def step_kernel(heads, steps, flows, shares, head_sums):
    step_pre, step_size, rate = steps[0], steps[1], heads[1:2, :]
    change = flows[0] - flows[1]
    before = running(change)
    grad_rate = before[LEN - 1 : LEN, :] - before + change
    sig = jax.nn.sigmoid(step_pre)
    tiny = step_size < 1e-30
    ratio = jnp.where(tiny, 1.0, sig / jnp.where(tiny, 1.0, step_size))
    grad_pre = flows[1] * ratio + grad_rate * rate * sig
    head_sums[0:1, :] = jnp.sum(grad_pre, axis=0, keepdims=True)
    head_sums[1:2, :] = jnp.sum(grad_rate * step_size, axis=0, keepdims=True) * rate
    head_sums[2:8, :] = jnp.zeros((6, TILE), F32)
    own_lane = lax.broadcasted_iota(jnp.int32, (LEN, TILE), 1) < 24
    for part, grad in ((0, grad_pre), (1, pltpu.roll(grad_pre, TILE - 24, 1))):
        shares[part, :, :TILE] = jnp.zeros((LEN, TILE), BF)
        shares[part, :, TILE:] = jnp.where(own_lane, grad, 0.0).astype(BF)


def step_backward(heads, steps, flows):
    return pl.pallas_call(
        step_kernel,
        in_specs=in_vmem(3),
        out_specs=in_vmem(2),
        out_shape=[near_core((2, LEN, 256), BF), jax.ShapeDtypeStruct((8, TILE), F32)],
        compiler_params=pltpu.CompilerParams(vmem_limit_bytes=12 * 1024 * 1024),
        cost_estimate=cost(1),
        name="step_backward",
    )(heads, steps, flows)


def tail_backward(mine, other, act, pre, seg_col, seg_row, masks, taps, bias, shares, *first):
    shapes = [((2, LEN, 256), BF), ((8, 256), F32)]
    return pl.pallas_call(
        tail_kernel,
        in_specs=in_vmem(10) + anywhere(len(first)),
        out_specs=in_vmem(len(shapes)),
        out_shape=[near_core(*shapes[0]), jax.ShapeDtypeStruct(*shapes[1])],
        scratch_shapes=[pltpu.VMEM((LEN, LEN), F32)],
        compiler_params=pltpu.CompilerParams(vmem_limit_bytes=18 * 1024 * 1024),
        cost_estimate=cost(2),
        name="tail_backward",
    )(mine, other, act, pre, seg_col, seg_row, masks, taps, bias, shares, *first)


def bc_kernel(tails, weight, hidden, scale, first, part, gain):
    t = lax.axis_index("tensor")
    rows = pl.ds(pl.multiple_of(t * 256, 256), 256)
    values = dot_cols(tails[0, rows, :TILE], weight[0]) + dot_cols(tails[1, rows, :TILE], weight[1])
    part[...] = values
    gain[...] = jnp.sum(values * hidden[...].astype(F32) * scale[rows, :1], axis=0, keepdims=True)


def bc_normed(tails, weight, hidden, scale, first):
    return pl.pallas_call(
        bc_kernel,
        grid=(1,),
        in_specs=[in_vmem(1)[0], full(2, 1536, TILE), full(256, 1536), full(LEN, TILE)] + anywhere(1),
        out_specs=[out_full(256, 1536), out_full(1, 1536)],
        out_shape=[outside((256, 1536), F32), jax.ShapeDtypeStruct((1, 1536), F32)],
        compiler_params=params(16),
        cost_estimate=cost(1.5),
        name="bc_normed",
    )(tails, far_off(weight), far_off(hidden), far_off(scale), first)


def normed_kernel(before, low_own, low_peer, shares, inner_own, inner_peer, resid, scale, *refs):
    low, gain, total = refs[-3:]
    step = pl.program_id(0)

    @pl.when(step == 0)
    def _():
        total[...] = before[...]

    for test, left, weight in (
        (step < 3, low_peer, inner_peer),
        ((step >= 3) & (step < 6), low_own, inner_own),
        (step == 6, shares, inner_own),
        (step == 7, shares, inner_peer),
    ):

        @pl.when(test)
        def _(left=left, weight=weight):
            values = left[0] if left is shares else left[...]
            total[...] += dot_cols(values, weight[0])

    @pl.when(step == 7)
    def _():
        for i in range(3):
            lanes = slice(i * LEN, (i + 1) * LEN)
            values = total[:, lanes]
            low[:, lanes] = values.astype(BF)
            gain[:, lanes] = jnp.sum(values * resid[:, lanes].astype(F32) * scale[:, :1], axis=0, keepdims=True)


def normed_backward(before, low_own, low_peer, shares, inner_own, inner_peer, resid, scale, *first):
    return pl.pallas_call(
        normed_kernel,
        grid=(8,),
        in_specs=[
            in_vmem(1)[0],
            pl.BlockSpec((LEN, BLOCK), lambda i: (0, jnp.clip(i - 3, 0, 2))),
            pl.BlockSpec((LEN, BLOCK), lambda i: (0, jnp.minimum(i, 2))),
            pl.BlockSpec((1, LEN, BLOCK), lambda i: (jnp.clip(i - 6, 0, 1), 0, 0)),
            pl.BlockSpec((1, 1536, BLOCK), lambda i: (jnp.clip(i - 3, 0, 3), 0, 0)),
            pl.BlockSpec((1, 1536, BLOCK), lambda i: (jnp.where(i < 3, i, 3), 0, 0)),
            in_vmem(1)[0],
            full(LEN, TILE),
        ]
        + anywhere(len(first)),
        out_specs=in_vmem(2),
        out_shape=[jax.ShapeDtypeStruct((LEN, 1536), BF), jax.ShapeDtypeStruct((1, 1536), F32)],
        scratch_shapes=[pltpu.VMEM((LEN, 1536), F32)],
        compiler_params=params(24),
        cost_estimate=cost(6),
        name="normed_backward",
    )(before, low_own, low_peer, shares, inner_own, inner_peer, resid, scale, *first)


def hidden_kernel(hidden, cotangent, scale, gain, low, got, bc_part, first, out):
    t = lax.axis_index("tensor")
    rows = pl.ds(pl.multiple_of(t * 256, 256), 256)
    grad = low[rows, :].astype(F32) + got[...].astype(F32) + bc_part[...]
    values = hidden[...].astype(F32)
    scaled = grad * gain[...]
    inv = scale[rows, :1]
    stat = jnp.sum(scaled * values, axis=1, keepdims=True) * (inv * inv * inv * (1.0 / 1536.0))
    out[...] = cotangent[...].astype(F32) + inv * scaled - values * stat


def hidden_grad(hidden, cotangent, scale, gain, low, got, bc_part, first):
    return pl.pallas_call(
        hidden_kernel,
        grid=(1,),
        in_specs=[
            full(256, 1536),
            full(256, 1536),
            full(LEN, TILE),
            full(1, 1536),
            full(LEN, 1536),
            full(256, 1536),
            full(256, 1536),
            pl.BlockSpec(memory_space=pl.ANY),
        ],
        out_specs=out_full(256, 1536),
        out_shape=jax.ShapeDtypeStruct((256, 1536), F32),
        compiler_params=params(20),
        cost_estimate=cost(3),
        name="hidden_grad",
    )(far_off(hidden), far_off(cotangent), far_off(scale), gain, low, got, far_off(bc_part), first)


def precise(left, right):
    return jnp.dot(left, right, preferred_element_type=F32, precision=lax.Precision.HIGHEST)


def small_kernel(sums_own, sums_peer, gain, norm_grad, norm_bc, bc_sums, head_sums, *refs):
    whole = refs[-1]
    core = lax.rem(lax.axis_index("dp"), 2)
    for row, own, peer in (
        (0, sums_own[0:5], sums_peer[0:5]),
        (5, gain[:, :768], gain[:, 768:]),
    ):
        flag = jnp.full(own.shape, core) == 0
        whole[row : row + own.shape[0], :768] = jnp.where(flag, own, peer)
        whole[row : row + own.shape[0], 768:] = jnp.where(flag, peer, own)
    whole[6:7, :] = norm_grad[...] + norm_bc[...]
    for tap in range(5):
        whole[7:8, tap * 256 : (tap + 1) * 256] = bc_sums[tap : tap + 1, :]
    unit = lax.broadcasted_iota(jnp.int32, (768, TILE), 0) // 64
    lane = lax.broadcasted_iota(jnp.int32, (768, TILE), 1)
    spot = (unit // 4) * 8 + unit % 4
    own = precise(sums_own[...], (lane == spot).astype(F32))
    peer = precise(sums_peer[...], (lane == spot + 24).astype(F32))
    heads = head_sums[...]
    rows = (heads[0:1], heads[1:2], (own + peer)[5:6])
    lane = lax.broadcasted_iota(jnp.int32, (1, TILE), 1)
    flag = jnp.full((1, TILE), core) == 0
    step, decay, skip = [
        jnp.where(flag, v, jnp.where(lane < 24, pltpu.roll(v, TILE - 24, 1), pltpu.roll(v, 24, 1))) for v in rows
    ]
    whole[7:8, 1280:1408] = jnp.where(lane < 64, step, pltpu.roll(skip, 64, 1))
    whole[7:8, 1408:1536] = decay


def small_of(*parts):
    shapes = [(8, 768), (8, 768), (1, 1536), (1, 1536), (1, 1536), (8, 256), (8, TILE)]
    return pl.pallas_call(
        small_kernel,
        grid=(1,),
        in_specs=[full(*shape) for shape in shapes] + anywhere(len(parts) - 7),
        out_specs=in_vmem(1)[0],
        out_shape=jax.ShapeDtypeStruct((8, 1536), F32),
        compiler_params=params(8),
        cost_estimate=cost(1),
        name="small_pack",
    )(*parts)


def outputs_kernel(mine, other, conv_grad, bias_grad, gain_grad, norm_grad, heads):
    def halves(rows, width):
        flag = jnp.full(mine[rows, :width].shape, lax.axis_index("tensor")) == 0
        a, b = mine[rows, :width], other[rows, :width]
        return jnp.where(flag, a, b), jnp.where(flag, b, a)

    for rows, target in ((slice(0, 4), conv_grad), (slice(4, 5), bias_grad), (slice(5, 6), gain_grad)):
        low, high = halves(rows, 1536)
        target[:, :1536] = low
        target[:, 1536:3072] = high
    for tap in range(4):
        conv_grad[tap : tap + 1, 3072:] = mine[7:8, tap * 256 : (tap + 1) * 256]
    bias_grad[:, 3072:] = mine[7:8, 1024:1280]
    norm_grad[...] = mine[6:7, :] + other[6:7, :]
    lane = lax.broadcasted_iota(jnp.int32, (TILE, 24), 0)
    head = lax.broadcasted_iota(jnp.int32, (TILE, 24), 1)
    spot = (head // 4) * 8 + head % 4
    for part, at in enumerate((1280, 1408)):
        flag = jnp.full((8, TILE), lax.axis_index("tensor")) == 0
        a, b = mine[:, at : at + TILE], other[:, at : at + TILE]
        for half, values in enumerate((jnp.where(flag, a, b), jnp.where(flag, b, a))):
            lanes = slice(half * 24, half * 24 + 24)
            heads[8 * part : 8 * part + 8, lanes] = precise(values, (lane == spot).astype(F32))
            if not part:
                heads[16:24, lanes] = precise(values, (lane == spot + 64).astype(F32))


def outputs_of(mine, other):
    shapes = [(4, 3328), (1, 3328), (1, 3072), (1, 1536), (24, 48)]
    return pl.pallas_call(
        outputs_kernel,
        in_specs=in_vmem(2),
        out_specs=in_vmem(5),
        out_shape=[jax.ShapeDtypeStruct(shape, F32) for shape in shapes],
        compiler_params=pltpu.CompilerParams(vmem_limit_bytes=16 * 1024 * 1024),
        cost_estimate=cost(1.5),
        name="small_unpack",
    )(mine, other)


def on_device(
    hidden,
    segments,
    norm_gain,
    in_weight,
    bc_weight,
    step_weight,
    conv_weight,
    conv_bias,
    step_bias,
    decay_log,
    skip_gain,
    gate_gain,
    out_weight,
    cotangent,
):
    t = lax.axis_index("tensor")
    d = lax.axis_index("dp")
    spot = (d // 16, (d // 8) % 2, (d // 2) % 4, d % 2)
    c = spot[3]

    def own_first(values, size):
        base = 2 * t * size
        return jnp.concatenate(
            [
                lax.dynamic_slice_in_dim(values, base + c * size, size, values.ndim - 1),
                lax.dynamic_slice_in_dim(values, base + (1 - c) * size, size, values.ndim - 1),
            ],
            values.ndim - 1,
        )

    def in_lanes(values):
        return jnp.pad(jnp.pad(values.reshape(6, 4), ((0, 0), (0, 4))).reshape(48), (0, 80))

    planes = pair_planes(pair_rows(*pack(in_weight, bc_weight, step_weight, out_weight), c), spot[1])
    tokens_other = swap_tensor(after(jnp.concatenate([hidden, cotangent], 0), planes))

    taps = own_first(conv_weight[:, :3072], 768)
    bias = own_first(conv_bias[None, :3072], 768)
    gain = own_first(gate_gain[None, :], 768)
    skip = jnp.repeat(own_first(skip_gain, 12), 64)[None, :]
    heads = jnp.stack(
        [in_lanes(own_first(step_bias, 12)), in_lanes(-jnp.exp(own_first(decay_log, 12)))]
        + [jnp.zeros((TILE,), F32)] * 6
    )
    bc_taps, bc_bias = conv_weight[:, 3072:], conv_bias[None, 3072:]
    seg = segments[0]
    seg_col, seg_row = segments.T, segments
    masks = jnp.stack(
        [(jnp.pad(seg, (o, 0), constant_values=-1)[:LEN] == seg).astype(F32) for o in range(4)], 1
    )

    a_near, b_near = ring(planes[..., :1280], YS), ring(planes[..., 1280:], XS)
    settings = (taps, bias, gain, skip, heads, bc_taps, bc_bias, seg_col, masks)
    a_first, b_first = place_near(a_near, b_near, 0, 512, settings)
    hidden_all, normed, norm_scale, cot_all = norm_of(hidden, cotangent, tokens_other, norm_gain[None])
    a_far, b_far = sides(a_first, XS), sides(b_first, YS)
    a_far, b_far = a_far + opposite(a_far, XS, 0), b_far + opposite(b_far, YS, 0)
    inner_own = place_far(a_far, b_far, 256, (normed,))
    inner_peer = send(inner_own, CORE)
    a_rest, b_rest = place_near(a_near, b_near, 512, 768, (inner_own,))
    a_rest, b_rest = sides(a_rest, XS), sides(b_rest, YS)

    bc_w, scores, scores_t, bc_act, bc_pre, cols, rows, steps = prepare(
        normed, inner_own, inner_peer, seg_col, seg_row, masks, bc_taps, bc_bias, heads
    )
    mixer = (taps, bias, masks, scores, cols, rows)
    pre_own, act_own, mixed_own = mix_forward(0, normed, inner_own, *mixer)
    a_more, b_more = opposites(a_rest, b_rest, act_own)
    a_rest, b_rest = a_rest + a_more, b_rest + b_more
    pre_peer, act_peer, mixed_peer = mix_forward(1, normed, inner_peer, *mixer)
    rest_own = place_far(a_rest, b_rest, WIDE, (act_peer,))
    rest_peer = send(rest_own, CORE)
    gate_own, gn_own, sums_own = gate_forward(0, normed, cot_all, rest_own, act_own, mixed_own, skip, gain)
    gate_peer, gn_peer, stats = gate_forward(1, normed, cot_all, rest_peer, act_peer, mixed_peer, skip, gain, (sums_own,))
    others = swap_tensor(stats)

    def other_tokens(values):
        return swap_tensor(lax.dynamic_slice_in_dim(values, (1 - t) * 256, 256, 0))

    def own_tokens(values, got=None):
        got = other_tokens(values) if got is None else got
        return lax.dynamic_slice_in_dim(values, t * 256, 256, 0).astype(F32) + got.astype(F32)

    (
        grad_y_peer,
        gate_low_peer,
        gnormed_peer,
        grad_y_own,
        gate_low,
        gnormed,
        gain_grad,
        gate_got,
        out_got,
    ) = gate_backward(
        stats,
        others,
        (gate_peer, gn_peer, act_peer, mixed_peer),
        (gate_own, gn_own, act_own, mixed_own),
        skip,
        gain,
        normed,
        cot_all,
    )
    gate_got, out_got = send(gate_got, CORE), send(out_got, CORE)
    branch = product(gnormed, gnormed_peer, rest_own, rest_peer, 1, BF)
    branch_got = other_tokens(branch)
    gate_pieces = weight_pieces(True, normed, (gate_low,), ((0, 768),), (gate_got,), (branch,))
    out_pieces = weight_pieces(False, cot_all, (gnormed,), ((0, 768),), (out_got,), (branch,))
    gate_grads = product(gate_low, gate_low_peer, rest_own, rest_peer, 0, F32, gate_pieces[3], out_pieces[3])
    mixed = (hidden.astype(F32) + own_tokens(branch, branch_got)).astype(BF)
    gate_passed, out_passed = pass_on(True, gate_pieces, gate_grads), pass_on(False, out_pieces, gate_grads)

    mixer = (scores_t, taps, bias, masks, cols, rows, skip)
    inner_peer_low, sums_peer, flows, grad_scores = mix_backward(
        1, grad_y_peer, act_peer, mixed_peer, pre_peer, *mixer, (), (gate_passed[0], out_passed[0])
    )
    a_part = weight_pieces(True, normed, (inner_peer_low,), ((0, 512),))
    a_got = send(a_part, CORE)
    gate_near = scatter_near(True, gate_pieces, gate_passed, a_part)
    out_near = scatter_near(False, out_pieces, out_passed, a_part)
    inner_own_low, sums_own, flows, grad_scores, scores_low = mix_backward(
        0, grad_y_own, act_own, mixed_own, pre_own, *mixer, (flows, grad_scores), (gate_near[1], out_near[1], branch_got)
    )
    scores_other = swap_tensor(scores_low)
    gate_far, out_far = send_far(True, gate_near), send_far(False, out_near)
    a_pieces = weight_pieces(True, normed, (inner_own_low,), ((0, 512),), (a_got,), tuple(gate_far))
    shares, head_sums = step_backward(heads, steps, flows)
    grad_low, norm_grad = normed_backward(
        gate_grads, inner_own_low, inner_peer_low, shares, inner_own, inner_peer, hidden_all, norm_scale, a_pieces[3]
    )
    grad_got = other_tokens(grad_low)
    a_passed = pass_on(True, a_pieces, norm_grad)
    tails, bc_sums = tail_backward(
        grad_scores, scores_other, bc_act, bc_pre, seg_col, seg_row, masks, bc_taps, bc_bias, shares, a_passed[0], *out_far
    )
    b_part = weight_pieces(False, normed, (inner_peer_low, tails), ((512, 768), (1, 256)))
    b_got = send(b_part, CORE)
    bc_part, norm_bc = bc_normed(tails, bc_w, hidden, norm_scale, b_part)
    small = small_of(sums_own, sums_peer, gain_grad, norm_grad, norm_bc, bc_sums, head_sums, norm_bc)
    small = small + send(small, CORE)
    b_pieces = weight_pieces(False, normed, (inner_own_low, tails), ((512, 768), (0, 256)), (b_got,), (small,))
    a_near_sum = scatter_near(True, a_pieces, a_passed, b_pieces[3])
    small = around(small, YS)
    rest_parts = jnp.concatenate([sum_far(gate_near, gate_far), sum_far(out_near, out_far)], 2)
    rest_other = plane_other(rest_parts, spot[1])
    b_passed = pass_on(False, b_pieces, a_near_sum[1], small, rest_other)
    grad_hidden = hidden_grad(
        hidden, cotangent, norm_scale, norm_gain[None], grad_low, grad_got, bc_part, b_passed[0]
    )
    b_near_sum = scatter_near(False, b_pieces, b_passed, grad_hidden)
    a_near_sum = [a_near_sum[0]] + [after(piece, b_passed[0]) for piece in a_near_sum[1:]]
    a_far, b_far = send_far(True, a_near_sum), send_far(False, b_near_sum)
    small = around(after(small, b_near_sum[1]), XS)
    small = small + send(small, ZHI)
    first_parts = jnp.concatenate([sum_far(a_near_sum, a_far), sum_far(b_near_sum, b_far)], 2)
    first_total = plane_sum(first_parts, plane_other(first_parts, spot[1]), spot[1])
    rest_total = plane_sum(rest_parts, rest_other, spot[1])
    both_rows = own_rows(jnp.concatenate([first_total, rest_total], 1), c)

    def columns(rows_of, start, size):
        return jnp.concatenate([part[:, start : start + size] for part in rows_of], 1)

    grad_in = jnp.stack([columns(both_rows, 1024, 768), columns(both_rows, 0, 768)])
    grad_bc = columns(both_rows, 768, 128)
    grad_step = jnp.concatenate(
        [part[:, 896:920].reshape(24, 3, 8)[:, :, :4].reshape(24, 12) for part in both_rows], 1
    )
    grad_out = columns(both_rows, 1792, 768).T

    conv_grad, bias_grad, gate_gain_grad, norm_gain_grad, head_grads = outputs_of(small, swap_tensor(small))
    return (
        mixed,
        grad_hidden,
        norm_gain_grad[0],
        grad_in,
        grad_bc,
        grad_step,
        conv_grad,
        bias_grad[0],
        head_grads[7],
        head_grads[15],
        head_grads[23],
        gate_gain_grad[0],
        grad_out,
    )


def solution(mesh):
    return jax.shard_map(
        on_device,
        mesh=mesh,
        in_specs=(
            P(("dp", "tensor"), None),
            P("dp", None),
            P(),
            P(None, "dp", "tensor"),
            P("dp", None),
            P("dp", "tensor"),
            P(),
            P(),
            P(),
            P(),
            P(),
            P(),
            P("tensor", "dp"),
            P(("dp", "tensor"), None),
        ),
        out_specs=(
            P(("dp", "tensor"), None),
            P(("dp", "tensor"), None),
            P(),
            P(None, "dp", "tensor"),
            P("dp", None),
            P("dp", "tensor"),
            P(),
            P(),
            P(),
            P(),
            P(),
            P(),
            P("tensor", "dp"),
        ),
        check_vma=False,
    )
```

```python
import jax
import jax.numpy as jnp
from jax import lax
from jax.experimental import pallas as pl
from jax.experimental.pallas import tpu as pltpu
from jax.sharding import PartitionSpec as P

EPS = 1e-05
LOG2E = 1.4426950408889634
BF = jnp.bfloat16
F32 = jnp.float32
LEN = 512
TILE = 128
BLOCK = 256


def cost(us):
    return pl.CostEstimate(flops=int(us * 1.0 * 1e9), bytes_accessed=int(us * 1.0 * 2.5e6), transcendentals=0)


SWAP = [(0, 1), (1, 0)]


def dp_index(x, z, y, c):
    return ((x * 2 + z) * 4 + y) * 2 + c


def dp_pairs(move):
    return [
        (dp_index(x, z, y, c), dp_index(*move(x, z, y, c)))
        for x in range(4)
        for z in range(2)
        for y in range(4)
        for c in range(2)
    ]


CORE = dp_pairs(lambda x, z, y, c: (x, z, y, 1 - c))
ACROSS = [
    (2 * dp_index(x, z, y, c) + t, 2 * dp_index(x, 1 - z, y, c) + 1 - t)
    for x in range(4)
    for z in range(2)
    for y in range(4)
    for c in range(2)
    for t in range(2)
]
ZHI = dp_pairs(lambda x, z, y, c: (x, 1 - z, y, c))
XS = {k: dp_pairs(lambda x, z, y, c, k=k: ((x + k) % 4, z, y, c)) for k in (1, 2, 3)}
YS = {k: dp_pairs(lambda x, z, y, c, k=k: (x, z, (y + k) % 4, c)) for k in (1, 2, 3)}


def send(values, pairs):
    return lax.ppermute(values, "dp", pairs)


def swap_tensor(values):
    return lax.ppermute(values, "tensor", SWAP)


def near_core(shape, kind):
    return pltpu.VMEM(shape, kind)


def outside(shape, kind):
    return pltpu.HBM(shape, kind)


def far_off(values):
    return pltpu.with_memory_space_constraint(values, pltpu.HBM)


def anywhere(count):
    return [pl.BlockSpec(memory_space=pl.ANY)] * count


def in_vmem(count):
    return [pl.BlockSpec(memory_space=pltpu.VMEM)] * count


def after(values, *first):
    return pl.pallas_call(
        lambda *refs: None,
        in_specs=anywhere(1 + len(first)),
        out_specs=pl.BlockSpec(memory_space=pl.ANY),
        out_shape=jax.ShapeDtypeStruct(values.shape, values.dtype),
        input_output_aliases={0: 0},
        cost_estimate=cost(0.01),
        name="after",
    )(values, *first)


def sides(values, perms):
    return [values, send(values, perms[1]), send(values, perms[3])]


def opposite(pieces, perms, axis):
    half = pieces[0].shape[axis] // 2
    front = lax.slice_in_dim(pieces[1], 0, half, axis=axis)
    back = lax.slice_in_dim(pieces[2], half, 2 * half, axis=axis)
    return [send(front, perms[1]), send(back, perms[3])]


def halves_kernel(a_back, a_ahead, b_back, b_ahead, first, a_front, a_rear, b_front, b_rear, sems):
    a_half, b_half = a_front.shape[0], b_front.shape[0]
    copy_all(
        [
            (a_back.at[pl.ds(0, a_half)], a_front),
            (a_ahead.at[pl.ds(a_half, a_half)], a_rear),
            (b_back.at[pl.ds(0, b_half)], b_front),
            (b_ahead.at[pl.ds(b_half, b_half)], b_rear),
        ],
        sems,
    )


def opposites(a_pieces, b_pieces, first):
    shapes = [(v.shape[0] // 2, *v.shape[1:]) for v in (a_pieces[0], a_pieces[0], b_pieces[0], b_pieces[0])]
    parts = pl.pallas_call(
        halves_kernel,
        in_specs=in_vmem(4) + anywhere(1),
        out_specs=in_vmem(4),
        out_shape=[jax.ShapeDtypeStruct(shape, BF) for shape in shapes],
        scratch_shapes=[pltpu.SemaphoreType.DMA((4,))],
        compiler_params=pltpu.CompilerParams(vmem_limit_bytes=16 * 1024 * 1024),
        cost_estimate=cost(1),
        name="halves",
    )(*a_pieces[1:], *b_pieces[1:], first)
    return [send(parts[0], XS[1]), send(parts[1], XS[3])], [send(parts[2], YS[1]), send(parts[3], YS[3])]


def ring(values, perms):
    return [values] + [send(values, perms[k]) for k in (1, 3, 2)]


BACK = (0, 1, 3, 2)


def copy_all(copies, sems):
    started = [pltpu.make_async_copy(source, target, sems.at[i]) for i, (source, target) in enumerate(copies)]
    for copy in started:
        copy.start()
    for copy in started:
        copy.wait()


def place_near(a_pieces, b_pieces, start, width, first=()):
    def kernel(*refs):
        d = lax.axis_index("dp")
        x, y = d // 16, (d // 2) % 4
        a_whole, b_whole, sems = refs[8 + len(first) :]
        copies = []
        for i, back in enumerate(BACK):
            at_y, at_x = lax.rem(y + 4 - back, 4), lax.rem(x + 4 - back, 4)
            copies.append((refs[i].at[:, :, pl.ds(start, width)], a_whole.at[:, at_y]))
            copies.append((refs[4 + i].at[:, :, pl.ds(start, width)], b_whole.at[at_x]))
        copy_all(copies, sems)

    return pl.pallas_call(
        kernel,
        in_specs=in_vmem(8) + anywhere(len(first)),
        out_specs=in_vmem(2),
        out_shape=[jax.ShapeDtypeStruct(shape, BF) for shape in ((2, 4, 48, width), (4, 2, 48, width))],
        scratch_shapes=[pltpu.SemaphoreType.DMA((8,))],
        compiler_params=pltpu.CompilerParams(vmem_limit_bytes=16 * 1024 * 1024),
        cost_estimate=cost(1.5),
        name="place_near",
    )(*a_pieces, *b_pieces, *first)


def place_far(a_pieces, b_pieces, columns, first=()):
    count = a_pieces[0].shape[-1] // columns

    def kernel(*refs):
        d = lax.axis_index("dp")
        x, y = d // 16, (d // 2) % 4
        whole, sems = refs[10 + len(first) :]
        copies = []
        for i, back in enumerate((0, 1, 3, 2, 2)):
            at_y, at_x = lax.rem(y + 4 - back, 4), lax.rem(x + 4 - back, 4)
            for j in range(count):
                lanes = pl.ds(j * columns, columns)
                z = pl.ds(i - 3, 1) if i > 2 else pl.ds(0, 2)
                xs = pl.ds(2 * (i - 3), 2) if i > 2 else pl.ds(0, 4)
                copies.append((refs[i].at[:, :, :, lanes], whole.at[j, at_x, z]))
                copies.append((refs[5 + i].at[:, :, :, lanes], whole.at[count + j, xs, :, at_y]))
        copy_all(copies, sems)

    return pl.pallas_call(
        kernel,
        in_specs=in_vmem(10) + anywhere(len(first)),
        out_specs=pl.BlockSpec(memory_space=pltpu.VMEM),
        out_shape=jax.ShapeDtypeStruct((2 * count, 4, 2, 4, 48, columns), BF),
        scratch_shapes=[pltpu.SemaphoreType.DMA((10 * count,))],
        compiler_params=pltpu.CompilerParams(vmem_limit_bytes=24 * 1024 * 1024),
        cost_estimate=cost(2),
        name="place_far",
    )(*a_pieces, *b_pieces, *first).reshape(2 * count, 1536, columns)


def pack_kernel(in_weight, bc_weight, step_weight, out_weight, mine, other):
    c = lax.rem(lax.axis_index("dp"), 2)
    out_rows = out_weight[...].T
    steps = step_weight[...]
    for target, half in ((mine, c), (other, 1 - c)):
        at = pl.multiple_of(half * 768, 128)
        target[:, 0:512] = in_weight[1, :, pl.ds(at, 512)]
        target[:, 512:1280] = in_weight[0, :, pl.ds(at, 768)]
        target[:, 1280:1536] = in_weight[1, :, pl.ds(pl.multiple_of(at + 512, 128), 256)]
        target[:, 1536:1664] = bc_weight[:, pl.ds(pl.multiple_of(half * 128, 128), 128)]
        second = jnp.full((24, 12), half) == 1
        own = jnp.where(second, steps[:, 12:].astype(F32), steps[:, :12].astype(F32))
        gap = jnp.zeros((24, 4), F32)
        parts = [own[:, 0:4], gap, own[:, 4:8], gap, own[:, 8:12], jnp.zeros((24, 108), F32)]
        target[:, 1664:1792] = jnp.concatenate(parts, 1).astype(BF)
        wanted = jnp.full((24, 768), half) == 1
        pieces = (out_rows[:, 768:].astype(F32), out_rows[:, :768].astype(F32))
        target[:, 1792:2560] = jnp.where(wanted, *pieces).astype(BF)


def pack(in_weight, bc_weight, step_weight, out_weight):
    return pl.pallas_call(
        pack_kernel,
        in_specs=in_vmem(4),
        out_specs=in_vmem(2),
        out_shape=[jax.ShapeDtypeStruct((24, 2560), BF)] * 2,
        compiler_params=pltpu.CompilerParams(vmem_limit_bytes=16 * 1024 * 1024),
        cost_estimate=cost(1.5),
        name="pack",
    )(in_weight, bc_weight, step_weight, out_weight)


def pair_rows(mine, other, c):
    got = send(other, CORE)
    return jnp.concatenate([jnp.where(c == 0, mine, got), jnp.where(c == 0, got, mine)], 0)


def pair_planes(rows, z):
    other = send(rows, ZHI)
    return jnp.stack([jnp.where(z == 0, rows, other), jnp.where(z == 0, other, rows)], 0)


def here():
    d = lax.axis_index("dp")
    return d // 16, (d // 2) % 4


def ahead(at, k):
    return lax.rem(at + k, 4)


def pieces_kernel(by_x, own, widths, left, *refs):
    rights, refs = refs[: len(widths)], refs[len(widths) :]
    got = refs[0] if own else None
    outs = refs[1:6] if own else refs[:1]
    x, y = here()
    right = jnp.concatenate([r[:, a:b] if len(r.shape) == 2 else r[a] for r, (a, b) in zip(rights, widths)], 1)

    def write(k, part, values):
        if not own:
            outs[0][(k, *part)] = values.astype(BF)
            return
        values = values + got[(k, *part)].astype(F32)
        if k == 2 and by_x:
            outs[3][...] = values[:192].astype(BF)
            outs[4][...] = values[192:].astype(BF)
        elif k == 2:
            outs[3 + part[0] // 2][part[0] % 2, part[1]] = values.astype(BF)
        else:
            outs[(0, 1, None, 2)[k]][part or Ellipsis] = values

    if by_x:
        for k in range(4):
            rows = pl.ds(pl.multiple_of(ahead(x, k) * 384, 128), 384)
            write(k, (), dot_rows(left[:, rows], right))
    else:
        whole = refs[-1]
        for i in range(4):
            whole[i] = dot_rows(left[:, i * 384 : (i + 1) * 384], right)
        for k in range(4):
            for i in range(4):
                for z in range(2):
                    rows = pl.ds(pl.multiple_of((z * 4 + ahead(y, k)) * 48, 16), 48)
                    write(k, (i, z), whole[i, rows, :])


def weight_pieces(by_x, left, rights, widths, got=(), first=()):
    width = sum(b - a if r.ndim == 2 else b for r, (a, b) in zip(rights, widths))
    shape = (384, width) if by_x else (4, 2, 48, width)
    if got:
        near, far = near_core(shape, F32), near_core((shape[0] // 2, *shape[1:]), BF)
        outs = [near] * 3 + [far] * 2
    else:
        outs = jax.ShapeDtypeStruct((4, *shape), BF)
    count = 1 + len(rights) + len(got)

    def kernel(*refs):
        pieces_kernel(by_x, bool(got), widths, *refs[:count], *refs[count + len(first) :])

    return pl.pallas_call(
        kernel,
        in_specs=in_vmem(count) + anywhere(len(first)),
        out_specs=in_vmem(5) if got else in_vmem(1)[0],
        out_shape=outs,
        scratch_shapes=[] if by_x else [pltpu.VMEM((4, 384, width), F32)],
        compiler_params=pltpu.CompilerParams(vmem_limit_bytes=24 * 1024 * 1024),
        cost_estimate=cost(2),
        name="weight_pieces",
    )(left, *rights, *got, *first)


def pass_kernel(plus, minus, left, right, *refs):
    on, back = refs[-2:]
    half = left.shape[0]
    on[:half] = (plus[:half] + left[...].astype(F32)).astype(BF)
    on[half:] = plus[half:].astype(BF)
    back[:half] = minus[:half].astype(BF)
    back[half:] = (minus[half:] + right[...].astype(F32)).astype(BF)


def pass_on(by_x, pieces, *first):
    perms = XS if by_x else YS
    left, right = send(pieces[3], perms[1]), send(pieces[4], perms[3])
    shape = near_core(pieces[1].shape, BF)
    return pl.pallas_call(
        pass_kernel,
        in_specs=in_vmem(4) + anywhere(len(first)),
        out_specs=in_vmem(2),
        out_shape=[shape, shape],
        compiler_params=pltpu.CompilerParams(vmem_limit_bytes=16 * 1024 * 1024),
        cost_estimate=cost(1),
        name="pass_on",
    )(pieces[1], pieces[2], left, right, *first)


def near_sum_kernel(by_x, own, one, two, *outs):
    outs = outs[-5:]
    x, y = here()
    total = own[...] + one[...].astype(F32) + two[...].astype(F32)
    whole = outs[4]
    whole[...] = total.reshape(whole.shape)
    for k in range(4):
        if by_x:
            for z in range(2):
                outs[k][z] = whole[z, ahead(y, k)].astype(outs[k].dtype)
        else:
            outs[k][...] = whole[ahead(x, k)].astype(outs[k].dtype)


def near_sum(by_x, own, got, first):
    width = own.shape[-1]
    shape = (2, 48, width)
    return pl.pallas_call(
        lambda *refs: near_sum_kernel(by_x, *refs),
        in_specs=in_vmem(3) + anywhere(len(first)),
        out_specs=in_vmem(4),
        out_shape=[near_core(shape, F32)] + [near_core(shape, BF)] * 3,
        scratch_shapes=[pltpu.VMEM((2, 4, 48, width) if by_x else (4, 2, 48, width), F32)],
        compiler_params=pltpu.CompilerParams(vmem_limit_bytes=16 * 1024 * 1024),
        cost_estimate=cost(1),
        name="near_sum",
    )(own, *got, *first)


def scatter_near(by_x, pieces, passed, *first):
    near = XS if by_x else YS
    return near_sum(by_x, pieces[0], [send(passed[0], near[1]), send(passed[1], near[3])], first)


def send_far(by_x, pieces):
    far = YS if by_x else XS
    return [send(pieces[k], far[k]) for k in (1, 2, 3)]


def sum_far(pieces, got):
    got = [values.astype(F32) for values in got]
    return pieces[0] + got[1] + (got[0] + got[2])


def plane_other(values, z):
    return send(lax.dynamic_index_in_dim(values, 1 - z, 0, keepdims=False).astype(BF), ZHI)


def plane_sum(values, other, z):
    return lax.dynamic_index_in_dim(values, z, 0, keepdims=False) + other.astype(F32)


def rows_kernel(first, rest, got, grad_in, grad_bc, grad_step, grad_out):
    c = lax.rem(lax.axis_index("dp"), 2)
    rows = pl.ds(pl.multiple_of(c * 24, 8), 24)

    def halves(values, start, width):
        mine = values[rows, start : start + width]
        other = got[:, (0 if values is first else 1024) + start : (0 if values is first else 1024) + start + width]
        flag = jnp.full((24, width), c) == 0
        return jnp.where(flag, mine, other), jnp.where(flag, other, mine)

    for i, (values, start) in enumerate(((rest, 0), (first, 0))):
        grad_in[i, :, :768], grad_in[i, :, 768:] = halves(values, start, 768)
    grad_bc[:, :TILE], grad_bc[:, TILE:] = halves(first, 768, TILE)
    for half, values in enumerate(halves(first, 896, TILE)):
        for group in range(3):
            grad_step[:, half * 12 + group * 4 : half * 12 + group * 4 + 4] = values[:, group * 8 : group * 8 + 4]
    grad_out[:768, :], grad_out[768:, :] = [values.T for values in halves(rest, 768, 768)]


def weight_rows(first, rest):
    c = lax.axis_index("dp") % 2
    both = jnp.concatenate([lax.dynamic_slice_in_dim(v, (1 - c) * 24, 24, 0) for v in (first, rest)], 1)
    shapes = [(2, 24, 1536), (24, 256), (24, 24), (1536, 24)]
    return pl.pallas_call(
        rows_kernel,
        in_specs=in_vmem(3),
        out_specs=in_vmem(4),
        out_shape=[jax.ShapeDtypeStruct(shape, F32) for shape in shapes],
        compiler_params=pltpu.CompilerParams(vmem_limit_bytes=16 * 1024 * 1024),
        cost_estimate=cost(1.5),
        name="weight_rows",
    )(first, rest, send(both, CORE))


def around(values, perms):
    got = [send(values, perms[k]) for k in (1, 2, 3)]
    return (values + got[1]) + (got[0] + got[2])


def dot(left, right):
    return jnp.dot(left, right, preferred_element_type=F32)


def dot_rows(left, right):
    return lax.dot_general(left, right, (((0,), (0,)), ((), ())), preferred_element_type=F32)


def dot_cols(left, right):
    return lax.dot_general(left, right, (((1,), (1,)), ((), ())), preferred_element_type=F32)


def silu_slope(values):
    sig = jax.nn.sigmoid(values)
    return sig * (1.0 + values * (1.0 - sig))


def down(values, offset):
    return values if offset == 0 else pltpu.roll(values, offset, 0)


def up(values, offset):
    return values if offset == 0 else pltpu.roll(values, values.shape[0] - offset, 0)


def conv_of(pre, taps, bias, masks):
    out = bias + taps[3:4] * pre
    for offset in (1, 2, 3):
        out = out + taps[3 - offset : 4 - offset] * (down(pre, offset) * masks[:, offset : offset + 1])
    return out


def lane_halves(values):
    low = lax.broadcasted_iota(jnp.int32, (1, TILE), 1) < 64
    zero = jnp.zeros_like(values)
    return jnp.where(low, values, zero), jnp.where(low, zero, values)


def params(mebibytes):
    return pltpu.CompilerParams(dimension_semantics=("arbitrary",), vmem_limit_bytes=mebibytes * 1024 * 1024)


def full(*shape):
    return pl.BlockSpec(shape, lambda i: (0,) * len(shape), pipeline_mode=pl.Buffered(1))


def out_full(*shape):
    return pl.BlockSpec(shape, lambda i: (0,) * len(shape))


def block(count):
    return pl.BlockSpec((count, BLOCK), lambda i: (0, i))


WIDE = 384


def wide(count):
    return pl.BlockSpec((count, WIDE), lambda i: (0, i))


def running(values):
    row = lax.broadcasted_iota(jnp.int32, values.shape, 0)
    offset = 1
    while offset < values.shape[0]:
        values = values + jnp.where(row >= offset, pltpu.roll(values, offset, 0), 0.0)
        offset *= 2
    return values


def visible_of(seg_col, seg_row, later_rows):
    row = lax.broadcasted_iota(jnp.int32, (LEN, LEN), 0)
    col = lax.broadcasted_iota(jnp.int32, (LEN, LEN), 1)
    ordered = (row <= col) if later_rows else (row >= col)
    return ordered & (seg_col[...] == seg_row[...])


def prep_kernel(normed, tail_own, tail_peer, seg_col, seg_row, masks, taps, bias, heads, bc_w, scores, scores_t, act, pre, cols, rows, steps):
    bc_w[0] = tail_own[0, :, :TILE]
    bc_w[1] = tail_peer[0, :, :TILE]
    own = dot(normed[...], tail_own[0])
    peer = dot(normed[...], tail_peer[0])
    core0 = jnp.full((LEN, TILE), lax.rem(lax.axis_index("dp"), 2)) == 0
    pre[:, :TILE] = jnp.where(core0, own[:, :TILE], peer[:, :TILE])
    pre[:, TILE:] = jnp.where(core0, peer[:, :TILE], own[:, :TILE])
    conv_out = conv_of(pre[...], taps[...], bias[...], masks[...])
    act[...] = (conv_out * jax.nn.sigmoid(conv_out)).astype(BF)
    b_proj, c_proj = act[:, :TILE], act[:, TILE:]
    scores[...] = jnp.where(visible_of(seg_col, seg_row, False), dot_cols(c_proj, b_proj), 0.0)
    scores_t[...] = jnp.where(visible_of(seg_col, seg_row, True), dot_cols(b_proj, c_proj), 0.0)
    step_pre = own[:, TILE:] + pltpu.roll(peer[:, TILE:], 24, 1) + heads[0:1, :]
    step_size = jnp.maximum(step_pre, 0.0) + jnp.log1p(jnp.exp(-jnp.abs(step_pre)))
    sums = running(step_size * heads[1:2, :]) * LOG2E
    logs = jnp.log(step_size) * LOG2E
    steps[0] = step_pre
    steps[1] = step_size
    for i, values in enumerate((sums, sums - logs, logs)):
        cols[i] = values
        rows[i] = values.T


def prepare(normed, inner_own, inner_peer, seg_col, seg_row, masks, taps, bias, heads):
    tail = pl.BlockSpec((1, 1536, 256), lambda i: (3, 0, 0), pipeline_mode=pl.Buffered(1))
    shapes = [
        ((2, 1536, TILE), BF),
        ((LEN, LEN), F32),
        ((LEN, LEN), F32),
        ((LEN, 256), BF),
        ((LEN, 256), F32),
        ((3, LEN, TILE), F32),
        ((3, TILE, LEN), F32),
        ((2, LEN, TILE), F32),
    ]
    return pl.pallas_call(
        prep_kernel,
        grid=(1,),
        in_specs=[in_vmem(1)[0], tail, tail, full(LEN, 1), full(1, LEN), full(LEN, 4), full(4, 256), full(1, 256), full(8, TILE)],
        out_specs=in_vmem(len(shapes)),
        out_shape=[(near_core if i in (1, 5, 6) else outside)(shape, kind) for i, (shape, kind) in enumerate(shapes)],
        compiler_params=params(24),
        cost_estimate=cost(2),
        name="prepare",
    )(normed, inner_own, inner_peer, seg_col, seg_row, masks, taps, bias, heads)


def norm_kernel(hidden, cotangent, other, gain, whole, normed, scale, cot):
    first = jnp.full((256, 1536), lax.axis_index("tensor")) == 0
    mine, theirs = hidden[...].astype(F32), other[0:256].astype(F32)
    for part, values in enumerate((jnp.where(first, mine, theirs), jnp.where(first, theirs, mine))):
        rows = slice(part * 256, (part + 1) * 256)
        whole[rows, :] = values.astype(BF)
        inv = lax.rsqrt(jnp.sum(values * values, axis=1, keepdims=True) * (1.0 / 1536.0) + EPS)
        scale[rows, :] = jnp.broadcast_to(inv, (256, TILE))
        normed[rows, :] = (values * inv * gain[...]).astype(BF)
    mine, theirs = cotangent[...].astype(F32), other[256:512].astype(F32)
    cot[0:256, :] = jnp.where(first, mine, theirs).astype(BF)
    cot[256:512, :] = jnp.where(first, theirs, mine).astype(BF)


def norm_of(hidden, cotangent, other, gain):
    whole = near_core((LEN, 1536), BF)
    return pl.pallas_call(
        norm_kernel,
        in_specs=in_vmem(4),
        out_specs=in_vmem(4),
        out_shape=[outside((LEN, 1536), BF), whole, outside((LEN, TILE), F32), whole],
        compiler_params=pltpu.CompilerParams(vmem_limit_bytes=24 * 1024 * 1024),
        cost_estimate=cost(2),
        name="input_norm",
    )(hidden, cotangent, other, gain)


def mix_kernel(half, normed, weight, taps, bias, masks, scores, cols, rows, pre, act, mixed):
    pre[...] = dot(normed[...], weight[0])
    conv_out = conv_of(pre[...], taps[...], bias[...], masks[...])
    act[...] = (conv_out * jax.nn.sigmoid(conv_out)).astype(BF)
    sums_all = pltpu.roll(cols[0], lax.rem(TILE - 24 * half - 8 * pl.program_id(0), TILE), 1)
    for pair in range(2):
        lanes = slice(pair * TILE, (pair + 1) * TILE)
        halves = lane_halves(act[:, lanes])
        for tile in range(4):
            here = slice(tile * TILE, (tile + 1) * TILE)
            weights, values = [], []
            for side in range(2):
                head = 2 * pair + side
                sums = sums_all[here, head : head + 1]
                if tile:
                    decay = jnp.exp2(sums - rows[1, head : head + 1, : tile * TILE])
                    weights.append((scores[here, : tile * TILE] * decay).astype(BF))
                    values.append(halves[side][: tile * TILE])
                decay = jnp.exp2(jnp.minimum(sums - rows[1, head : head + 1, here], rows[2, head : head + 1, here]))
                weights.append((scores[here, here] * decay).astype(BF))
                values.append(halves[side][here])
            mixed[here, lanes] = dot(jnp.concatenate(weights, 1), jnp.concatenate(values, 0))


def third_of(count, half):
    return pl.BlockSpec((count, BLOCK), lambda i: (0, 3 * half + i))


def rows_of(half):
    return pl.BlockSpec((3, 8, LEN), lambda i: (0, 3 * half + i, 0))


def mix_forward(half, normed, weight, taps, bias, masks, scores, cols, rows):
    return pl.pallas_call(
        lambda *refs: mix_kernel(half, *refs),
        grid=(3,),
        in_specs=[
            in_vmem(1)[0],
            pl.BlockSpec((1, 1536, BLOCK), lambda i: (i, 0, 0)),
            third_of(4, half),
            third_of(1, half),
            full(LEN, 4),
            in_vmem(1)[0],
            in_vmem(1)[0],
            rows_of(half),
        ],
        out_specs=[block(LEN)] * 3,
        out_shape=[
            outside((LEN, 768), F32),
            near_core((LEN, 768), BF),
            near_core((LEN, 768), F32),
        ],
        compiler_params=params(24),
        cost_estimate=cost(6.2),
        name="mix_forward",
    )(normed, weight, taps, bias, masks, scores, cols, rows)


def gate_kernel(last, normed, cot, gate_w, out_w, act, mixed, skip, gain, *refs):
    step = pl.program_id(0)
    before = refs[0] if last else None
    gate_pre, grad_gn, stats, squares, dots = refs[last:]

    @pl.when(step == 0)
    def _():
        squares[...] = before[0] if last else jnp.zeros_like(squares)
        dots[...] = before[1] if last else jnp.zeros_like(dots)

    pre = dot(normed[...], gate_w[0])
    upper = dot(cot[...], out_w[0])
    gate_pre[...] = pre
    grad_gn[...] = upper
    mixer_y = mixed[...] + skip[...] * act[...].astype(F32)
    gated = mixer_y * (pre * jax.nn.sigmoid(pre))
    square = gated * gated
    product = upper * gain[...] * gated
    squares[...] += square[:, :TILE] + square[:, TILE : 2 * TILE] + square[:, 2 * TILE :]
    dots[...] += product[:, :TILE] + product[:, TILE : 2 * TILE] + product[:, 2 * TILE :]

    @pl.when(step == 1)
    def _():
        if last:
            stats[0:1, :] = jnp.sum(squares[...].T, axis=0, keepdims=True)
            stats[1:2, :] = jnp.sum(dots[...].T, axis=0, keepdims=True)
            stats[2:8, :] = jnp.zeros((6, LEN), F32)
        else:
            stats[0] = squares[...]
            stats[1] = dots[...]


def half_of(count, half):
    return pl.BlockSpec((count, WIDE), lambda i: (0, 2 * half + i))


def gate_forward(half, normed, cot, rest, act, mixed, skip, gain, before=()):
    weight = lambda part: pl.BlockSpec((1, 1536, WIDE), lambda i: (2 * part + i, 0, 0))
    stats = (8, LEN) if half else (2, LEN, TILE)
    kept = near_core
    return pl.pallas_call(
        lambda *refs: gate_kernel(half, *refs),
        grid=(2,),
        in_specs=[
            *in_vmem(2),
            weight(0),
            weight(1),
            wide(LEN),
            wide(LEN),
            half_of(1, half),
            half_of(1, half),
        ]
        + [full(2, LEN, TILE)] * half,
        out_specs=[wide(LEN), wide(LEN), out_full(*stats)],
        out_shape=[
            kept((LEN, 768), F32),
            kept((LEN, 768), F32),
            jax.ShapeDtypeStruct(stats, F32),
        ],
        scratch_shapes=[pltpu.VMEM((LEN, TILE), F32)] * 2,
        compiler_params=params(24),
        cost_estimate=cost(4.2),
        name="gate_forward",
    )(normed, cot, rest, rest, act, mixed, skip, gain, *before)


def slope_kernel(stats, others, *refs):
    peer_in, own_in, skip, gain, normed, cot = refs[0:4], refs[4:8], *refs[8:12]
    peer_out, own_out, gain_grad = refs[12:15], refs[15:18], refs[18]
    part_gate, part_out, scale, dots, whole = refs[19:]
    step = pl.program_id(0)

    @pl.when(step == 0)
    def _():
        inv = lax.rsqrt((stats[0:1, :] + others[0:1, :]) * (1.0 / 3072.0) + EPS)
        both = (stats[1:2, :] + others[1:2, :]) * (1.0 / 3072.0)
        scale[...] = jnp.broadcast_to(inv, (TILE, LEN)).T
        dots[...] = jnp.broadcast_to(inv * inv * inv * both, (TILE, LEN)).T

    def slopes(gate_pre, grad_gn, act, mixed, grad_y, gate_low, gnormed):
        for part in range(3):
            lanes = slice(part * TILE, (part + 1) * TILE)
            q = scale[...]
            pre = gate_pre[:, lanes]
            sig = jax.nn.sigmoid(pre)
            gate_act = pre * sig
            mixer_y = mixed[:, lanes] + skip[:, lanes] * act[:, lanes].astype(F32)
            gated = mixer_y * gate_act
            scaled = gated * q
            gnormed[:, lanes] = (scaled * gain[:, lanes]).astype(BF)
            upper = grad_gn[:, lanes]
            gain_grad[:, lanes] = jnp.sum(upper * scaled, axis=0, keepdims=True)
            grad_gated = q * gain[:, lanes] * upper - gated * dots[...]
            grad_y[:, lanes] = grad_gated * gate_act
            gate_low[:, lanes] = (grad_gated * mixer_y * (sig * (1.0 + pre * (1.0 - sig)))).astype(BF)

    @pl.when(step >= 2)
    def _():
        slopes(*own_in, *own_out)

    @pl.when(step < 2)
    def _():
        slopes(*peer_in, *peer_out)
        x, y = here()
        for k in range(4):
            rows = pl.ds(pl.multiple_of(ahead(x, k) * 384, 128), 384)
            part_gate[k] = dot_rows(normed[:, rows], peer_out[1][...]).astype(BF)
        for i in range(4):
            whole[...] = dot_rows(cot[:, i * 384 : (i + 1) * 384], peer_out[2][...])
            for k in range(4):
                for z in range(2):
                    rows = pl.ds(pl.multiple_of((z * 4 + ahead(y, k)) * 48, 16), 48)
                    part_out[k, i, z] = whole[rows, :].astype(BF)


def gate_backward(stats, others, peer, own, skip, gain, normed, cot):
    early, late = lambda i: jnp.minimum(i, 1), lambda i: jnp.maximum(i - 2, 0)
    early_block, late_block = [pl.BlockSpec((LEN, WIDE), lambda i, at=at: (0, at(i))) for at in (early, late)]
    turned = pl.BlockSpec((1, WIDE), lambda i: (0, (i + 2) % 4))
    low, full_y = outside((LEN, 768), BF), outside((LEN, 768), F32)
    return pl.pallas_call(
        slope_kernel,
        grid=(4,),
        in_specs=[full(8, LEN), full(8, LEN)] + [early_block] * 4 + [late_block] * 4 + [turned] * 2 + in_vmem(2),
        out_specs=[early_block] * 3
        + [late_block] * 3
        + [
            turned,
            pl.BlockSpec((4, 384, WIDE), lambda i: (0, 0, early(i))),
            pl.BlockSpec((4, 4, 2, 48, WIDE), lambda i: (0, 0, 0, 0, early(i))),
        ],
        out_shape=[full_y, low, low] * 2
        + [
            jax.ShapeDtypeStruct((1, 1536), F32),
            jax.ShapeDtypeStruct((4, 384, 768), BF),
            jax.ShapeDtypeStruct((4, 4, 2, 48, 768), BF),
        ],
        scratch_shapes=[pltpu.VMEM((LEN, TILE), F32)] * 2 + [pltpu.VMEM((384, WIDE), F32)],
        compiler_params=params(28),
        cost_estimate=cost(10),
        name="gate_backward",
    )(stats, others, *peer, *own, skip, gain, normed, cot)


def product_kernel(own, peer, weight_own, weight_peer, *refs):
    target, total = refs[-2:]
    step = pl.program_id(0)
    for test, left, weight in ((step < 2, own, weight_own), (step >= 2, peer, weight_peer)):

        @pl.when(test)
        def _(left=left, weight=weight):
            part = dot_cols(left[...], weight[0])

            @pl.when(step == 0)
            def _():
                total[...] = part

            @pl.when(step > 0)
            def _():
                total[...] += part

    @pl.when(step == 3)
    def _():
        target[...] = total[...].astype(target.dtype)


def product(own, peer, rest_own, rest_peer, kind, target, *first):
    early = lambda i: jnp.minimum(i, 1)
    late = lambda i: jnp.maximum(i - 2, 0)
    return pl.pallas_call(
        product_kernel,
        grid=(4,),
        in_specs=[
            pl.BlockSpec((LEN, WIDE), lambda i: (0, early(i))),
            pl.BlockSpec((LEN, WIDE), lambda i: (0, late(i))),
            pl.BlockSpec((1, 1536, WIDE), lambda i: (2 * kind + early(i), 0, 0)),
            pl.BlockSpec((1, 1536, WIDE), lambda i: (2 * kind + late(i), 0, 0)),
        ]
        + anywhere(len(first)),
        out_specs=in_vmem(1)[0],
        out_shape=jax.ShapeDtypeStruct((LEN, 1536), target),
        scratch_shapes=[pltpu.VMEM((LEN, 1536), F32)],
        compiler_params=params(24),
        cost_estimate=cost(4),
        name="product",
    )(far_off(own), far_off(peer), far_off(rest_own), far_off(rest_peer), *first)


SEEN = [(j, i) for j in range(4) for i in range(j, 4)]


def back_kernel(half, grad_y, act, mixed, pre, scores, taps, bias, masks, cols, rows, skip, *refs):
    step = pl.program_id(0)
    if half:
        inner_low, sums, flows, grad_scores, grad_act = refs[-5:]
    else:
        flows_0, scores_0 = refs[:2]
        inner_low, sums, flows, grad_scores, scores_low, grad_act = refs[-6:]

    @pl.when(step == 0)
    def _():
        grad_scores[...] = jnp.zeros_like(grad_scores) if half else scores_0[...]
        flows[...] = jnp.zeros_like(flows) if half else flows_0[...]

    turn = lax.rem(TILE - 24 * half - 8 * step, TILE)
    back_all, most_all = pltpu.roll(cols[1], turn, 1), pltpu.roll(cols[2], turn, 1)

    pairs = []
    for pair in range(2):
        lanes = slice(pair * TILE, (pair + 1) * TILE)
        low = grad_y[:, lanes].astype(BF)
        pairs.append((lane_halves(act[:, lanes]), low, lane_halves(low)))
    for tile in range(4):
        here = slice(tile * TILE, (tile + 1) * TILE)
        after = slice((tile + 1) * TILE, LEN)
        add_diag, add_rest = 0.0, 0.0
        for pair in range(2):
            act_halves, low, low_halves = pairs[pair]
            weights, values = [], []
            stacked = jnp.concatenate([act_halves[0][here], act_halves[1][here]], 0)
            grad_w = dot_cols(stacked, low[tile * TILE :])
            for side in range(2):
                head = 2 * pair + side
                back = back_all[here, head : head + 1]
                most = most_all[here, head : head + 1]
                own = slice(side * TILE, (side + 1) * TILE)
                decay = jnp.exp2(jnp.minimum(rows[0, head : head + 1, here] - back, most))
                add_diag = add_diag + grad_w[own, :TILE] * decay
                weights.append((scores[here, here] * decay).astype(BF))
                values.append(low_halves[side][here])
                if tile < 3:
                    decay = jnp.exp2(rows[0, head : head + 1, after] - back)
                    add_rest = add_rest + grad_w[own, TILE:] * decay
                    weights.append((scores[here, after] * decay).astype(BF))
                    values.append(low_halves[side][after])
            lanes = slice(pair * TILE, (pair + 1) * TILE)
            grad_act[here, lanes] = dot(jnp.concatenate(weights, 1), jnp.concatenate(values, 0))
        grad_scores[here, here] += add_diag
        if tile < 3:
            grad_scores[here, after] += add_rest

    if not half:

        @pl.when(step == 2)
        def _():
            for at, (j, i) in enumerate(SEEN):
                rows_j, cols_i = slice(j * TILE, (j + 1) * TILE), slice(i * TILE, (i + 1) * TILE)
                scores_low[at] = grad_scores[rows_j, cols_i].astype(BF)

    lane = lax.broadcasted_iota(jnp.int32, (1, TILE), 1)
    row_flows, col_flows = 0.0, 0.0

    low_lane = lax.broadcasted_iota(jnp.int32, (1, TILE), 1) < 64
    for pair in range(2):
        lanes = slice(pair * TILE, (pair + 1) * TILE)
        values = act[:, lanes].astype(F32)
        grad = grad_y[:, lanes]
        row_flow = grad.astype(BF).astype(F32) * mixed[:, lanes]
        col_flow = values * grad_act[:, lanes]
        for side, mask in ((0, low_lane), (1, ~low_lane)):
            head = 2 * pair + side
            here = lane == 24 * half + 8 * step + head
            row_flows += jnp.where(here, jnp.sum(jnp.where(mask, row_flow, 0.0), axis=1, keepdims=True), 0.0)
            col_flows += jnp.where(here, jnp.sum(jnp.where(mask, col_flow, 0.0), axis=1, keepdims=True), 0.0)
        taps_l, masks_v = taps[:, lanes], masks[...]
        pre_l = pre[:, lanes]
        conv_out = conv_of(pre_l, taps_l, bias[:, lanes], masks_v)
        grad_conv = (grad_act[:, lanes] + skip[:, lanes] * grad) * silu_slope(conv_out)
        grad_pre = taps_l[3:4] * grad_conv
        sums[3:4, lanes] = jnp.sum(grad_conv * pre_l, axis=0, keepdims=True)
        for offset in (1, 2, 3):
            masked = grad_conv * masks_v[:, offset : offset + 1]
            tap = 3 - offset
            sums[tap : tap + 1, lanes] = jnp.sum(masked * down(pre_l, offset), axis=0, keepdims=True)
            grad_pre = grad_pre + taps_l[tap : tap + 1] * up(masked, offset)
        sums[4:5, lanes] = jnp.sum(grad_conv, axis=0, keepdims=True)
        sums[5:6, lanes] = jnp.sum(grad * values, axis=0, keepdims=True)
        sums[6:8, lanes] = jnp.zeros((2, TILE), F32)
        inner_low[:, lanes] = grad_pre.astype(BF)
    flows[0] += row_flows
    flows[1] += col_flows


def mix_backward(half, grad_y, act, mixed, pre, scores_t, taps, bias, masks, cols, rows, skip, before=(), first=()):
    low = [] if half else [jax.ShapeDtypeStruct((10, TILE, TILE), BF)]
    return pl.pallas_call(
        lambda *refs: back_kernel(half, *refs),
        grid=(3,),
        in_specs=[
            block(LEN),
            block(LEN),
            block(LEN),
            block(LEN),
            in_vmem(1)[0],
            third_of(4, half),
            third_of(1, half),
            full(LEN, 4),
            in_vmem(1)[0],
            rows_of(half),
            third_of(1, half),
            *in_vmem(len(before)),
            *anywhere(len(first)),
        ],
        out_specs=[block(LEN), block(8), *in_vmem(2 + len(low))],
        out_shape=[
            near_core((LEN, 768), BF),
            jax.ShapeDtypeStruct((8, 768), F32),
            near_core((2, LEN, TILE), F32),
            near_core((LEN, LEN), F32),
        ]
        + low,
        scratch_shapes=[pltpu.VMEM((LEN, BLOCK), F32)],
        compiler_params=params(24),
        cost_estimate=cost(9.8),
        name="mix_backward",
    )(grad_y, act, mixed, pre, scores_t, taps, bias, masks, cols, rows, skip, *before, *first)


def tail_kernel(mine, other, act, pre, seg_col, seg_row, masks, taps, bias, shares, *refs):
    tails, bc_sums, both = refs[-3:]
    seen = visible_of(seg_col, seg_row, True)
    for at, (j, i) in enumerate(SEEN):
        tile = (slice(j * TILE, (j + 1) * TILE), slice(i * TILE, (i + 1) * TILE))
        both[tile] = mine[tile] + other[at].astype(F32)
        if i > j:
            both[tile[1], tile[0]] = jnp.zeros((TILE, TILE), F32)
    low = jnp.where(seen, both[...], 0.0).astype(BF)
    b_proj, c_proj = act[:, :TILE], act[:, TILE:]
    core0 = jnp.full((LEN, TILE), lax.rem(lax.axis_index("dp"), 2)) == 0
    bc_low = []
    for part, grad in ((0, dot(low, c_proj)), (1, dot_rows(low, b_proj))):
        lanes = slice(part * TILE, (part + 1) * TILE)
        taps_l, pre_l, masks_v = taps[:, lanes], pre[:, lanes], masks[...]
        grad_conv = grad * silu_slope(conv_of(pre_l, taps_l, bias[:, lanes], masks_v))
        grad_pre = taps_l[3:4] * grad_conv
        bc_sums[3:4, lanes] = jnp.sum(grad_conv * pre_l, axis=0, keepdims=True)
        for offset in (1, 2, 3):
            masked = grad_conv * masks_v[:, offset : offset + 1]
            tap = 3 - offset
            bc_sums[tap : tap + 1, lanes] = jnp.sum(masked * down(pre_l, offset), axis=0, keepdims=True)
            grad_pre = grad_pre + taps_l[tap : tap + 1] * up(masked, offset)
        bc_sums[4:5, lanes] = jnp.sum(grad_conv, axis=0, keepdims=True)
        bc_sums[5:8, lanes] = jnp.zeros((3, TILE), F32)
        bc_low.append(grad_pre)
    for part, bc in ((0, jnp.where(core0, bc_low[0], bc_low[1])), (1, jnp.where(core0, bc_low[1], bc_low[0]))):
        tails[part, :, :TILE] = bc.astype(BF)
        tails[part, :, TILE:] = shares[part, :, TILE:]


def step_kernel(heads, steps, flows, shares, head_sums):
    step_pre, step_size, rate = steps[0], steps[1], heads[1:2, :]
    change = flows[0] - flows[1]
    before = running(change)
    grad_rate = before[LEN - 1 : LEN, :] - before + change
    sig = jax.nn.sigmoid(step_pre)
    tiny = step_size < 1e-30
    ratio = jnp.where(tiny, 1.0, sig / jnp.where(tiny, 1.0, step_size))
    grad_pre = flows[1] * ratio + grad_rate * rate * sig
    head_sums[0:1, :] = jnp.sum(grad_pre, axis=0, keepdims=True)
    head_sums[1:2, :] = jnp.sum(grad_rate * step_size, axis=0, keepdims=True) * rate
    head_sums[2:8, :] = jnp.zeros((6, TILE), F32)
    own_lane = lax.broadcasted_iota(jnp.int32, (LEN, TILE), 1) < 24
    for part, grad in ((0, grad_pre), (1, pltpu.roll(grad_pre, TILE - 24, 1))):
        shares[part, :, :TILE] = jnp.zeros((LEN, TILE), BF)
        shares[part, :, TILE:] = jnp.where(own_lane, grad, 0.0).astype(BF)


def step_backward(heads, steps, flows):
    return pl.pallas_call(
        step_kernel,
        in_specs=in_vmem(3),
        out_specs=in_vmem(2),
        out_shape=[near_core((2, LEN, 256), BF), jax.ShapeDtypeStruct((8, TILE), F32)],
        compiler_params=pltpu.CompilerParams(vmem_limit_bytes=12 * 1024 * 1024),
        cost_estimate=cost(1),
        name="step_backward",
    )(heads, steps, flows)


def tail_backward(mine, other, act, pre, seg_col, seg_row, masks, taps, bias, shares, *first):
    shapes = [((2, LEN, 256), BF), ((8, 256), F32)]
    return pl.pallas_call(
        tail_kernel,
        in_specs=in_vmem(10) + anywhere(len(first)),
        out_specs=in_vmem(len(shapes)),
        out_shape=[near_core(*shapes[0]), jax.ShapeDtypeStruct(*shapes[1])],
        scratch_shapes=[pltpu.VMEM((LEN, LEN), F32)],
        compiler_params=pltpu.CompilerParams(vmem_limit_bytes=18 * 1024 * 1024),
        cost_estimate=cost(2),
        name="tail_backward",
    )(mine, other, act, pre, seg_col, seg_row, masks, taps, bias, shares, *first)


def bc_kernel(tails, weight, hidden, scale, first, part, gain):
    t = lax.axis_index("tensor")
    rows = pl.ds(pl.multiple_of(t * 256, 256), 256)
    values = dot_cols(tails[0, rows, :TILE], weight[0]) + dot_cols(tails[1, rows, :TILE], weight[1])
    part[...] = values
    gain[...] = jnp.sum(values * hidden[...].astype(F32) * scale[rows, :1], axis=0, keepdims=True)


def bc_normed(tails, weight, hidden, scale, first):
    return pl.pallas_call(
        bc_kernel,
        grid=(1,),
        in_specs=[in_vmem(1)[0], full(2, 1536, TILE), full(256, 1536), full(LEN, TILE)] + anywhere(1),
        out_specs=[out_full(256, 1536), out_full(1, 1536)],
        out_shape=[outside((256, 1536), F32), jax.ShapeDtypeStruct((1, 1536), F32)],
        compiler_params=params(16),
        cost_estimate=cost(1.5),
        name="bc_normed",
    )(tails, far_off(weight), far_off(hidden), far_off(scale), first)


def normed_kernel(before, low_own, low_peer, shares, inner_own, inner_peer, resid, scale, *refs):
    low, gain, total = refs[-3:]
    step = pl.program_id(0)

    @pl.when(step == 0)
    def _():
        total[...] = before[...]

    for test, left, weight in (
        (step < 3, low_peer, inner_peer),
        ((step >= 3) & (step < 6), low_own, inner_own),
        (step == 6, shares, inner_own),
        (step == 7, shares, inner_peer),
    ):

        @pl.when(test)
        def _(left=left, weight=weight):
            values = left[0] if left is shares else left[...]
            total[...] += dot_cols(values, weight[0])

    @pl.when(step == 7)
    def _():
        for i in range(3):
            lanes = slice(i * LEN, (i + 1) * LEN)
            values = total[:, lanes]
            low[:, lanes] = values.astype(BF)
            gain[:, lanes] = jnp.sum(values * resid[:, lanes].astype(F32) * scale[:, :1], axis=0, keepdims=True)


def normed_backward(before, low_own, low_peer, shares, inner_own, inner_peer, resid, scale, *first):
    return pl.pallas_call(
        normed_kernel,
        grid=(8,),
        in_specs=[
            in_vmem(1)[0],
            pl.BlockSpec((LEN, BLOCK), lambda i: (0, jnp.clip(i - 3, 0, 2))),
            pl.BlockSpec((LEN, BLOCK), lambda i: (0, jnp.minimum(i, 2))),
            pl.BlockSpec((1, LEN, BLOCK), lambda i: (jnp.clip(i - 6, 0, 1), 0, 0)),
            pl.BlockSpec((1, 1536, BLOCK), lambda i: (jnp.clip(i - 3, 0, 3), 0, 0)),
            pl.BlockSpec((1, 1536, BLOCK), lambda i: (jnp.where(i < 3, i, 3), 0, 0)),
            in_vmem(1)[0],
            full(LEN, TILE),
        ]
        + anywhere(len(first)),
        out_specs=in_vmem(2),
        out_shape=[jax.ShapeDtypeStruct((LEN, 1536), BF), jax.ShapeDtypeStruct((1, 1536), F32)],
        scratch_shapes=[pltpu.VMEM((LEN, 1536), F32)],
        compiler_params=params(24),
        cost_estimate=cost(6),
        name="normed_backward",
    )(before, low_own, low_peer, shares, inner_own, inner_peer, resid, scale, *first)


def hidden_kernel(hidden, cotangent, scale, gain, low, got, bc_part, first, out):
    t = lax.axis_index("tensor")
    rows = pl.ds(pl.multiple_of(t * 256, 256), 256)
    grad = low[rows, :].astype(F32) + got[...].astype(F32) + bc_part[...]
    values = hidden[...].astype(F32)
    scaled = grad * gain[...]
    inv = scale[rows, :1]
    stat = jnp.sum(scaled * values, axis=1, keepdims=True) * (inv * inv * inv * (1.0 / 1536.0))
    out[...] = cotangent[...].astype(F32) + inv * scaled - values * stat


def hidden_grad(hidden, cotangent, scale, gain, low, got, bc_part, first):
    return pl.pallas_call(
        hidden_kernel,
        grid=(1,),
        in_specs=[
            full(256, 1536),
            full(256, 1536),
            full(LEN, TILE),
            full(1, 1536),
            full(LEN, 1536),
            full(256, 1536),
            full(256, 1536),
            pl.BlockSpec(memory_space=pl.ANY),
        ],
        out_specs=out_full(256, 1536),
        out_shape=jax.ShapeDtypeStruct((256, 1536), F32),
        compiler_params=params(20),
        cost_estimate=cost(3),
        name="hidden_grad",
    )(far_off(hidden), far_off(cotangent), far_off(scale), gain, low, got, far_off(bc_part), first)


def precise(left, right):
    return jnp.dot(left, right, preferred_element_type=F32, precision=lax.Precision.HIGHEST)


def small_kernel(sums_own, sums_peer, gain, norm_grad, norm_bc, bc_sums, head_sums, *refs):
    whole = refs[-1]
    core = lax.rem(lax.axis_index("dp"), 2)
    for row, own, peer in (
        (0, sums_own[0:5], sums_peer[0:5]),
        (5, gain[:, :768], gain[:, 768:]),
    ):
        flag = jnp.full(own.shape, core) == 0
        whole[row : row + own.shape[0], :768] = jnp.where(flag, own, peer)
        whole[row : row + own.shape[0], 768:] = jnp.where(flag, peer, own)
    whole[6:7, :] = norm_grad[...] + norm_bc[...]
    for tap in range(5):
        whole[7:8, tap * 256 : (tap + 1) * 256] = bc_sums[tap : tap + 1, :]
    unit = lax.broadcasted_iota(jnp.int32, (768, TILE), 0) // 64
    lane = lax.broadcasted_iota(jnp.int32, (768, TILE), 1)
    spot = (unit // 4) * 8 + unit % 4
    own = precise(sums_own[...], (lane == spot).astype(F32))
    peer = precise(sums_peer[...], (lane == spot + 24).astype(F32))
    heads = head_sums[...]
    rows = (heads[0:1], heads[1:2], (own + peer)[5:6])
    lane = lax.broadcasted_iota(jnp.int32, (1, TILE), 1)
    flag = jnp.full((1, TILE), core) == 0
    step, decay, skip = [
        jnp.where(flag, v, jnp.where(lane < 24, pltpu.roll(v, TILE - 24, 1), pltpu.roll(v, 24, 1))) for v in rows
    ]
    whole[7:8, 1280:1408] = jnp.where(lane < 64, step, pltpu.roll(skip, 64, 1))
    whole[7:8, 1408:1536] = decay


def small_of(*parts):
    shapes = [(8, 768), (8, 768), (1, 1536), (1, 1536), (1, 1536), (8, 256), (8, TILE)]
    return pl.pallas_call(
        small_kernel,
        grid=(1,),
        in_specs=[full(*shape) for shape in shapes] + anywhere(len(parts) - 7),
        out_specs=in_vmem(1)[0],
        out_shape=jax.ShapeDtypeStruct((8, 1536), F32),
        compiler_params=params(8),
        cost_estimate=cost(1),
        name="small_pack",
    )(*parts)


def outputs_kernel(mine, other, conv_grad, bias_grad, gain_grad, norm_grad, heads):
    def halves(rows, width):
        flag = jnp.full(mine[rows, :width].shape, lax.axis_index("tensor")) == 0
        a, b = mine[rows, :width], other[rows, :width]
        return jnp.where(flag, a, b), jnp.where(flag, b, a)

    for rows, target in ((slice(0, 4), conv_grad), (slice(4, 5), bias_grad), (slice(5, 6), gain_grad)):
        low, high = halves(rows, 1536)
        target[:, :1536] = low
        target[:, 1536:3072] = high
    for tap in range(4):
        conv_grad[tap : tap + 1, 3072:] = mine[7:8, tap * 256 : (tap + 1) * 256]
    bias_grad[:, 3072:] = mine[7:8, 1024:1280]
    norm_grad[...] = mine[6:7, :] + other[6:7, :]
    lane = lax.broadcasted_iota(jnp.int32, (TILE, 24), 0)
    head = lax.broadcasted_iota(jnp.int32, (TILE, 24), 1)
    spot = (head // 4) * 8 + head % 4
    for part, at in enumerate((1280, 1408)):
        flag = jnp.full((8, TILE), lax.axis_index("tensor")) == 0
        a, b = mine[:, at : at + TILE], other[:, at : at + TILE]
        for half, values in enumerate((jnp.where(flag, a, b), jnp.where(flag, b, a))):
            lanes = slice(half * 24, half * 24 + 24)
            heads[8 * part : 8 * part + 8, lanes] = precise(values, (lane == spot).astype(F32))
            if not part:
                heads[16:24, lanes] = precise(values, (lane == spot + 64).astype(F32))


def outputs_of(mine, other):
    shapes = [(4, 3328), (1, 3328), (1, 3072), (1, 1536), (24, 48)]
    return pl.pallas_call(
        outputs_kernel,
        in_specs=in_vmem(2),
        out_specs=in_vmem(5),
        out_shape=[jax.ShapeDtypeStruct(shape, F32) for shape in shapes],
        compiler_params=pltpu.CompilerParams(vmem_limit_bytes=16 * 1024 * 1024),
        cost_estimate=cost(1.5),
        name="small_unpack",
    )(mine, other)


def on_device(
    hidden,
    segments,
    norm_gain,
    in_weight,
    bc_weight,
    step_weight,
    conv_weight,
    conv_bias,
    step_bias,
    decay_log,
    skip_gain,
    gate_gain,
    out_weight,
    cotangent,
):
    t = lax.axis_index("tensor")
    d = lax.axis_index("dp")
    spot = (d // 16, (d // 8) % 2, (d // 2) % 4, d % 2)
    c = spot[3]

    def own_first(values, size):
        base = 2 * t * size
        return jnp.concatenate(
            [
                lax.dynamic_slice_in_dim(values, base + c * size, size, values.ndim - 1),
                lax.dynamic_slice_in_dim(values, base + (1 - c) * size, size, values.ndim - 1),
            ],
            values.ndim - 1,
        )

    def in_lanes(values):
        return jnp.pad(jnp.pad(values.reshape(6, 4), ((0, 0), (0, 4))).reshape(48), (0, 80))

    planes = pair_planes(pair_rows(*pack(in_weight, bc_weight, step_weight, out_weight), c), spot[1])
    tokens_other = swap_tensor(after(jnp.concatenate([hidden, cotangent], 0), planes))

    taps = own_first(conv_weight[:, :3072], 768)
    bias = own_first(conv_bias[None, :3072], 768)
    gain = own_first(gate_gain[None, :], 768)
    skip = jnp.repeat(own_first(skip_gain, 12), 64)[None, :]
    heads = jnp.stack(
        [in_lanes(own_first(step_bias, 12)), in_lanes(-jnp.exp(own_first(decay_log, 12)))]
        + [jnp.zeros((TILE,), F32)] * 6
    )
    bc_taps, bc_bias = conv_weight[:, 3072:], conv_bias[None, 3072:]
    seg = segments[0]
    seg_col, seg_row = segments.T, segments
    masks = jnp.stack(
        [(jnp.pad(seg, (o, 0), constant_values=-1)[:LEN] == seg).astype(F32) for o in range(4)], 1
    )

    a_near, b_near = ring(planes[..., :1280], YS), ring(planes[..., 1280:], XS)
    settings = (taps, bias, gain, skip, heads, bc_taps, bc_bias, seg_col, masks)
    a_first, b_first = place_near(a_near, b_near, 0, 512, settings)
    hidden_all, normed, norm_scale, cot_all = norm_of(hidden, cotangent, tokens_other, norm_gain[None])
    a_far, b_far = sides(a_first, XS), sides(b_first, YS)
    a_far, b_far = a_far + opposite(a_far, XS, 0), b_far + opposite(b_far, YS, 0)
    inner_own = place_far(a_far, b_far, 256, (normed,))
    inner_peer = send(inner_own, CORE)
    a_rest, b_rest = place_near(a_near, b_near, 512, 768, (inner_own,))
    a_rest, b_rest = sides(a_rest, XS), sides(b_rest, YS)

    bc_w, scores, scores_t, bc_act, bc_pre, cols, rows, steps = prepare(
        normed, inner_own, inner_peer, seg_col, seg_row, masks, bc_taps, bc_bias, heads
    )
    mixer = (taps, bias, masks, scores, cols, rows)
    pre_own, act_own, mixed_own = mix_forward(0, normed, inner_own, *mixer)
    a_more, b_more = opposites(a_rest, b_rest, act_own)
    a_rest, b_rest = a_rest + a_more, b_rest + b_more
    pre_peer, act_peer, mixed_peer = mix_forward(1, normed, inner_peer, *mixer)
    rest_own = place_far(a_rest, b_rest, WIDE, (act_peer,))
    rest_peer = send(rest_own, CORE)
    gate_own, gn_own, sums_own = gate_forward(0, normed, cot_all, rest_own, act_own, mixed_own, skip, gain)
    gate_peer, gn_peer, stats = gate_forward(1, normed, cot_all, rest_peer, act_peer, mixed_peer, skip, gain, (sums_own,))
    others = swap_tensor(stats)

    def other_tokens(values):
        return swap_tensor(lax.dynamic_slice_in_dim(values, (1 - t) * 256, 256, 0))

    def own_tokens(values, got=None):
        got = other_tokens(values) if got is None else got
        return lax.dynamic_slice_in_dim(values, t * 256, 256, 0).astype(F32) + got.astype(F32)

    (
        grad_y_peer,
        gate_low_peer,
        gnormed_peer,
        grad_y_own,
        gate_low,
        gnormed,
        gain_grad,
        gate_got,
        out_got,
    ) = gate_backward(
        stats,
        others,
        (gate_peer, gn_peer, act_peer, mixed_peer),
        (gate_own, gn_own, act_own, mixed_own),
        skip,
        gain,
        normed,
        cot_all,
    )
    gate_got, out_got = send(gate_got, CORE), send(out_got, CORE)
    branch = product(gnormed, gnormed_peer, rest_own, rest_peer, 1, BF)
    branch_got = other_tokens(branch)
    gate_pieces = weight_pieces(True, normed, (gate_low,), ((0, 768),), (gate_got,), (branch,))
    out_pieces = weight_pieces(False, cot_all, (gnormed,), ((0, 768),), (out_got,), (branch,))
    gate_grads = product(gate_low, gate_low_peer, rest_own, rest_peer, 0, F32, gate_pieces[3], out_pieces[3])
    mixed = (hidden.astype(F32) + own_tokens(branch, branch_got)).astype(BF)
    gate_passed, out_passed = pass_on(True, gate_pieces, gate_grads), pass_on(False, out_pieces, gate_grads)

    mixer = (scores_t, taps, bias, masks, cols, rows, skip)
    inner_peer_low, sums_peer, flows, grad_scores = mix_backward(
        1, grad_y_peer, act_peer, mixed_peer, pre_peer, *mixer, (), (gate_passed[0], out_passed[0])
    )
    a_part = weight_pieces(True, normed, (inner_peer_low,), ((0, 512),))
    a_got = send(a_part, CORE)
    gate_near = scatter_near(True, gate_pieces, gate_passed, a_part)
    out_near = scatter_near(False, out_pieces, out_passed, a_part)
    inner_own_low, sums_own, flows, grad_scores, scores_low = mix_backward(
        0, grad_y_own, act_own, mixed_own, pre_own, *mixer, (flows, grad_scores), (gate_near[1], out_near[1], branch_got)
    )
    scores_other = swap_tensor(scores_low)
    gate_far, out_far = send_far(True, gate_near), send_far(False, out_near)
    a_pieces = weight_pieces(True, normed, (inner_own_low,), ((0, 512),), (a_got,), tuple(gate_far))
    shares, head_sums = step_backward(heads, steps, flows)
    grad_low, norm_grad = normed_backward(
        gate_grads, inner_own_low, inner_peer_low, shares, inner_own, inner_peer, hidden_all, norm_scale, a_pieces[3]
    )
    grad_got = other_tokens(grad_low)
    a_passed = pass_on(True, a_pieces, norm_grad)
    tails, bc_sums = tail_backward(
        grad_scores, scores_other, bc_act, bc_pre, seg_col, seg_row, masks, bc_taps, bc_bias, shares, a_passed[0]
    )
    b_part = weight_pieces(False, normed, (inner_peer_low, tails), ((512, 768), (1, 256)))
    b_got = send(b_part, CORE)
    bc_part, norm_bc = bc_normed(tails, bc_w, hidden, norm_scale, b_part)
    small = small_of(sums_own, sums_peer, gain_grad, norm_grad, norm_bc, bc_sums, head_sums, norm_bc)
    small = small + send(small, CORE)
    b_pieces = weight_pieces(False, normed, (inner_own_low, tails), ((512, 768), (0, 256)), (b_got,), (small,))
    a_near_sum = scatter_near(True, a_pieces, a_passed, b_pieces[3])
    small = around(small, YS)
    b_passed = pass_on(False, b_pieces, a_near_sum[1], small)
    b_near_sum = scatter_near(False, b_pieces, b_passed, grad_got)
    late = b_near_sum[1]
    a_near_sum = [a_near_sum[0]] + [after(piece, b_passed[0]) for piece in a_near_sum[1:]]
    a_far, b_far = send_far(True, a_near_sum), send_far(False, b_near_sum)
    grad_hidden = hidden_grad(hidden, cotangent, norm_scale, norm_gain[None], grad_low, grad_got, bc_part, b_far[2])
    small = around(after(small, late), XS)
    small, small_other = small + send(small, ZHI), swap_tensor(small) + lax.ppermute(small, ("dp", "tensor"), ACROSS)
    rest_parts = jnp.concatenate(
        [sum_far([after(gate_near[0], late)], gate_far), sum_far([after(out_near[0], late)], out_far)], 2
    )
    rest_other = plane_other(rest_parts, spot[1])
    first_parts = jnp.concatenate([sum_far(a_near_sum, a_far), sum_far(b_near_sum, b_far)], 2)
    first_total = plane_sum(first_parts, plane_other(first_parts, spot[1]), spot[1])
    rest_total = plane_sum(rest_parts, rest_other, spot[1])
    grad_in, grad_bc, grad_step, grad_out = weight_rows(first_total, rest_total)
    conv_grad, bias_grad, gate_gain_grad, norm_gain_grad, head_grads = outputs_of(small, small_other)
    return (
        mixed,
        grad_hidden,
        norm_gain_grad[0],
        grad_in,
        grad_bc,
        grad_step,
        conv_grad,
        bias_grad[0],
        head_grads[7],
        head_grads[15],
        head_grads[23],
        gate_gain_grad[0],
        grad_out,
    )


def solution(mesh):
    return jax.shard_map(
        on_device,
        mesh=mesh,
        in_specs=(
            P(("dp", "tensor"), None),
            P("dp", None),
            P(),
            P(None, "dp", "tensor"),
            P("dp", None),
            P("dp", "tensor"),
            P(),
            P(),
            P(),
            P(),
            P(),
            P(),
            P("tensor", "dp"),
            P(("dp", "tensor"), None),
        ),
        out_specs=(
            P(("dp", "tensor"), None),
            P(("dp", "tensor"), None),
            P(),
            P(None, "dp", "tensor"),
            P("dp", None),
            P("dp", "tensor"),
            P(),
            P(),
            P(),
            P(),
            P(),
            P(),
            P("tensor", "dp"),
        ),
        check_vma=False,
    )
```

```python
import jax
import jax.numpy as jnp
from jax import lax
from jax.experimental import pallas as pl
from jax.experimental.pallas import tpu as pltpu
from jax.sharding import PartitionSpec as P

EPS = 1e-05
LOG2E = 1.4426950408889634
BF = jnp.bfloat16
F32 = jnp.float32
LEN = 512
TILE = 128
BLOCK = 256


def cost(us):
    return pl.CostEstimate(flops=int(us * 1.0 * 1e9), bytes_accessed=int(us * 1.0 * 2.5e6), transcendentals=0)


SWAP = [(0, 1), (1, 0)]


def dp_index(x, z, y, c):
    return ((x * 2 + z) * 4 + y) * 2 + c


def dp_pairs(move):
    return [
        (dp_index(x, z, y, c), dp_index(*move(x, z, y, c)))
        for x in range(4)
        for z in range(2)
        for y in range(4)
        for c in range(2)
    ]


CORE = dp_pairs(lambda x, z, y, c: (x, z, y, 1 - c))
ACROSS = [
    (2 * dp_index(x, z, y, c) + t, 2 * dp_index(x, 1 - z, y, c) + 1 - t)
    for x in range(4)
    for z in range(2)
    for y in range(4)
    for c in range(2)
    for t in range(2)
]
ZHI = dp_pairs(lambda x, z, y, c: (x, 1 - z, y, c))
XS = {k: dp_pairs(lambda x, z, y, c, k=k: ((x + k) % 4, z, y, c)) for k in (1, 2, 3)}
YS = {k: dp_pairs(lambda x, z, y, c, k=k: (x, z, (y + k) % 4, c)) for k in (1, 2, 3)}


def send(values, pairs):
    return lax.ppermute(values, "dp", pairs)


def swap_tensor(values):
    return lax.ppermute(values, "tensor", SWAP)


def near_core(shape, kind):
    return pltpu.VMEM(shape, kind)


def outside(shape, kind):
    return pltpu.HBM(shape, kind)


def far_off(values):
    return pltpu.with_memory_space_constraint(values, pltpu.HBM)


def anywhere(count):
    return [pl.BlockSpec(memory_space=pl.ANY)] * count


def in_vmem(count):
    return [pl.BlockSpec(memory_space=pltpu.VMEM)] * count


def after(values, *first):
    return pl.pallas_call(
        lambda *refs: None,
        in_specs=anywhere(1 + len(first)),
        out_specs=pl.BlockSpec(memory_space=pl.ANY),
        out_shape=jax.ShapeDtypeStruct(values.shape, values.dtype),
        input_output_aliases={0: 0},
        cost_estimate=cost(0.01),
        name="after",
    )(values, *first)


def sides(values, perms):
    return [values, send(values, perms[1]), send(values, perms[3])]


def opposite(pieces, perms, axis):
    half = pieces[0].shape[axis] // 2
    front = lax.slice_in_dim(pieces[1], 0, half, axis=axis)
    back = lax.slice_in_dim(pieces[2], half, 2 * half, axis=axis)
    return [send(front, perms[1]), send(back, perms[3])]


def halves_kernel(a_back, a_ahead, b_back, b_ahead, first, a_front, a_rear, b_front, b_rear, sems):
    a_half, b_half = a_front.shape[0], b_front.shape[0]
    copy_all(
        [
            (a_back.at[pl.ds(0, a_half)], a_front),
            (a_ahead.at[pl.ds(a_half, a_half)], a_rear),
            (b_back.at[pl.ds(0, b_half)], b_front),
            (b_ahead.at[pl.ds(b_half, b_half)], b_rear),
        ],
        sems,
    )


def opposites(a_pieces, b_pieces, first):
    shapes = [(v.shape[0] // 2, *v.shape[1:]) for v in (a_pieces[0], a_pieces[0], b_pieces[0], b_pieces[0])]
    parts = pl.pallas_call(
        halves_kernel,
        in_specs=in_vmem(4) + anywhere(1),
        out_specs=in_vmem(4),
        out_shape=[jax.ShapeDtypeStruct(shape, BF) for shape in shapes],
        scratch_shapes=[pltpu.SemaphoreType.DMA((4,))],
        compiler_params=pltpu.CompilerParams(vmem_limit_bytes=16 * 1024 * 1024),
        cost_estimate=cost(1),
        name="halves",
    )(*a_pieces[1:], *b_pieces[1:], first)
    return [send(parts[0], XS[1]), send(parts[1], XS[3])], [send(parts[2], YS[1]), send(parts[3], YS[3])]


def ring(values, perms):
    return [values] + [send(values, perms[k]) for k in (1, 3, 2)]


BACK = (0, 1, 3, 2)


def copy_all(copies, sems):
    started = [pltpu.make_async_copy(source, target, sems.at[i]) for i, (source, target) in enumerate(copies)]
    for copy in started:
        copy.start()
    for copy in started:
        copy.wait()


def place_near(a_pieces, b_pieces, start, width, first=()):
    def kernel(*refs):
        d = lax.axis_index("dp")
        x, y = d // 16, (d // 2) % 4
        a_whole, b_whole, sems = refs[8 + len(first) :]
        copies = []
        for i, back in enumerate(BACK):
            at_y, at_x = lax.rem(y + 4 - back, 4), lax.rem(x + 4 - back, 4)
            copies.append((refs[i].at[:, :, pl.ds(start, width)], a_whole.at[:, at_y]))
            copies.append((refs[4 + i].at[:, :, pl.ds(start, width)], b_whole.at[at_x]))
        copy_all(copies, sems)

    return pl.pallas_call(
        kernel,
        in_specs=in_vmem(8) + anywhere(len(first)),
        out_specs=in_vmem(2),
        out_shape=[jax.ShapeDtypeStruct(shape, BF) for shape in ((2, 4, 48, width), (4, 2, 48, width))],
        scratch_shapes=[pltpu.SemaphoreType.DMA((8,))],
        compiler_params=pltpu.CompilerParams(vmem_limit_bytes=16 * 1024 * 1024),
        cost_estimate=cost(1.5),
        name="place_near",
    )(*a_pieces, *b_pieces, *first)


def place_far(a_pieces, b_pieces, columns, first=()):
    count = a_pieces[0].shape[-1] // columns

    def kernel(*refs):
        d = lax.axis_index("dp")
        x, y = d // 16, (d // 2) % 4
        whole, sems = refs[10 + len(first) :]
        copies = []
        for i, back in enumerate((0, 1, 3, 2, 2)):
            at_y, at_x = lax.rem(y + 4 - back, 4), lax.rem(x + 4 - back, 4)
            for j in range(count):
                lanes = pl.ds(j * columns, columns)
                z = pl.ds(i - 3, 1) if i > 2 else pl.ds(0, 2)
                xs = pl.ds(2 * (i - 3), 2) if i > 2 else pl.ds(0, 4)
                copies.append((refs[i].at[:, :, :, lanes], whole.at[j, at_x, z]))
                copies.append((refs[5 + i].at[:, :, :, lanes], whole.at[count + j, xs, :, at_y]))
        copy_all(copies, sems)

    return pl.pallas_call(
        kernel,
        in_specs=in_vmem(10) + anywhere(len(first)),
        out_specs=pl.BlockSpec(memory_space=pltpu.VMEM),
        out_shape=jax.ShapeDtypeStruct((2 * count, 4, 2, 4, 48, columns), BF),
        scratch_shapes=[pltpu.SemaphoreType.DMA((10 * count,))],
        compiler_params=pltpu.CompilerParams(vmem_limit_bytes=24 * 1024 * 1024),
        cost_estimate=cost(2),
        name="place_far",
    )(*a_pieces, *b_pieces, *first).reshape(2 * count, 1536, columns)


def pack_kernel(in_weight, bc_weight, step_weight, out_weight, mine, other):
    c = lax.rem(lax.axis_index("dp"), 2)
    out_rows = out_weight[...].T
    steps = step_weight[...]
    for target, half in ((mine, c), (other, 1 - c)):
        at = pl.multiple_of(half * 768, 128)
        target[:, 0:512] = in_weight[1, :, pl.ds(at, 512)]
        target[:, 512:1280] = in_weight[0, :, pl.ds(at, 768)]
        target[:, 1280:1536] = in_weight[1, :, pl.ds(pl.multiple_of(at + 512, 128), 256)]
        target[:, 1536:1664] = bc_weight[:, pl.ds(pl.multiple_of(half * 128, 128), 128)]
        second = jnp.full((24, 12), half) == 1
        own = jnp.where(second, steps[:, 12:].astype(F32), steps[:, :12].astype(F32))
        gap = jnp.zeros((24, 4), F32)
        parts = [own[:, 0:4], gap, own[:, 4:8], gap, own[:, 8:12], jnp.zeros((24, 108), F32)]
        target[:, 1664:1792] = jnp.concatenate(parts, 1).astype(BF)
        wanted = jnp.full((24, 768), half) == 1
        pieces = (out_rows[:, 768:].astype(F32), out_rows[:, :768].astype(F32))
        target[:, 1792:2560] = jnp.where(wanted, *pieces).astype(BF)


def pack(in_weight, bc_weight, step_weight, out_weight):
    return pl.pallas_call(
        pack_kernel,
        in_specs=in_vmem(4),
        out_specs=in_vmem(2),
        out_shape=[jax.ShapeDtypeStruct((24, 2560), BF)] * 2,
        compiler_params=pltpu.CompilerParams(vmem_limit_bytes=16 * 1024 * 1024),
        cost_estimate=cost(1.5),
        name="pack",
    )(in_weight, bc_weight, step_weight, out_weight)


def pair_rows(mine, other, c):
    got = send(other, CORE)
    return jnp.concatenate([jnp.where(c == 0, mine, got), jnp.where(c == 0, got, mine)], 0)


def pair_planes(rows, z):
    other = send(rows, ZHI)
    return jnp.stack([jnp.where(z == 0, rows, other), jnp.where(z == 0, other, rows)], 0)


def here():
    d = lax.axis_index("dp")
    return d // 16, (d // 2) % 4


def ahead(at, k):
    return lax.rem(at + k, 4)


def pieces_kernel(by_x, own, widths, left, *refs):
    rights, refs = refs[: len(widths)], refs[len(widths) :]
    got = refs[0] if own else None
    outs = refs[1:6] if own else refs[:1]
    x, y = here()
    right = jnp.concatenate([r[:, a:b] if len(r.shape) == 2 else r[a] for r, (a, b) in zip(rights, widths)], 1)

    def write(k, part, values):
        if not own:
            outs[0][(k, *part)] = values.astype(BF)
            return
        values = values + got[(k, *part)].astype(F32)
        if k == 2 and by_x:
            outs[3][...] = values[:192].astype(BF)
            outs[4][...] = values[192:].astype(BF)
        elif k == 2:
            outs[3 + part[0] // 2][part[0] % 2, part[1]] = values.astype(BF)
        else:
            outs[(0, 1, None, 2)[k]][part or Ellipsis] = values

    if by_x:
        for k in range(4):
            rows = pl.ds(pl.multiple_of(ahead(x, k) * 384, 128), 384)
            write(k, (), dot_rows(left[:, rows], right))
    else:
        whole = refs[-1]
        for i in range(4):
            whole[i] = dot_rows(left[:, i * 384 : (i + 1) * 384], right)
        for k in range(4):
            for i in range(4):
                for z in range(2):
                    rows = pl.ds(pl.multiple_of((z * 4 + ahead(y, k)) * 48, 16), 48)
                    write(k, (i, z), whole[i, rows, :])


def weight_pieces(by_x, left, rights, widths, got=(), first=()):
    width = sum(b - a if r.ndim == 2 else b for r, (a, b) in zip(rights, widths))
    shape = (384, width) if by_x else (4, 2, 48, width)
    if got:
        near, far = near_core(shape, F32), near_core((shape[0] // 2, *shape[1:]), BF)
        outs = [near] * 3 + [far] * 2
    else:
        outs = jax.ShapeDtypeStruct((4, *shape), BF)
    count = 1 + len(rights) + len(got)

    def kernel(*refs):
        pieces_kernel(by_x, bool(got), widths, *refs[:count], *refs[count + len(first) :])

    return pl.pallas_call(
        kernel,
        in_specs=in_vmem(count) + anywhere(len(first)),
        out_specs=in_vmem(5) if got else in_vmem(1)[0],
        out_shape=outs,
        scratch_shapes=[] if by_x else [pltpu.VMEM((4, 384, width), F32)],
        compiler_params=pltpu.CompilerParams(vmem_limit_bytes=24 * 1024 * 1024),
        cost_estimate=cost(2),
        name="weight_pieces",
    )(left, *rights, *got, *first)


def pass_kernel(plus, minus, left, right, *refs):
    on, back = refs[-2:]
    half = left.shape[0]
    on[:half] = (plus[:half] + left[...].astype(F32)).astype(BF)
    on[half:] = plus[half:].astype(BF)
    back[:half] = minus[:half].astype(BF)
    back[half:] = (minus[half:] + right[...].astype(F32)).astype(BF)


def pass_on(by_x, pieces, *first):
    perms = XS if by_x else YS
    left, right = send(pieces[3], perms[1]), send(pieces[4], perms[3])
    shape = near_core(pieces[1].shape, BF)
    return pl.pallas_call(
        pass_kernel,
        in_specs=in_vmem(4) + anywhere(len(first)),
        out_specs=in_vmem(2),
        out_shape=[shape, shape],
        compiler_params=pltpu.CompilerParams(vmem_limit_bytes=16 * 1024 * 1024),
        cost_estimate=cost(1),
        name="pass_on",
    )(pieces[1], pieces[2], left, right, *first)


def near_sum_kernel(by_x, own, one, two, *outs):
    outs = outs[-5:]
    x, y = here()
    total = own[...] + one[...].astype(F32) + two[...].astype(F32)
    whole = outs[4]
    whole[...] = total.reshape(whole.shape)
    for k in range(4):
        if by_x:
            for z in range(2):
                outs[k][z] = whole[z, ahead(y, k)].astype(outs[k].dtype)
        else:
            outs[k][...] = whole[ahead(x, k)].astype(outs[k].dtype)


def near_sum(by_x, own, got, first):
    width = own.shape[-1]
    shape = (2, 48, width)
    return pl.pallas_call(
        lambda *refs: near_sum_kernel(by_x, *refs),
        in_specs=in_vmem(3) + anywhere(len(first)),
        out_specs=in_vmem(4),
        out_shape=[near_core(shape, F32)] + [near_core(shape, BF)] * 3,
        scratch_shapes=[pltpu.VMEM((2, 4, 48, width) if by_x else (4, 2, 48, width), F32)],
        compiler_params=pltpu.CompilerParams(vmem_limit_bytes=16 * 1024 * 1024),
        cost_estimate=cost(1),
        name="near_sum",
    )(own, *got, *first)


def scatter_near(by_x, pieces, passed, *first):
    near = XS if by_x else YS
    return near_sum(by_x, pieces[0], [send(passed[0], near[1]), send(passed[1], near[3])], first)


def send_far(by_x, pieces):
    far = YS if by_x else XS
    return [send(pieces[k], far[k]) for k in (1, 2, 3)]


def sum_far(pieces, got):
    got = [values.astype(F32) for values in got]
    return pieces[0] + got[1] + (got[0] + got[2])


def plane_other(values, z):
    return send(lax.dynamic_index_in_dim(values, 1 - z, 0, keepdims=False).astype(BF), ZHI)


def plane_sum(values, other, z):
    return lax.dynamic_index_in_dim(values, z, 0, keepdims=False) + other.astype(F32)


def rows_kernel(first, rest, got, grad_in, grad_bc, grad_step, grad_out):
    c = lax.rem(lax.axis_index("dp"), 2)
    rows = pl.ds(pl.multiple_of(c * 24, 8), 24)

    def halves(values, start, width):
        mine = values[rows, start : start + width]
        other = got[:, (0 if values is first else 1024) + start : (0 if values is first else 1024) + start + width]
        flag = jnp.full((24, width), c) == 0
        return jnp.where(flag, mine, other), jnp.where(flag, other, mine)

    for i, (values, start) in enumerate(((rest, 0), (first, 0))):
        grad_in[i, :, :768], grad_in[i, :, 768:] = halves(values, start, 768)
    grad_bc[:, :TILE], grad_bc[:, TILE:] = halves(first, 768, TILE)
    for half, values in enumerate(halves(first, 896, TILE)):
        for group in range(3):
            grad_step[:, half * 12 + group * 4 : half * 12 + group * 4 + 4] = values[:, group * 8 : group * 8 + 4]
    grad_out[:768, :], grad_out[768:, :] = [values.T for values in halves(rest, 768, 768)]


def weight_rows(first, rest):
    c = lax.axis_index("dp") % 2
    both = jnp.concatenate([lax.dynamic_slice_in_dim(v, (1 - c) * 24, 24, 0) for v in (first, rest)], 1)
    shapes = [(2, 24, 1536), (24, 256), (24, 24), (1536, 24)]
    return pl.pallas_call(
        rows_kernel,
        in_specs=in_vmem(3),
        out_specs=in_vmem(4),
        out_shape=[jax.ShapeDtypeStruct(shape, F32) for shape in shapes],
        compiler_params=pltpu.CompilerParams(vmem_limit_bytes=16 * 1024 * 1024),
        cost_estimate=cost(1.5),
        name="weight_rows",
    )(first, rest, send(both, CORE))


def around(values, perms):
    got = [send(values, perms[k]) for k in (1, 2, 3)]
    return (values + got[1]) + (got[0] + got[2])


def dot(left, right):
    return jnp.dot(left, right, preferred_element_type=F32)


def dot_rows(left, right):
    return lax.dot_general(left, right, (((0,), (0,)), ((), ())), preferred_element_type=F32)


def dot_cols(left, right):
    return lax.dot_general(left, right, (((1,), (1,)), ((), ())), preferred_element_type=F32)


def silu_slope(values):
    sig = jax.nn.sigmoid(values)
    return sig * (1.0 + values * (1.0 - sig))


def down(values, offset):
    return values if offset == 0 else pltpu.roll(values, offset, 0)


def up(values, offset):
    return values if offset == 0 else pltpu.roll(values, values.shape[0] - offset, 0)


def conv_of(pre, taps, bias, masks):
    out = bias + taps[3:4] * pre
    for offset in (1, 2, 3):
        out = out + taps[3 - offset : 4 - offset] * (down(pre, offset) * masks[:, offset : offset + 1])
    return out


def lane_halves(values):
    low = lax.broadcasted_iota(jnp.int32, (1, TILE), 1) < 64
    zero = jnp.zeros_like(values)
    return jnp.where(low, values, zero), jnp.where(low, zero, values)


def params(mebibytes):
    return pltpu.CompilerParams(dimension_semantics=("arbitrary",), vmem_limit_bytes=mebibytes * 1024 * 1024)


def full(*shape):
    return pl.BlockSpec(shape, lambda i: (0,) * len(shape), pipeline_mode=pl.Buffered(1))


def out_full(*shape):
    return pl.BlockSpec(shape, lambda i: (0,) * len(shape))


def block(count):
    return pl.BlockSpec((count, BLOCK), lambda i: (0, i))


WIDE = 384


def wide(count):
    return pl.BlockSpec((count, WIDE), lambda i: (0, i))


def running(values):
    row = lax.broadcasted_iota(jnp.int32, values.shape, 0)
    offset = 1
    while offset < values.shape[0]:
        values = values + jnp.where(row >= offset, pltpu.roll(values, offset, 0), 0.0)
        offset *= 2
    return values


def visible_of(seg_col, seg_row, later_rows):
    row = lax.broadcasted_iota(jnp.int32, (LEN, LEN), 0)
    col = lax.broadcasted_iota(jnp.int32, (LEN, LEN), 1)
    ordered = (row <= col) if later_rows else (row >= col)
    return ordered & (seg_col[...] == seg_row[...])


def prep_kernel(normed, tail_own, tail_peer, seg_col, seg_row, masks, taps, bias, heads, bc_w, scores, scores_t, act, pre, cols, rows, steps):
    bc_w[0] = tail_own[0, :, :TILE]
    bc_w[1] = tail_peer[0, :, :TILE]
    own = dot(normed[...], tail_own[0])
    peer = dot(normed[...], tail_peer[0])
    core0 = jnp.full((LEN, TILE), lax.rem(lax.axis_index("dp"), 2)) == 0
    pre[:, :TILE] = jnp.where(core0, own[:, :TILE], peer[:, :TILE])
    pre[:, TILE:] = jnp.where(core0, peer[:, :TILE], own[:, :TILE])
    conv_out = conv_of(pre[...], taps[...], bias[...], masks[...])
    act[...] = (conv_out * jax.nn.sigmoid(conv_out)).astype(BF)
    b_proj, c_proj = act[:, :TILE], act[:, TILE:]
    scores[...] = jnp.where(visible_of(seg_col, seg_row, False), dot_cols(c_proj, b_proj), 0.0)
    scores_t[...] = jnp.where(visible_of(seg_col, seg_row, True), dot_cols(b_proj, c_proj), 0.0)
    step_pre = own[:, TILE:] + pltpu.roll(peer[:, TILE:], 24, 1) + heads[0:1, :]
    step_size = jnp.maximum(step_pre, 0.0) + jnp.log1p(jnp.exp(-jnp.abs(step_pre)))
    sums = running(step_size * heads[1:2, :]) * LOG2E
    logs = jnp.log(step_size) * LOG2E
    steps[0] = step_pre
    steps[1] = step_size
    for i, values in enumerate((sums, sums - logs, logs)):
        cols[i] = values
        rows[i] = values.T


def prepare(normed, inner_own, inner_peer, seg_col, seg_row, masks, taps, bias, heads):
    tail = pl.BlockSpec((1, 1536, 256), lambda i: (3, 0, 0), pipeline_mode=pl.Buffered(1))
    shapes = [
        ((2, 1536, TILE), BF),
        ((LEN, LEN), F32),
        ((LEN, LEN), F32),
        ((LEN, 256), BF),
        ((LEN, 256), F32),
        ((3, LEN, TILE), F32),
        ((3, TILE, LEN), F32),
        ((2, LEN, TILE), F32),
    ]
    return pl.pallas_call(
        prep_kernel,
        grid=(1,),
        in_specs=[in_vmem(1)[0], tail, tail, full(LEN, 1), full(1, LEN), full(LEN, 4), full(4, 256), full(1, 256), full(8, TILE)],
        out_specs=in_vmem(len(shapes)),
        out_shape=[(near_core if i in (1, 5, 6) else outside)(shape, kind) for i, (shape, kind) in enumerate(shapes)],
        compiler_params=params(24),
        cost_estimate=cost(2),
        name="prepare",
    )(normed, inner_own, inner_peer, seg_col, seg_row, masks, taps, bias, heads)


def norm_kernel(hidden, cotangent, other, gain, whole, normed, scale, cot):
    first = jnp.full((256, 1536), lax.axis_index("tensor")) == 0
    mine, theirs = hidden[...].astype(F32), other[0:256].astype(F32)
    for part, values in enumerate((jnp.where(first, mine, theirs), jnp.where(first, theirs, mine))):
        rows = slice(part * 256, (part + 1) * 256)
        whole[rows, :] = values.astype(BF)
        inv = lax.rsqrt(jnp.sum(values * values, axis=1, keepdims=True) * (1.0 / 1536.0) + EPS)
        scale[rows, :] = jnp.broadcast_to(inv, (256, TILE))
        normed[rows, :] = (values * inv * gain[...]).astype(BF)
    mine, theirs = cotangent[...].astype(F32), other[256:512].astype(F32)
    cot[0:256, :] = jnp.where(first, mine, theirs).astype(BF)
    cot[256:512, :] = jnp.where(first, theirs, mine).astype(BF)


def norm_of(hidden, cotangent, other, gain):
    whole = near_core((LEN, 1536), BF)
    return pl.pallas_call(
        norm_kernel,
        in_specs=in_vmem(4),
        out_specs=in_vmem(4),
        out_shape=[outside((LEN, 1536), BF), whole, outside((LEN, TILE), F32), whole],
        compiler_params=pltpu.CompilerParams(vmem_limit_bytes=24 * 1024 * 1024),
        cost_estimate=cost(2),
        name="input_norm",
    )(hidden, cotangent, other, gain)


def mix_kernel(half, normed, weight, taps, bias, masks, scores, cols, rows, pre, act, mixed):
    pre[...] = dot(normed[...], weight[0])
    conv_out = conv_of(pre[...], taps[...], bias[...], masks[...])
    act[...] = (conv_out * jax.nn.sigmoid(conv_out)).astype(BF)
    sums_all = pltpu.roll(cols[0], lax.rem(TILE - 24 * half - 8 * pl.program_id(0), TILE), 1)
    for pair in range(2):
        lanes = slice(pair * TILE, (pair + 1) * TILE)
        halves = lane_halves(act[:, lanes])
        for tile in range(4):
            here = slice(tile * TILE, (tile + 1) * TILE)
            weights, values = [], []
            for side in range(2):
                head = 2 * pair + side
                sums = sums_all[here, head : head + 1]
                if tile:
                    decay = jnp.exp2(sums - rows[1, head : head + 1, : tile * TILE])
                    weights.append((scores[here, : tile * TILE] * decay).astype(BF))
                    values.append(halves[side][: tile * TILE])
                decay = jnp.exp2(jnp.minimum(sums - rows[1, head : head + 1, here], rows[2, head : head + 1, here]))
                weights.append((scores[here, here] * decay).astype(BF))
                values.append(halves[side][here])
            mixed[here, lanes] = dot(jnp.concatenate(weights, 1), jnp.concatenate(values, 0))


def third_of(count, half):
    return pl.BlockSpec((count, BLOCK), lambda i: (0, 3 * half + i))


def rows_of(half):
    return pl.BlockSpec((3, 8, LEN), lambda i: (0, 3 * half + i, 0))


def mix_forward(half, normed, weight, taps, bias, masks, scores, cols, rows):
    return pl.pallas_call(
        lambda *refs: mix_kernel(half, *refs),
        grid=(3,),
        in_specs=[
            in_vmem(1)[0],
            pl.BlockSpec((1, 1536, BLOCK), lambda i: (i, 0, 0)),
            third_of(4, half),
            third_of(1, half),
            full(LEN, 4),
            in_vmem(1)[0],
            in_vmem(1)[0],
            rows_of(half),
        ],
        out_specs=[block(LEN)] * 3,
        out_shape=[
            outside((LEN, 768), F32),
            near_core((LEN, 768), BF),
            near_core((LEN, 768), F32),
        ],
        compiler_params=params(24),
        cost_estimate=cost(6.2),
        name="mix_forward",
    )(normed, weight, taps, bias, masks, scores, cols, rows)


def gate_kernel(last, normed, cot, gate_w, out_w, act, mixed, skip, gain, *refs):
    step = pl.program_id(0)
    before = refs[0] if last else None
    gate_pre, grad_gn, stats, squares, dots = refs[last:]

    @pl.when(step == 0)
    def _():
        squares[...] = before[0] if last else jnp.zeros_like(squares)
        dots[...] = before[1] if last else jnp.zeros_like(dots)

    pre = dot(normed[...], gate_w[0])
    upper = dot(cot[...], out_w[0])
    gate_pre[...] = pre
    grad_gn[...] = upper
    mixer_y = mixed[...] + skip[...] * act[...].astype(F32)
    gated = mixer_y * (pre * jax.nn.sigmoid(pre))
    square = gated * gated
    product = upper * gain[...] * gated
    squares[...] += square[:, :TILE] + square[:, TILE : 2 * TILE] + square[:, 2 * TILE :]
    dots[...] += product[:, :TILE] + product[:, TILE : 2 * TILE] + product[:, 2 * TILE :]

    @pl.when(step == 1)
    def _():
        if last:
            stats[0:1, :] = jnp.sum(squares[...].T, axis=0, keepdims=True)
            stats[1:2, :] = jnp.sum(dots[...].T, axis=0, keepdims=True)
            stats[2:8, :] = jnp.zeros((6, LEN), F32)
        else:
            stats[0] = squares[...]
            stats[1] = dots[...]


def half_of(count, half):
    return pl.BlockSpec((count, WIDE), lambda i: (0, 2 * half + i))


def gate_forward(half, normed, cot, rest, act, mixed, skip, gain, before=()):
    weight = lambda part: pl.BlockSpec((1, 1536, WIDE), lambda i: (2 * part + i, 0, 0))
    stats = (8, LEN) if half else (2, LEN, TILE)
    kept = near_core
    return pl.pallas_call(
        lambda *refs: gate_kernel(half, *refs),
        grid=(2,),
        in_specs=[
            *in_vmem(2),
            weight(0),
            weight(1),
            wide(LEN),
            wide(LEN),
            half_of(1, half),
            half_of(1, half),
        ]
        + [full(2, LEN, TILE)] * half,
        out_specs=[wide(LEN), wide(LEN), out_full(*stats)],
        out_shape=[
            kept((LEN, 768), F32),
            kept((LEN, 768), F32),
            jax.ShapeDtypeStruct(stats, F32),
        ],
        scratch_shapes=[pltpu.VMEM((LEN, TILE), F32)] * 2,
        compiler_params=params(24),
        cost_estimate=cost(4.2),
        name="gate_forward",
    )(normed, cot, rest, rest, act, mixed, skip, gain, *before)


def slope_kernel(stats, others, *refs):
    peer_in, own_in, skip, gain, normed, cot = refs[0:4], refs[4:8], *refs[8:12]
    peer_out, own_out, gain_grad = refs[12:15], refs[15:18], refs[18]
    part_gate, part_out, scale, dots, whole = refs[19:]
    step = pl.program_id(0)

    @pl.when(step == 0)
    def _():
        inv = lax.rsqrt((stats[0:1, :] + others[0:1, :]) * (1.0 / 3072.0) + EPS)
        both = (stats[1:2, :] + others[1:2, :]) * (1.0 / 3072.0)
        scale[...] = jnp.broadcast_to(inv, (TILE, LEN)).T
        dots[...] = jnp.broadcast_to(inv * inv * inv * both, (TILE, LEN)).T

    def slopes(gate_pre, grad_gn, act, mixed, grad_y, gate_low, gnormed):
        for part in range(3):
            lanes = slice(part * TILE, (part + 1) * TILE)
            q = scale[...]
            pre = gate_pre[:, lanes]
            sig = jax.nn.sigmoid(pre)
            gate_act = pre * sig
            mixer_y = mixed[:, lanes] + skip[:, lanes] * act[:, lanes].astype(F32)
            gated = mixer_y * gate_act
            scaled = gated * q
            gnormed[:, lanes] = (scaled * gain[:, lanes]).astype(BF)
            upper = grad_gn[:, lanes]
            gain_grad[:, lanes] = jnp.sum(upper * scaled, axis=0, keepdims=True)
            grad_gated = q * gain[:, lanes] * upper - gated * dots[...]
            grad_y[:, lanes] = grad_gated * gate_act
            gate_low[:, lanes] = (grad_gated * mixer_y * (sig * (1.0 + pre * (1.0 - sig)))).astype(BF)

    @pl.when(step >= 2)
    def _():
        slopes(*own_in, *own_out)

    @pl.when(step < 2)
    def _():
        slopes(*peer_in, *peer_out)
        x, y = here()
        for k in range(4):
            rows = pl.ds(pl.multiple_of(ahead(x, k) * 384, 128), 384)
            part_gate[k] = dot_rows(normed[:, rows], peer_out[1][...]).astype(BF)
        for i in range(4):
            whole[...] = dot_rows(cot[:, i * 384 : (i + 1) * 384], peer_out[2][...])
            for k in range(4):
                for z in range(2):
                    rows = pl.ds(pl.multiple_of((z * 4 + ahead(y, k)) * 48, 16), 48)
                    part_out[k, i, z] = whole[rows, :].astype(BF)


def gate_backward(stats, others, peer, own, skip, gain, normed, cot):
    early, late = lambda i: jnp.minimum(i, 1), lambda i: jnp.maximum(i - 2, 0)
    early_block, late_block = [pl.BlockSpec((LEN, WIDE), lambda i, at=at: (0, at(i))) for at in (early, late)]
    turned = pl.BlockSpec((1, WIDE), lambda i: (0, (i + 2) % 4))
    low, full_y = outside((LEN, 768), BF), outside((LEN, 768), F32)
    return pl.pallas_call(
        slope_kernel,
        grid=(4,),
        in_specs=[full(8, LEN), full(8, LEN)] + [early_block] * 4 + [late_block] * 4 + [turned] * 2 + in_vmem(2),
        out_specs=[early_block] * 3
        + [late_block] * 3
        + [
            turned,
            pl.BlockSpec((4, 384, WIDE), lambda i: (0, 0, early(i))),
            pl.BlockSpec((4, 4, 2, 48, WIDE), lambda i: (0, 0, 0, 0, early(i))),
        ],
        out_shape=[full_y, low, low] * 2
        + [
            jax.ShapeDtypeStruct((1, 1536), F32),
            jax.ShapeDtypeStruct((4, 384, 768), BF),
            jax.ShapeDtypeStruct((4, 4, 2, 48, 768), BF),
        ],
        scratch_shapes=[pltpu.VMEM((LEN, TILE), F32)] * 2 + [pltpu.VMEM((384, WIDE), F32)],
        compiler_params=params(28),
        cost_estimate=cost(10),
        name="gate_backward",
    )(stats, others, *peer, *own, skip, gain, normed, cot)


def product_kernel(own, peer, weight_own, weight_peer, *refs):
    target, total = refs[-2:]
    step = pl.program_id(0)
    for test, left, weight in ((step < 2, own, weight_own), (step >= 2, peer, weight_peer)):

        @pl.when(test)
        def _(left=left, weight=weight):
            part = dot_cols(left[...], weight[0])

            @pl.when(step == 0)
            def _():
                total[...] = part

            @pl.when(step > 0)
            def _():
                total[...] += part

    @pl.when(step == 3)
    def _():
        target[...] = total[...].astype(target.dtype)


def product(own, peer, rest_own, rest_peer, kind, target, *first):
    early = lambda i: jnp.minimum(i, 1)
    late = lambda i: jnp.maximum(i - 2, 0)
    return pl.pallas_call(
        product_kernel,
        grid=(4,),
        in_specs=[
            pl.BlockSpec((LEN, WIDE), lambda i: (0, early(i))),
            pl.BlockSpec((LEN, WIDE), lambda i: (0, late(i))),
            pl.BlockSpec((1, 1536, WIDE), lambda i: (2 * kind + early(i), 0, 0)),
            pl.BlockSpec((1, 1536, WIDE), lambda i: (2 * kind + late(i), 0, 0)),
        ]
        + anywhere(len(first)),
        out_specs=in_vmem(1)[0],
        out_shape=jax.ShapeDtypeStruct((LEN, 1536), target),
        scratch_shapes=[pltpu.VMEM((LEN, 1536), F32)],
        compiler_params=params(24),
        cost_estimate=cost(4),
        name="product",
    )(far_off(own), far_off(peer), far_off(rest_own), far_off(rest_peer), *first)


SEEN = [(j, i) for j in range(4) for i in range(j, 4)]


def back_kernel(half, grad_y, act, mixed, pre, scores, taps, bias, masks, cols, rows, skip, *refs):
    step = pl.program_id(0)
    if half:
        inner_low, sums, flows, grad_scores, grad_act = refs[-5:]
    else:
        flows_0, scores_0 = refs[:2]
        inner_low, sums, flows, grad_scores, scores_low, grad_act = refs[-6:]

    @pl.when(step == 0)
    def _():
        grad_scores[...] = jnp.zeros_like(grad_scores) if half else scores_0[...]
        flows[...] = jnp.zeros_like(flows) if half else flows_0[...]

    turn = lax.rem(TILE - 24 * half - 8 * step, TILE)
    back_all, most_all = pltpu.roll(cols[1], turn, 1), pltpu.roll(cols[2], turn, 1)

    pairs = []
    for pair in range(2):
        lanes = slice(pair * TILE, (pair + 1) * TILE)
        low = grad_y[:, lanes].astype(BF)
        pairs.append((lane_halves(act[:, lanes]), low, lane_halves(low)))
    for tile in range(4):
        here = slice(tile * TILE, (tile + 1) * TILE)
        after = slice((tile + 1) * TILE, LEN)
        add_diag, add_rest = 0.0, 0.0
        for pair in range(2):
            act_halves, low, low_halves = pairs[pair]
            weights, values = [], []
            stacked = jnp.concatenate([act_halves[0][here], act_halves[1][here]], 0)
            grad_w = dot_cols(stacked, low[tile * TILE :])
            for side in range(2):
                head = 2 * pair + side
                back = back_all[here, head : head + 1]
                most = most_all[here, head : head + 1]
                own = slice(side * TILE, (side + 1) * TILE)
                decay = jnp.exp2(jnp.minimum(rows[0, head : head + 1, here] - back, most))
                add_diag = add_diag + grad_w[own, :TILE] * decay
                weights.append((scores[here, here] * decay).astype(BF))
                values.append(low_halves[side][here])
                if tile < 3:
                    decay = jnp.exp2(rows[0, head : head + 1, after] - back)
                    add_rest = add_rest + grad_w[own, TILE:] * decay
                    weights.append((scores[here, after] * decay).astype(BF))
                    values.append(low_halves[side][after])
            lanes = slice(pair * TILE, (pair + 1) * TILE)
            grad_act[here, lanes] = dot(jnp.concatenate(weights, 1), jnp.concatenate(values, 0))
        grad_scores[here, here] += add_diag
        if tile < 3:
            grad_scores[here, after] += add_rest

    if not half:

        @pl.when(step == 2)
        def _():
            for at, (j, i) in enumerate(SEEN):
                rows_j, cols_i = slice(j * TILE, (j + 1) * TILE), slice(i * TILE, (i + 1) * TILE)
                scores_low[at] = grad_scores[rows_j, cols_i].astype(BF)

    lane = lax.broadcasted_iota(jnp.int32, (1, TILE), 1)
    row_flows, col_flows = 0.0, 0.0

    low_lane = lax.broadcasted_iota(jnp.int32, (1, TILE), 1) < 64
    for pair in range(2):
        lanes = slice(pair * TILE, (pair + 1) * TILE)
        values = act[:, lanes].astype(F32)
        grad = grad_y[:, lanes]
        row_flow = grad.astype(BF).astype(F32) * mixed[:, lanes]
        col_flow = values * grad_act[:, lanes]
        for side, mask in ((0, low_lane), (1, ~low_lane)):
            head = 2 * pair + side
            here = lane == 24 * half + 8 * step + head
            row_flows += jnp.where(here, jnp.sum(jnp.where(mask, row_flow, 0.0), axis=1, keepdims=True), 0.0)
            col_flows += jnp.where(here, jnp.sum(jnp.where(mask, col_flow, 0.0), axis=1, keepdims=True), 0.0)
        taps_l, masks_v = taps[:, lanes], masks[...]
        pre_l = pre[:, lanes]
        conv_out = conv_of(pre_l, taps_l, bias[:, lanes], masks_v)
        grad_conv = (grad_act[:, lanes] + skip[:, lanes] * grad) * silu_slope(conv_out)
        grad_pre = taps_l[3:4] * grad_conv
        sums[3:4, lanes] = jnp.sum(grad_conv * pre_l, axis=0, keepdims=True)
        for offset in (1, 2, 3):
            masked = grad_conv * masks_v[:, offset : offset + 1]
            tap = 3 - offset
            sums[tap : tap + 1, lanes] = jnp.sum(masked * down(pre_l, offset), axis=0, keepdims=True)
            grad_pre = grad_pre + taps_l[tap : tap + 1] * up(masked, offset)
        sums[4:5, lanes] = jnp.sum(grad_conv, axis=0, keepdims=True)
        sums[5:6, lanes] = jnp.sum(grad * values, axis=0, keepdims=True)
        sums[6:8, lanes] = jnp.zeros((2, TILE), F32)
        inner_low[:, lanes] = grad_pre.astype(BF)
    flows[0] += row_flows
    flows[1] += col_flows


def mix_backward(half, grad_y, act, mixed, pre, scores_t, taps, bias, masks, cols, rows, skip, before=(), first=()):
    low = [] if half else [jax.ShapeDtypeStruct((10, TILE, TILE), BF)]
    return pl.pallas_call(
        lambda *refs: back_kernel(half, *refs),
        grid=(3,),
        in_specs=[
            block(LEN),
            block(LEN),
            block(LEN),
            block(LEN),
            in_vmem(1)[0],
            third_of(4, half),
            third_of(1, half),
            full(LEN, 4),
            in_vmem(1)[0],
            rows_of(half),
            third_of(1, half),
            *in_vmem(len(before)),
            *anywhere(len(first)),
        ],
        out_specs=[block(LEN), block(8), *in_vmem(2 + len(low))],
        out_shape=[
            near_core((LEN, 768), BF),
            jax.ShapeDtypeStruct((8, 768), F32),
            near_core((2, LEN, TILE), F32),
            near_core((LEN, LEN), F32),
        ]
        + low,
        scratch_shapes=[pltpu.VMEM((LEN, BLOCK), F32)],
        compiler_params=params(24),
        cost_estimate=cost(9.8),
        name="mix_backward",
    )(grad_y, act, mixed, pre, scores_t, taps, bias, masks, cols, rows, skip, *before, *first)


def tail_kernel(mine, other, act, pre, seg_col, seg_row, masks, taps, bias, shares, *refs):
    tails, bc_sums, both = refs[-3:]
    seen = visible_of(seg_col, seg_row, True)
    for at, (j, i) in enumerate(SEEN):
        tile = (slice(j * TILE, (j + 1) * TILE), slice(i * TILE, (i + 1) * TILE))
        both[tile] = mine[tile] + other[at].astype(F32)
        if i > j:
            both[tile[1], tile[0]] = jnp.zeros((TILE, TILE), F32)
    low = jnp.where(seen, both[...], 0.0).astype(BF)
    b_proj, c_proj = act[:, :TILE], act[:, TILE:]
    core0 = jnp.full((LEN, TILE), lax.rem(lax.axis_index("dp"), 2)) == 0
    bc_low = []
    for part, grad in ((0, dot(low, c_proj)), (1, dot_rows(low, b_proj))):
        lanes = slice(part * TILE, (part + 1) * TILE)
        taps_l, pre_l, masks_v = taps[:, lanes], pre[:, lanes], masks[...]
        grad_conv = grad * silu_slope(conv_of(pre_l, taps_l, bias[:, lanes], masks_v))
        grad_pre = taps_l[3:4] * grad_conv
        bc_sums[3:4, lanes] = jnp.sum(grad_conv * pre_l, axis=0, keepdims=True)
        for offset in (1, 2, 3):
            masked = grad_conv * masks_v[:, offset : offset + 1]
            tap = 3 - offset
            bc_sums[tap : tap + 1, lanes] = jnp.sum(masked * down(pre_l, offset), axis=0, keepdims=True)
            grad_pre = grad_pre + taps_l[tap : tap + 1] * up(masked, offset)
        bc_sums[4:5, lanes] = jnp.sum(grad_conv, axis=0, keepdims=True)
        bc_sums[5:8, lanes] = jnp.zeros((3, TILE), F32)
        bc_low.append(grad_pre)
    for part, bc in ((0, jnp.where(core0, bc_low[0], bc_low[1])), (1, jnp.where(core0, bc_low[1], bc_low[0]))):
        tails[part, :, :TILE] = bc.astype(BF)
        tails[part, :, TILE:] = shares[part, :, TILE:]


def step_kernel(heads, steps, flows, shares, head_sums):
    step_pre, step_size, rate = steps[0], steps[1], heads[1:2, :]
    change = flows[0] - flows[1]
    before = running(change)
    grad_rate = before[LEN - 1 : LEN, :] - before + change
    sig = jax.nn.sigmoid(step_pre)
    tiny = step_size < 1e-30
    ratio = jnp.where(tiny, 1.0, sig / jnp.where(tiny, 1.0, step_size))
    grad_pre = flows[1] * ratio + grad_rate * rate * sig
    head_sums[0:1, :] = jnp.sum(grad_pre, axis=0, keepdims=True)
    head_sums[1:2, :] = jnp.sum(grad_rate * step_size, axis=0, keepdims=True) * rate
    head_sums[2:8, :] = jnp.zeros((6, TILE), F32)
    own_lane = lax.broadcasted_iota(jnp.int32, (LEN, TILE), 1) < 24
    for part, grad in ((0, grad_pre), (1, pltpu.roll(grad_pre, TILE - 24, 1))):
        shares[part, :, :TILE] = jnp.zeros((LEN, TILE), BF)
        shares[part, :, TILE:] = jnp.where(own_lane, grad, 0.0).astype(BF)


def step_backward(heads, steps, flows):
    return pl.pallas_call(
        step_kernel,
        in_specs=in_vmem(3),
        out_specs=in_vmem(2),
        out_shape=[near_core((2, LEN, 256), BF), jax.ShapeDtypeStruct((8, TILE), F32)],
        compiler_params=pltpu.CompilerParams(vmem_limit_bytes=12 * 1024 * 1024),
        cost_estimate=cost(1),
        name="step_backward",
    )(heads, steps, flows)


def tail_backward(mine, other, act, pre, seg_col, seg_row, masks, taps, bias, shares, *first):
    shapes = [((2, LEN, 256), BF), ((8, 256), F32)]
    return pl.pallas_call(
        tail_kernel,
        in_specs=in_vmem(10) + anywhere(len(first)),
        out_specs=in_vmem(len(shapes)),
        out_shape=[near_core(*shapes[0]), jax.ShapeDtypeStruct(*shapes[1])],
        scratch_shapes=[pltpu.VMEM((LEN, LEN), F32)],
        compiler_params=pltpu.CompilerParams(vmem_limit_bytes=18 * 1024 * 1024),
        cost_estimate=cost(2),
        name="tail_backward",
    )(mine, other, act, pre, seg_col, seg_row, masks, taps, bias, shares, *first)


def bc_kernel(tails, weight, hidden, scale, first, part, gain):
    t = lax.axis_index("tensor")
    rows = pl.ds(pl.multiple_of(t * 256, 256), 256)
    values = dot_cols(tails[0, rows, :TILE], weight[0]) + dot_cols(tails[1, rows, :TILE], weight[1])
    part[...] = values
    gain[...] = jnp.sum(values * hidden[...].astype(F32) * scale[rows, :1], axis=0, keepdims=True)


def bc_normed(tails, weight, hidden, scale, first):
    return pl.pallas_call(
        bc_kernel,
        grid=(1,),
        in_specs=[in_vmem(1)[0], full(2, 1536, TILE), full(256, 1536), full(LEN, TILE)] + anywhere(1),
        out_specs=[out_full(256, 1536), out_full(1, 1536)],
        out_shape=[outside((256, 1536), F32), jax.ShapeDtypeStruct((1, 1536), F32)],
        compiler_params=params(16),
        cost_estimate=cost(1.5),
        name="bc_normed",
    )(tails, far_off(weight), far_off(hidden), far_off(scale), first)


def normed_kernel(before, low_own, low_peer, shares, inner_own, inner_peer, resid, scale, *refs):
    low, gain, total = refs[-3:]
    step = pl.program_id(0)

    @pl.when(step == 0)
    def _():
        total[...] = before[...]

    for test, left, weight in (
        (step < 3, low_peer, inner_peer),
        ((step >= 3) & (step < 6), low_own, inner_own),
        (step == 6, shares, inner_own),
        (step == 7, shares, inner_peer),
    ):

        @pl.when(test)
        def _(left=left, weight=weight):
            values = left[0] if left is shares else left[...]
            total[...] += dot_cols(values, weight[0])

    @pl.when(step == 7)
    def _():
        for i in range(3):
            lanes = slice(i * LEN, (i + 1) * LEN)
            values = total[:, lanes]
            low[:, lanes] = values.astype(BF)
            gain[:, lanes] = jnp.sum(values * resid[:, lanes].astype(F32) * scale[:, :1], axis=0, keepdims=True)


def normed_backward(before, low_own, low_peer, shares, inner_own, inner_peer, resid, scale, *first):
    return pl.pallas_call(
        normed_kernel,
        grid=(8,),
        in_specs=[
            in_vmem(1)[0],
            pl.BlockSpec((LEN, BLOCK), lambda i: (0, jnp.clip(i - 3, 0, 2))),
            pl.BlockSpec((LEN, BLOCK), lambda i: (0, jnp.minimum(i, 2))),
            pl.BlockSpec((1, LEN, BLOCK), lambda i: (jnp.clip(i - 6, 0, 1), 0, 0)),
            pl.BlockSpec((1, 1536, BLOCK), lambda i: (jnp.clip(i - 3, 0, 3), 0, 0)),
            pl.BlockSpec((1, 1536, BLOCK), lambda i: (jnp.where(i < 3, i, 3), 0, 0)),
            in_vmem(1)[0],
            full(LEN, TILE),
        ]
        + anywhere(len(first)),
        out_specs=in_vmem(2),
        out_shape=[jax.ShapeDtypeStruct((LEN, 1536), BF), jax.ShapeDtypeStruct((1, 1536), F32)],
        scratch_shapes=[pltpu.VMEM((LEN, 1536), F32)],
        compiler_params=params(24),
        cost_estimate=cost(6),
        name="normed_backward",
    )(before, low_own, low_peer, shares, inner_own, inner_peer, resid, scale, *first)


def hidden_kernel(hidden, cotangent, scale, gain, low, got, bc_part, first, out):
    t = lax.axis_index("tensor")
    rows = pl.ds(pl.multiple_of(t * 256, 256), 256)
    grad = low[rows, :].astype(F32) + got[...].astype(F32) + bc_part[...]
    values = hidden[...].astype(F32)
    scaled = grad * gain[...]
    inv = scale[rows, :1]
    stat = jnp.sum(scaled * values, axis=1, keepdims=True) * (inv * inv * inv * (1.0 / 1536.0))
    out[...] = cotangent[...].astype(F32) + inv * scaled - values * stat


def hidden_grad(hidden, cotangent, scale, gain, low, got, bc_part, first):
    return pl.pallas_call(
        hidden_kernel,
        grid=(1,),
        in_specs=[
            full(256, 1536),
            full(256, 1536),
            full(LEN, TILE),
            full(1, 1536),
            full(LEN, 1536),
            full(256, 1536),
            full(256, 1536),
            pl.BlockSpec(memory_space=pl.ANY),
        ],
        out_specs=out_full(256, 1536),
        out_shape=jax.ShapeDtypeStruct((256, 1536), F32),
        compiler_params=params(20),
        cost_estimate=cost(3),
        name="hidden_grad",
    )(far_off(hidden), far_off(cotangent), far_off(scale), gain, low, got, far_off(bc_part), first)


def precise(left, right):
    return jnp.dot(left, right, preferred_element_type=F32, precision=lax.Precision.HIGHEST)


def small_kernel(sums_own, sums_peer, gain, norm_grad, norm_bc, bc_sums, head_sums, *refs):
    whole = refs[-1]
    core = lax.rem(lax.axis_index("dp"), 2)
    for row, own, peer in (
        (0, sums_own[0:5], sums_peer[0:5]),
        (5, gain[:, :768], gain[:, 768:]),
    ):
        flag = jnp.full(own.shape, core) == 0
        whole[row : row + own.shape[0], :768] = jnp.where(flag, own, peer)
        whole[row : row + own.shape[0], 768:] = jnp.where(flag, peer, own)
    whole[6:7, :] = norm_grad[...] + norm_bc[...]
    for tap in range(5):
        whole[7:8, tap * 256 : (tap + 1) * 256] = bc_sums[tap : tap + 1, :]
    unit = lax.broadcasted_iota(jnp.int32, (768, TILE), 0) // 64
    lane = lax.broadcasted_iota(jnp.int32, (768, TILE), 1)
    spot = (unit // 4) * 8 + unit % 4
    own = precise(sums_own[...], (lane == spot).astype(F32))
    peer = precise(sums_peer[...], (lane == spot + 24).astype(F32))
    heads = head_sums[...]
    rows = (heads[0:1], heads[1:2], (own + peer)[5:6])
    lane = lax.broadcasted_iota(jnp.int32, (1, TILE), 1)
    flag = jnp.full((1, TILE), core) == 0
    step, decay, skip = [
        jnp.where(flag, v, jnp.where(lane < 24, pltpu.roll(v, TILE - 24, 1), pltpu.roll(v, 24, 1))) for v in rows
    ]
    whole[7:8, 1280:1408] = jnp.where(lane < 64, step, pltpu.roll(skip, 64, 1))
    whole[7:8, 1408:1536] = decay


def small_of(*parts):
    shapes = [(8, 768), (8, 768), (1, 1536), (1, 1536), (1, 1536), (8, 256), (8, TILE)]
    return pl.pallas_call(
        small_kernel,
        grid=(1,),
        in_specs=[full(*shape) for shape in shapes] + anywhere(len(parts) - 7),
        out_specs=in_vmem(1)[0],
        out_shape=jax.ShapeDtypeStruct((8, 1536), F32),
        compiler_params=params(8),
        cost_estimate=cost(1),
        name="small_pack",
    )(*parts)


def outputs_kernel(mine, other, conv_grad, bias_grad, gain_grad, norm_grad, heads):
    def halves(rows, width):
        flag = jnp.full(mine[rows, :width].shape, lax.axis_index("tensor")) == 0
        a, b = mine[rows, :width], other[rows, :width]
        return jnp.where(flag, a, b), jnp.where(flag, b, a)

    for rows, target in ((slice(0, 4), conv_grad), (slice(4, 5), bias_grad), (slice(5, 6), gain_grad)):
        low, high = halves(rows, 1536)
        target[:, :1536] = low
        target[:, 1536:3072] = high
    for tap in range(4):
        conv_grad[tap : tap + 1, 3072:] = mine[7:8, tap * 256 : (tap + 1) * 256]
    bias_grad[:, 3072:] = mine[7:8, 1024:1280]
    norm_grad[...] = mine[6:7, :] + other[6:7, :]
    lane = lax.broadcasted_iota(jnp.int32, (TILE, 24), 0)
    head = lax.broadcasted_iota(jnp.int32, (TILE, 24), 1)
    spot = (head // 4) * 8 + head % 4
    for part, at in enumerate((1280, 1408)):
        flag = jnp.full((8, TILE), lax.axis_index("tensor")) == 0
        a, b = mine[:, at : at + TILE], other[:, at : at + TILE]
        for half, values in enumerate((jnp.where(flag, a, b), jnp.where(flag, b, a))):
            lanes = slice(half * 24, half * 24 + 24)
            heads[8 * part : 8 * part + 8, lanes] = precise(values, (lane == spot).astype(F32))
            if not part:
                heads[16:24, lanes] = precise(values, (lane == spot + 64).astype(F32))


def outputs_of(mine, other):
    shapes = [(4, 3328), (1, 3328), (1, 3072), (1, 1536), (24, 48)]
    return pl.pallas_call(
        outputs_kernel,
        in_specs=in_vmem(2),
        out_specs=in_vmem(5),
        out_shape=[jax.ShapeDtypeStruct(shape, F32) for shape in shapes],
        compiler_params=pltpu.CompilerParams(vmem_limit_bytes=16 * 1024 * 1024),
        cost_estimate=cost(1.5),
        name="small_unpack",
    )(mine, other)


def on_device(
    hidden,
    segments,
    norm_gain,
    in_weight,
    bc_weight,
    step_weight,
    conv_weight,
    conv_bias,
    step_bias,
    decay_log,
    skip_gain,
    gate_gain,
    out_weight,
    cotangent,
):
    t = lax.axis_index("tensor")
    d = lax.axis_index("dp")
    spot = (d // 16, (d // 8) % 2, (d // 2) % 4, d % 2)
    c = spot[3]

    def own_first(values, size):
        base = 2 * t * size
        return jnp.concatenate(
            [
                lax.dynamic_slice_in_dim(values, base + c * size, size, values.ndim - 1),
                lax.dynamic_slice_in_dim(values, base + (1 - c) * size, size, values.ndim - 1),
            ],
            values.ndim - 1,
        )

    def in_lanes(values):
        return jnp.pad(jnp.pad(values.reshape(6, 4), ((0, 0), (0, 4))).reshape(48), (0, 80))

    planes = pair_planes(pair_rows(*pack(in_weight, bc_weight, step_weight, out_weight), c), spot[1])
    tokens_other = swap_tensor(after(jnp.concatenate([hidden, cotangent], 0), planes))

    taps = own_first(conv_weight[:, :3072], 768)
    bias = own_first(conv_bias[None, :3072], 768)
    gain = own_first(gate_gain[None, :], 768)
    skip = jnp.repeat(own_first(skip_gain, 12), 64)[None, :]
    heads = jnp.stack(
        [in_lanes(own_first(step_bias, 12)), in_lanes(-jnp.exp(own_first(decay_log, 12)))]
        + [jnp.zeros((TILE,), F32)] * 6
    )
    bc_taps, bc_bias = conv_weight[:, 3072:], conv_bias[None, 3072:]
    seg = segments[0]
    seg_col, seg_row = segments.T, segments
    masks = jnp.stack(
        [(jnp.pad(seg, (o, 0), constant_values=-1)[:LEN] == seg).astype(F32) for o in range(4)], 1
    )

    a_near, b_near = ring(planes[..., :1280], YS), ring(planes[..., 1280:], XS)
    settings = (taps, bias, gain, skip, heads, bc_taps, bc_bias, seg_col, masks)
    a_first, b_first = place_near(a_near, b_near, 0, 512, settings)
    hidden_all, normed, norm_scale, cot_all = norm_of(hidden, cotangent, tokens_other, norm_gain[None])
    a_far, b_far = sides(a_first, XS), sides(b_first, YS)
    a_far, b_far = a_far + opposite(a_far, XS, 0), b_far + opposite(b_far, YS, 0)
    inner_own = place_far(a_far, b_far, 256, (normed,))
    inner_peer = send(inner_own, CORE)
    a_rest, b_rest = place_near(a_near, b_near, 512, 768, (inner_own,))
    a_rest, b_rest = sides(a_rest, XS), sides(b_rest, YS)

    bc_w, scores, scores_t, bc_act, bc_pre, cols, rows, steps = prepare(
        normed, inner_own, inner_peer, seg_col, seg_row, masks, bc_taps, bc_bias, heads
    )
    mixer = (taps, bias, masks, scores, cols, rows)
    pre_own, act_own, mixed_own = mix_forward(0, normed, inner_own, *mixer)
    a_more, b_more = opposites(a_rest, b_rest, act_own)
    a_rest, b_rest = a_rest + a_more, b_rest + b_more
    pre_peer, act_peer, mixed_peer = mix_forward(1, normed, inner_peer, *mixer)
    rest_own = place_far(a_rest, b_rest, WIDE, (act_peer,))
    rest_peer = send(rest_own, CORE)
    gate_own, gn_own, sums_own = gate_forward(0, normed, cot_all, rest_own, act_own, mixed_own, skip, gain)
    gate_peer, gn_peer, stats = gate_forward(1, normed, cot_all, rest_peer, act_peer, mixed_peer, skip, gain, (sums_own,))
    others = swap_tensor(stats)

    def other_tokens(values):
        return swap_tensor(lax.dynamic_slice_in_dim(values, (1 - t) * 256, 256, 0))

    def own_tokens(values, got=None):
        got = other_tokens(values) if got is None else got
        return lax.dynamic_slice_in_dim(values, t * 256, 256, 0).astype(F32) + got.astype(F32)

    (
        grad_y_peer,
        gate_low_peer,
        gnormed_peer,
        grad_y_own,
        gate_low,
        gnormed,
        gain_grad,
        gate_got,
        out_got,
    ) = gate_backward(
        stats,
        others,
        (gate_peer, gn_peer, act_peer, mixed_peer),
        (gate_own, gn_own, act_own, mixed_own),
        skip,
        gain,
        normed,
        cot_all,
    )
    gate_got, out_got = send(gate_got, CORE), send(out_got, CORE)
    branch = product(gnormed, gnormed_peer, rest_own, rest_peer, 1, BF)
    branch_got = other_tokens(branch)
    gate_pieces = weight_pieces(True, normed, (gate_low,), ((0, 768),), (gate_got,), (branch,))
    out_pieces = weight_pieces(False, cot_all, (gnormed,), ((0, 768),), (out_got,), (branch,))
    gate_grads = product(gate_low, gate_low_peer, rest_own, rest_peer, 0, F32, gate_pieces[3], out_pieces[3])
    mixed = (hidden.astype(F32) + own_tokens(branch, branch_got)).astype(BF)
    gate_passed, out_passed = pass_on(True, gate_pieces, gate_grads), pass_on(False, out_pieces, gate_grads)

    mixer = (scores_t, taps, bias, masks, cols, rows, skip)
    inner_peer_low, sums_peer, flows, grad_scores = mix_backward(
        1, grad_y_peer, act_peer, mixed_peer, pre_peer, *mixer, (), (gate_passed[0], out_passed[0])
    )
    a_part = weight_pieces(True, normed, (inner_peer_low,), ((0, 512),))
    a_got = send(a_part, CORE)
    gate_near = scatter_near(True, gate_pieces, gate_passed, a_part)
    out_near = scatter_near(False, out_pieces, out_passed, a_part)
    inner_own_low, sums_own, flows, grad_scores, scores_low = mix_backward(
        0, grad_y_own, act_own, mixed_own, pre_own, *mixer, (flows, grad_scores), (gate_near[1], out_near[1], branch_got)
    )
    scores_other = swap_tensor(scores_low)
    gate_far, out_far = send_far(True, gate_near), send_far(False, out_near)
    a_pieces = weight_pieces(True, normed, (inner_own_low,), ((0, 512),), (a_got,), tuple(gate_far))
    shares, head_sums = step_backward(heads, steps, flows)
    grad_low, norm_grad = normed_backward(
        gate_grads, inner_own_low, inner_peer_low, shares, inner_own, inner_peer, hidden_all, norm_scale, a_pieces[3]
    )
    grad_got = other_tokens(grad_low)
    a_passed = pass_on(True, a_pieces, norm_grad)
    tails, bc_sums = tail_backward(
        grad_scores, scores_other, bc_act, bc_pre, seg_col, seg_row, masks, bc_taps, bc_bias, shares, a_passed[0]
    )
    b_part = weight_pieces(False, normed, (inner_peer_low, tails), ((512, 768), (1, 256)))
    b_got = send(b_part, CORE)
    bc_part, norm_bc = bc_normed(tails, bc_w, hidden, norm_scale, b_part)
    small = small_of(sums_own, sums_peer, gain_grad, norm_grad, norm_bc, bc_sums, head_sums, norm_bc)
    small = small + send(small, CORE)
    b_pieces = weight_pieces(False, normed, (inner_own_low, tails), ((512, 768), (0, 256)), (b_got,), (small,))
    a_near_sum = scatter_near(True, a_pieces, a_passed, b_pieces[3])
    small = around(small, YS)
    b_passed = pass_on(False, b_pieces, a_near_sum[1], small, grad_got)
    b_near_sum = scatter_near(False, b_pieces, b_passed)
    late = b_near_sum[1]
    a_near_sum = [a_near_sum[0]] + [after(piece, b_passed[0]) for piece in a_near_sum[1:]]
    a_far, b_far = send_far(True, a_near_sum), send_far(False, b_near_sum)
    grad_hidden = hidden_grad(hidden, cotangent, norm_scale, norm_gain[None], grad_low, grad_got, bc_part, b_far[2])
    small = around(after(small, late), XS)
    small, small_other = small + send(small, ZHI), swap_tensor(small) + lax.ppermute(small, ("dp", "tensor"), ACROSS)
    rest_parts = jnp.concatenate(
        [sum_far([after(gate_near[0], late)], gate_far), sum_far([after(out_near[0], late)], out_far)], 2
    )
    rest_other = plane_other(rest_parts, spot[1])
    first_parts = jnp.concatenate([sum_far(a_near_sum, a_far), sum_far(b_near_sum, b_far)], 2)
    first_total = plane_sum(first_parts, plane_other(first_parts, spot[1]), spot[1])
    rest_total = plane_sum(rest_parts, rest_other, spot[1])
    grad_in, grad_bc, grad_step, grad_out = weight_rows(first_total, rest_total)
    conv_grad, bias_grad, gate_gain_grad, norm_gain_grad, head_grads = outputs_of(small, small_other)
    return (
        mixed,
        grad_hidden,
        norm_gain_grad[0],
        grad_in,
        grad_bc,
        grad_step,
        conv_grad,
        bias_grad[0],
        head_grads[7],
        head_grads[15],
        head_grads[23],
        gate_gain_grad[0],
        grad_out,
    )


def solution(mesh):
    return jax.shard_map(
        on_device,
        mesh=mesh,
        in_specs=(
            P(("dp", "tensor"), None),
            P("dp", None),
            P(),
            P(None, "dp", "tensor"),
            P("dp", None),
            P("dp", "tensor"),
            P(),
            P(),
            P(),
            P(),
            P(),
            P(),
            P("tensor", "dp"),
            P(("dp", "tensor"), None),
        ),
        out_specs=(
            P(("dp", "tensor"), None),
            P(("dp", "tensor"), None),
            P(),
            P(None, "dp", "tensor"),
            P("dp", None),
            P("dp", "tensor"),
            P(),
            P(),
            P(),
            P(),
            P(),
            P(),
            P("tensor", "dp"),
        ),
        check_vma=False,
    )
```
